32 devices in a mesh: gx: 4 (over y, core), gy: 8 (over z, x).
Axes of the slice: x: 2, y: 2, z: 4, core: 2. Of those that a mesh axis runs over, the one named last changes fastest.
Arguments:
- control: float32 [1, 2, 6, 384, 1536], P(None, None, None, 'gy', 'gx'), may hold values from -6 to 6
- sigma: float32 [2, 6, 384, 1536], P(None, None, 'gy', 'gx'), may hold values from 0.5 to 5
- kappa: float32 [5, 384, 1536], P(None, 'gy', 'gx'), may hold values from 0.05 to 5
- beta: float32 [6, 384, 1536], P(None, 'gy', 'gx'), may hold values from -3 to 3
- sea_mask: int32 [384, 1536], P('gy', 'gx'), may hold values 0 or 1
- x_inverse: float32 [1536, 1536], P('gx'), as said below
- y_inverse: float32 [384, 384], P('gx')
- ssh_coef: float32 [2, 6], replicated, may hold values from -1.5 to 1.5
- obs_owner: int32 [1024, 1], P(('gx', 'gy')), may hold values from 0 to 31; in each aligned block of 32 rows (0 to 31, 32 to 63, ...) at most 2 rows name the same one
- tile_index: int32 [1024], P(('gx', 'gy')), may hold values from 0 to 18046, as said below
- obs_frac: float32 [2, 1024], P(None, ('gx', 'gy')), may hold values from 0 to 1
- obs_count: int32 [32], P(('gx', 'gy')), may hold values from 16 to 32
Outputs:
- increments: float32 [1, 2, 6, 384, 1536], P(None, None, None, 'gy', 'gx')
- sea_height: float32 [1, 384, 1536], P(None, 'gy', 'gx')
- obs_equiv: float32 [2, 13, 1024], P(None, None, ('gx', 'gy'))
The draws below stay inside these ranges and needn't reach their ends.
Inputs may be any that keep to these rules, and one draw needn't show every extreme that they name: `obs_owner`: among the slots of one device, at most 2 name the same owner. `tile_index`: row * 384 + column of a cell in the device's own tile, with row below 47 and column below 383. `x_inverse`: the zonal inverse is symmetric.
All inputs are finite; a program needn't handle non-finite values. No bound on the sum of `sea_mask` on one device may be relied on, other than what follows from the above.
Results may differ from the reference program's by a relative error of at most 0.00013.
Values sent between devices are 32-bit elements; how exact they have to be, the bound alone decides.
No kernel may reach another device: no remote copies, remote signals or barrier semaphores. Data moves between devices by JAX's collectives and lax.ppermute only.
A program may use at most 128 MiB of HBM per device.

```python
import math
import jax
import jax.numpy as jnp
import numpy as np
from jax import lax

VECS = 1
LEV = 6
LAT_DEV = 48
LON_DEV = 384
STEPS = 2
CAP = 2
NY = 384
NX = 1536
OBS_DEV = 32
REC = 13
N_GY = 8
DEVICES = 32


def draw_x_inverse(key, part):
    first_key, second_key = jax.random.split(jax.random.fold_in(key, 11))
    row_ids = jnp.arange(NX)[:, None]
    col_ids = jnp.arange(NX)[None, :]
    gap = jnp.abs(row_ids - col_ids)
    gap = jnp.minimum(gap, NX - gap).astype(jnp.float32)
    reach = 2.0 * LON_DEV
    rough = jax.random.uniform(first_key, (NX, NX), jnp.float32)
    rough = 0.5 * (rough + rough.T)
    spread = rough * jnp.exp(-gap / reach) * (0.5 / reach)
    diagonal = jax.random.uniform(second_key, (NX, 1), jnp.float32, 0.5, 1.0)
    return jnp.where(row_ids == col_ids, diagonal, spread).astype(jnp.float32)


def draw_y_inverse(key, part):
    first_key, second_key = jax.random.split(jax.random.fold_in(key, 23))
    row_ids = jnp.arange(NY)[:, None]
    col_ids = jnp.arange(NY)[None, :]
    gap = jnp.abs(row_ids - col_ids).astype(jnp.float32)
    reach = 2.0 * LAT_DEV
    rough = jax.random.uniform(first_key, (NY, NY), jnp.float32)
    spread = rough * jnp.exp(-gap / reach) * (0.5 / reach)
    diagonal = jax.random.uniform(second_key, (NY, 1), jnp.float32, 0.5, 1.0)
    return jnp.where(row_ids == col_ids, diagonal, spread).astype(jnp.float32)


def draw_tile_index(key, part):
    first_key, second_key = jax.random.split(jax.random.fold_in(key, 37))
    row_pick = jax.random.randint(first_key, (DEVICES * OBS_DEV,), 0, LAT_DEV - 1)
    col_pick = jax.random.randint(second_key, (DEVICES * OBS_DEV,), 0, LON_DEV - 1)
    picked = (row_pick * LON_DEV + col_pick).astype(jnp.int32)
    picked = picked.at[0].set(jnp.int32((LAT_DEV - 1) * LON_DEV - 2))
    picked = picked.at[1].set(jnp.int32(0))
    return picked.astype(jnp.int32)


def touch_ends(values, key, least, top_value):
    longest = values.shape.index(max(values.shape))
    spots = []
    for shift in (0, 1):
        where = [jax.random.randint(jax.random.fold_in(key, axis), (), 0, length) for axis, length in enumerate(values.shape)]
        where[longest] = (where[longest] + shift) % values.shape[longest]
        spots.append(tuple(where))
    return values.at[spots[0]].set(least).at[spots[1]].set(top_value)


def block_levels(key, dims, cuts, least, high):
    def one(dim, shards_of):
        steps = jax.random.uniform(jax.random.fold_in(jax.random.fold_in(key, 6), dim), (shards_of,), jnp.float32, least / len(cuts), high / len(cuts))
        return jnp.repeat(jnp.exp(steps), dims[dim] // shards_of).reshape((-1,) + (1,) * (len(dims) - dim - 1))

    gain = one(*cuts[0])
    for cut in cuts[1:]:
        gain = gain * one(*cut)
    return gain


def assign_block(rng, own, number, rows, amount, top, limit, lean):
    sequence = jax.random.permutation(rng, amount)
    heavy_load, usual = shares(amount, rows * top, limit, lean, True), shares(amount, rows * top, limit, lean, False)
    places = jnp.arange(amount)

    def named(tallies, rotation):
        used = int((tallies > 0).sum())
        fixed = max(1, used // 4)
        passed = fixed + (places - fixed + rotation * (used - fixed)) % max(1, amount - fixed)
        return jnp.zeros((amount,), jnp.int32).at[sequence[jnp.where(places < fixed, places, passed)]].set(jnp.asarray(tallies, jnp.int32))

    tallies = jnp.where(number % 4 == 0, named(heavy_load, number // 4), named(usual, number - number // 4 - 1))
    mixed = jax.random.permutation(jax.random.fold_in(own, 3), amount)
    donor, taker = mixed[0:amount // 2 * 2:2], mixed[1:amount // 2 * 2:2]
    margin = jnp.minimum(tallies[donor] - 1, limit - tallies[taker]) // 2
    margin = jnp.where((donor == sequence[0]) | (taker == sequence[0]) | (tallies[taker] == 0), 0, jnp.maximum(margin, 0))
    passed = jax.random.randint(jax.random.fold_in(own, 4), (amount // 2,), 0, 1 << 20) % (margin + 1)
    tallies = tallies.at[donor].add(-passed).at[taker].add(passed)
    labels = jnp.searchsorted(jnp.cumsum(tallies), jnp.arange(rows * top), side="right").astype(jnp.int32)
    listing = labels.reshape(top, rows).T
    listing = listing[jax.random.permutation(jax.random.fold_in(own, 1), rows)]
    rotation = jax.random.randint(jax.random.fold_in(own, 2), (rows, 1), 0, top)
    return jnp.take_along_axis(listing, (jnp.arange(top)[None, :] + rotation) % top, axis=1)


def shares(count, total, limit, lean, full):
    loads = [(1 << 20) // math.isqrt(rank ** lean) + 1 for rank in range(1, count + 1)]
    largest = limit if full else min(limit, max(-(-total // count), total * loads[0] // sum(loads)))
    least = 1 if total - largest >= count - 1 else 0
    given, spare = [largest] + [least] * (count - 1), total - largest - least * (count - 1)
    while spare > 0:
        candidates = [i for i in range(1, count) if given[i] < largest] or [i for i in range(1, count) if given[i] < limit]
        whole, remaining = sum([loads[i] for i in candidates]), spare
        for i in candidates:
            extra = min(limit - given[i], max(1, remaining * loads[i] // whole), spare)
            given[i] = given[i] + extra
            spare = spare - extra
    return np.array(given)


def centred(rng, shape, scale, most, cuts=(), kind=jnp.bfloat16):
    drawn = jax.random.normal(rng, shape, jnp.float32) * scale
    if len(cuts) > 0:
        drawn = block_levels(rng, shape, cuts, -0.22, 0.18) * drawn
    return jnp.clip(drawn, min=-most, max=most).astype(kind)


def setup_inputs(seed: int = 0) -> dict:
    key_list = jax.random.split(jax.random.key(seed), 13)
    control = centred(key_list[0], (VECS, 2, LEV, NY, NX), 1.0, 6.0, ((3, 8), (4, 4)), jnp.float32)
    sigma = jnp.clip(jnp.exp(math.log(5.0) - 2.3025851 * jax.random.uniform(key_list[1], (2, LEV, NY, NX), jnp.float32) ** block_levels(key_list[1], (2, LEV, NY, NX), ((2, 8), (3, 4)), -0.2, 0.2)), 0.5, 5.0)
    kappa = jnp.clip(jnp.exp(math.log(5.0) - 4.6051702 * jax.random.uniform(key_list[2], (LEV - 1, NY, NX), jnp.float32) ** block_levels(key_list[2], (LEV - 1, NY, NX), ((1, 8), (2, 4)), -0.2, 0.2)), 0.05, 5.0)
    beta = centred(key_list[3], (LEV, NY, NX), 0.5, 3.0, ((1, 8), (2, 4)), jnp.float32)
    sea_mask = touch_ends((jax.random.randint(key_list[4], (NY, NX), 0, 5) < 4).astype(jnp.int32), jax.random.fold_in(key_list[4], 1), 0, 1)
    x_inverse = draw_x_inverse(jax.random.fold_in(key_list[12], 71), 0)
    y_inverse = draw_y_inverse(jax.random.fold_in(key_list[12], 71), 0)
    ssh_coef = centred(key_list[7], (2, LEV), 0.3, 1.5, (), jnp.float32)
    obs_owner_keys = jax.random.split(jax.random.fold_in(key_list[8], 1), (DEVICES * OBS_DEV) // OBS_DEV)
    obs_owner_turns = jax.random.permutation(jax.random.fold_in(key_list[8], 3), (DEVICES * OBS_DEV) // OBS_DEV)
    obs_owner = jax.vmap(lambda own, number: assign_block(jax.random.fold_in(key_list[8], 2), own, number, OBS_DEV, DEVICES, 1, CAP, 2))(obs_owner_keys, obs_owner_turns).reshape((DEVICES * OBS_DEV, 1))
    tile_index = draw_tile_index(jax.random.fold_in(key_list[12], 71), 0)
    obs_frac = jnp.clip(1.0 * jax.random.uniform(key_list[10], (2, DEVICES * OBS_DEV), jnp.float32) ** block_levels(key_list[10], (2, DEVICES * OBS_DEV), ((1, 32),), -0.2, 0.2), 0.0, 1.0)
    obs_count = touch_ends(jax.random.randint(key_list[11], (DEVICES,), OBS_DEV // 2, OBS_DEV + 1), jax.random.fold_in(key_list[11], 1), OBS_DEV // 2, OBS_DEV).astype(jnp.int32)
    return dict(control=control, sigma=sigma, kappa=kappa, beta=beta, sea_mask=sea_mask, x_inverse=x_inverse, y_inverse=y_inverse, ssh_coef=ssh_coef, obs_owner=obs_owner, tile_index=tile_index, obs_frac=obs_frac, obs_count=obs_count)


def vertical(values, kappa):
    levels = values.shape[2]
    c_list = []
    d_list = []
    for level in range(levels):
        k_below = kappa[level - 1] if level > 0 else 0.0
        k_above = kappa[level] if level < levels - 1 else 0.0
        diag_term = 1.0 + k_below + k_above
        if level == 0:
            pivot = diag_term
            d_new = values[:, :, 0] / pivot
        else:
            pivot = diag_term + k_below * c_list[-1]
            d_new = (values[:, :, level] + k_below * d_list[-1]) / pivot
        c_list.append(-k_above / pivot)
        d_list.append(d_new)
    result = [d_list[-1]]
    for level in range(levels - 2, -1, -1):
        result.insert(0, d_list[level] - c_list[level] * result[0])
    return jnp.stack(result, axis=2)


def reference(control, sigma, kappa, beta, sea_mask, x_inverse, y_inverse, ssh_coef, obs_owner, tile_index, obs_frac, obs_count):
    highest = lax.Precision.HIGHEST
    sea_open = sea_mask.astype(jnp.float32)
    grid_field = control.reshape(VECS * 2 * LEV, NY, NX)
    for diffusion_step in range(STEPS):
        grid_field = sea_open * jnp.einsum('fyb,ab->fya', grid_field, x_inverse, precision=highest)
        grid_field = sea_open * jnp.einsum('ab,fbx->fax', y_inverse, grid_field, precision=highest)
        grid_field = vertical(grid_field.reshape(VECS, 2, LEV, NY, NX), kappa).reshape(VECS * 2 * LEV, NY, NX)
    grid_field = grid_field.reshape(VECS, 2, LEV, NY, NX)
    temper = sigma[0] * grid_field[:, 0]
    saline = sigma[1] * grid_field[:, 1] + beta * temper
    height = jnp.sum(ssh_coef[0][None, :, None, None] * temper + ssh_coef[1][None, :, None, None] * saline, axis=1)
    increments = jnp.stack([temper, saline], axis=1)
    profile = jnp.concatenate([temper, saline, height[:, None]], axis=1)
    every = jnp.arange(DEVICES * OBS_DEV, dtype=jnp.int32)
    source = every // OBS_DEV
    slot_index = every % OBS_DEV
    col_block = source // N_GY
    row_block = source % N_GY
    row_index = row_block * LAT_DEV + tile_index // LON_DEV
    col_index = col_block * LON_DEV + tile_index % LON_DEV
    frac_x = obs_frac[0]
    frac_y = obs_frac[1]
    corner_a = profile[:, :, row_index, col_index]
    corner_b = profile[:, :, row_index, col_index + 1]
    corner_c = profile[:, :, row_index + 1, col_index]
    corner_d = profile[:, :, row_index + 1, col_index + 1]
    interp = (1.0 - frac_y) * ((1.0 - frac_x) * corner_a + frac_x * corner_b) + frac_y * ((1.0 - frac_x) * corner_c + frac_x * corner_d)
    live_slot = (slot_index < obs_count[source]).astype(jnp.float32)
    interp = (interp * live_slot).reshape(REC, DEVICES * OBS_DEV)
    owners = obs_owner[:, 0]
    per_device = owners.reshape(DEVICES, OBS_DEV)
    one_hot = (per_device[:, :, None] == jnp.arange(DEVICES, dtype=jnp.int32)[None, None, :]).astype(jnp.int32)
    before = jnp.cumsum(one_hot, axis=1) - one_hot
    slot_rank = jnp.sum(before * one_hot, axis=2).reshape(-1).astype(jnp.int32)
    target = (owners * DEVICES + source).astype(jnp.int32)
    obs_equiv = jnp.zeros((CAP, REC, DEVICES * DEVICES), jnp.float32).at[slot_rank, :, target].set(interp.T)
    return increments, height, obs_equiv
```

```python
import functools

import jax
import jax.numpy as jnp
from jax import lax
from jax.experimental import pallas as pl
from jax.experimental.pallas import tpu as pltpu
from jax.sharding import PartitionSpec as P

STEPS = 2
CAP = 2
LANES = 128
SUB = 8
RANK_ROWS = 16
NN = (((1,), (0,)), ((), ()))
NT = (((1,), (1,)), ((), ()))


class Plan:
    def __init__(self, fields, rows, cols, parts):
        self.fields, self.rows, self.cols, self.parts = fields, rows, cols, parts
        self.blocks = cols // LANES
        tiles = fields * self.blocks
        share = fields * cols // parts
        self.full = share // LANES
        self.rest = share % LANES
        self.sides = LANES // self.rest if self.rest else 0
        self.groups = rows // SUB
        self.packs = -(-self.groups // self.sides) if self.rest else 0
        self.width = self.full * rows + self.packs * SUB
        self.columns = (self.full + (1 if self.rest else 0)) * LANES
        self.fits = (
            cols % LANES == 0
            and rows % SUB == 0
            and fields * cols % parts == 0
            and (self.rest == 0 or LANES % self.rest == 0)
            and tiles - self.full * parts == (parts // self.sides if self.rest else 0)
        )

    def home(self, tile):
        if tile < self.full * self.parts:
            return tile // self.full, tile % self.full
        return None, tile - self.full * self.parts

    def pack_rest(self, tile, place):
        lane_side = lax.broadcasted_iota(jnp.int32, (SUB, LANES), 1) // self.rest
        out = []
        for pack in range(self.packs):
            joined = None
            for side in range(self.sides):
                group = pack * self.sides + side
                if group >= self.groups:
                    break
                piece = tile[group * SUB : (group + 1) * SUB, :]
                shift = ((side - place) * self.rest) % LANES
                if shift:
                    piece = pltpu.roll(piece, shift, axis=1)
                joined = piece if joined is None else jnp.where(lane_side == side, piece, joined)
            out.append(joined)
        return out

    def unpack_rest(self, packs, place):
        pieces = []
        for group in range(self.groups):
            pack, side = divmod(group, self.sides)
            shift = ((place - side) * self.rest) % LANES
            piece = packs[pack]
            pieces.append(pltpu.roll(piece, shift, axis=1) if shift else piece)
        return jnp.concatenate(pieces, axis=0)

    def store_tile(self, out_ref, tile_index, tile):
        device, place = self.home(tile_index)
        if device is not None:
            out_ref[device, place * self.rows : (place + 1) * self.rows, :] = tile
            return
        for side in range(self.sides):
            device = place * self.sides + side
            for pack, value in enumerate(self.pack_rest(tile, side)):
                start = self.full * self.rows + pack * SUB
                out_ref[device, start : start + SUB, :] = value

    def load_tile(self, in_ref, tile_index):
        device, place = self.home(tile_index)
        if device is not None:
            return in_ref[device, place * self.rows : (place + 1) * self.rows, :]
        lane_side = lax.broadcasted_iota(jnp.int32, (self.rows, LANES), 1) // self.rest
        joined = None
        for side in range(self.sides):
            packs = self.load_packs(in_ref, place * self.sides + side)
            piece = self.unpack_rest(packs, side)
            joined = piece if joined is None else jnp.where(lane_side == side, piece, joined)
        return joined

    def load_packs(self, in_ref, device):
        base = self.full * self.rows
        return [in_ref[device, base + p * SUB : base + (p + 1) * SUB, :] for p in range(self.packs)]


def split(value):
    high = value.astype(jnp.bfloat16)
    low = (value - high.astype(jnp.float32)).astype(jnp.bfloat16)
    return high, low


def dot(a, b, dims=NN):
    return lax.dot_general(a, b, dims, preferred_element_type=jnp.float32)


def dot_split(a, b):
    return dot(a[0], b[0]) + (dot(a[0], b[1]) + dot(a[1], b[0]))


def call(kernel, out_shape, operands, scalars=(), flops=0):
    outs = out_shape if isinstance(out_shape, (list, tuple)) else [out_shape]
    moved = sum(a.size * a.dtype.itemsize for a in list(operands) + list(outs))
    specs = [
        pl.BlockSpec(memory_space=pltpu.SMEM if i in scalars else pltpu.VMEM)
        for i in range(len(operands))
    ]
    out_spec = pl.BlockSpec(memory_space=pltpu.VMEM)
    many = isinstance(out_shape, (list, tuple))
    return pl.pallas_call(
        kernel,
        out_shape=out_shape,
        in_specs=specs,
        out_specs=[out_spec] * len(outs) if many else out_spec,
        compiler_params=pltpu.CompilerParams(vmem_limit_bytes=min(48, 6 + 3 * moved // 2**20) * 2**20),
        cost_estimate=pl.CostEstimate(flops=flops, bytes_accessed=moved, transcendentals=0),
    )(*operands)


def gather_pieces(block, axis, count):
    held = [(0, block)]
    bit = count // 2
    while bit:
        pairs = [(i, i ^ bit) for i in range(count)]
        held = held + [(mask ^ bit, lax.ppermute(piece, axis, pairs)) for mask, piece in held]
        bit //= 2
    return held


def prepare_x(x_inverse):
    rows, cols = x_inverse.shape

    def kernel(x_ref, high_ref, low_ref):
        for start in range(0, cols, rows):
            high, low = split(jnp.transpose(x_ref[:, start : start + rows]))
            high_ref[start : start + rows, :] = high
            low_ref[start : start + rows, :] = low

    shape = jax.ShapeDtypeStruct((cols, rows), jnp.bfloat16)
    return call(kernel, [shape, shape], [x_inverse])


def prepare_y(masks, pieces, me):
    rows, cols = pieces[0].shape

    def kernel(me_ref, *refs):
        high_ref, low_ref = refs[-2:]
        for mask, ref in zip(masks, refs):
            start = pl.multiple_of((me_ref[0] ^ mask) * rows, rows)
            high, low = split(ref[...])
            high_ref[pl.ds(start, rows), :] = high
            low_ref[pl.ds(start, rows), :] = low

    shape = jax.ShapeDtypeStruct((cols, cols), jnp.bfloat16)
    return call(kernel, [shape, shape], [me] + pieces, scalars=(0,))


def zonal(plan, masks, pieces, me, x_high, x_low, sea_mask):
    fields, rows, cols = plan.fields, plan.rows, plan.cols

    def kernel(me_ref, high_ref, low_ref, sea_ref, *refs):
        out_ref = refs[-1]
        total = None
        for mask, ref in zip(masks, refs):
            start = pl.multiple_of((me_ref[0] ^ mask) * cols, cols)
            values = split(ref[...].reshape(fields * rows, cols))
            weights = (high_ref[pl.ds(start, cols), :], low_ref[pl.ds(start, cols), :])
            part = dot_split(values, weights)
            total = part if total is None else total + part
        total = total.reshape(fields, rows, cols)
        sea = sea_ref[...].astype(jnp.float32)
        for block in range(plan.blocks):
            lanes = slice(block * LANES, (block + 1) * LANES)
            for field in range(fields):
                tile = sea[:, lanes] * total[field, :, lanes]
                plan.store_tile(out_ref, field * plan.blocks + block, tile)

    return call(
        kernel,
        jax.ShapeDtypeStruct((plan.parts, plan.width, LANES), jnp.float32),
        [me, x_high, x_low, sea_mask] + pieces,
        scalars=(0,),
        flops=6 * fields * rows * cols * cols * len(pieces),
    )


def meridional(plan, lines, y_high, y_low):
    rows, parts = plan.rows, plan.parts

    def kernel(in_ref, high_ref, low_ref, out_ref):
        columns = [
            in_ref[:, i * rows : (i + 1) * rows, :].reshape(parts * rows, LANES)
            for i in range(plan.full)
        ]
        if plan.rest:
            columns.append(
                jnp.concatenate(
                    [plan.unpack_rest(plan.load_packs(in_ref, d), 0) for d in range(parts)], axis=0
                )
            )
        values = split(jnp.concatenate(columns, axis=1))
        solved = dot_split((high_ref[...], low_ref[...]), values)
        for i in range(plan.full):
            tile = solved[:, i * LANES : (i + 1) * LANES]
            out_ref[:, i * rows : (i + 1) * rows, :] = tile.reshape(parts, rows, LANES)
        if plan.rest:
            last = solved[:, plan.full * LANES :]
            for d in range(parts):
                packs = plan.pack_rest(last[d * rows : (d + 1) * rows, :], 0)
                for p, value in enumerate(packs):
                    start = plan.full * rows + p * SUB
                    out_ref[d, start : start + SUB, :] = value

    return call(
        kernel,
        jax.ShapeDtypeStruct(lines.shape, jnp.float32),
        [lines, y_high, y_low],
        flops=6 * (parts * rows) ** 2 * plan.columns,
    )


def solve_columns(plan, in_ref, kappa_ref, sea_ref, levels, store):
    kinds = plan.fields // levels
    for block in range(plan.blocks):
        lanes = slice(block * LANES, (block + 1) * LANES)
        sea = sea_ref[:, lanes].astype(jnp.float32)
        inverse, upper = [], []
        kappa = [kappa_ref[level, :, lanes] for level in range(levels - 1)]
        for level in range(levels):
            below = kappa[level - 1] if level > 0 else 0.0
            above = kappa[level] if level < levels - 1 else 0.0
            pivot = 1.0 + below + above
            if level > 0:
                pivot = pivot + below * upper[-1]
            inverse.append(1.0 / pivot)
            upper.append(-above * inverse[-1])
        for kind in range(kinds):
            forward = []
            for level in range(levels):
                tile = plan.load_tile(in_ref, (kind * levels + level) * plan.blocks + block)
                right = sea * tile
                if level > 0:
                    right = right + kappa[level - 1] * forward[-1]
                forward.append(right * inverse[level])
            value = forward[-1]
            store(kind, levels - 1, lanes, value)
            for level in range(levels - 2, -1, -1):
                value = forward[level] - upper[level] * value
                store(kind, level, lanes, value)


def vertical(plan, returned, kappa, sea_mask, levels):
    def kernel(in_ref, kappa_ref, sea_ref, out_ref):
        def store(kind, level, lanes, value):
            out_ref[kind * levels + level, :, lanes] = value

        solve_columns(plan, in_ref, kappa_ref, sea_ref, levels, store)

    return call(
        kernel,
        jax.ShapeDtypeStruct((plan.fields, plan.rows, plan.cols), jnp.float32),
        [returned, kappa, sea_mask],
    )


def finish(plan, returned, temper_field, kappa, sea_mask, sigma, beta, ssh_coef, obs, devices):
    levels = sigma.shape[1]
    rows, cols = plan.rows, plan.cols
    records = 2 * levels + 1
    owner_row, tile_index, obs_frac, obs_count, owner_col = obs
    slots = owner_row.shape[1]
    extra = [] if temper_field is None else [temper_field]

    def kernel(ssh_ref, count_ref, in_ref, kappa_ref, sea_ref, sigma_ref, beta_ref,
               owner_ref, tile_ref, frac_ref, column_ref, *refs):
        inc_ref, height_ref, send_ref, profile_ref = refs[-4:]

        def store(kind, level, lanes, value):
            profile_ref[(kind + len(extra)) * levels + level, :, lanes] = value

        solve_columns(plan, in_ref, kappa_ref, sea_ref, levels, store)
        for block in range(plan.blocks):
            lanes = slice(block * LANES, (block + 1) * LANES)
            height = None
            for level in range(levels):
                source = refs[0] if extra else profile_ref
                temper = sigma_ref[0, level, :, lanes] * source[level, :, lanes]
                saline = (
                    sigma_ref[1, level, :, lanes] * profile_ref[levels + level, :, lanes]
                    + beta_ref[level, :, lanes] * temper
                )
                term = ssh_ref[0, level] * temper + ssh_ref[1, level] * saline
                height = term if height is None else height + term
                profile_ref[level, :, lanes] = temper
                profile_ref[levels + level, :, lanes] = saline
                inc_ref[0, level, :, lanes] = temper
                inc_ref[1, level, :, lanes] = saline
            profile_ref[2 * levels, :, lanes] = height
            height_ref[:, lanes] = height

        cell = tile_ref[...]
        row, col = cell // cols, cell % cols
        frac_x, frac_y = frac_ref[0:1, :], frac_ref[1:2, :]
        along = lax.broadcasted_iota(jnp.int32, (cols, slots), 0)
        weight_x = jnp.where(along == col, 1.0 - frac_x, jnp.where(along == col + 1, frac_x, 0.0))
        across = lax.broadcasted_iota(jnp.int32, (rows, slots), 0)
        weight_y = jnp.where(across == row, 1.0 - frac_y, jnp.where(across == row + 1, frac_y, 0.0))
        partial = lax.dot_general(
            profile_ref[...].reshape(records * rows, cols),
            weight_x,
            NN,
            precision=lax.Precision.HIGHEST,
            preferred_element_type=jnp.float32,
        ).reshape(records, rows, slots)
        interp = jnp.sum(partial * weight_y[None], axis=1)
        slot = lax.broadcasted_iota(jnp.int32, (1, slots), 1)
        interp = interp * (slot < count_ref[0]).astype(jnp.float32)
        earlier = lax.broadcasted_iota(jnp.int32, (slots, slots), 0) < lax.broadcasted_iota(
            jnp.int32, (slots, slots), 1
        )
        owner = owner_ref[...]
        same = jnp.where((column_ref[...] == owner) & earlier, 1.0, 0.0)
        rank = jnp.sum(same, axis=0, keepdims=True).astype(jnp.int32)
        padded = jnp.concatenate(
            [interp, jnp.zeros((RANK_ROWS - records, slots), jnp.float32)], axis=0
        )
        ranked = jnp.concatenate(
            [jnp.where(rank == r, padded, 0.0) for r in range(CAP)], axis=0
        )
        ranked = jnp.concatenate(
            [ranked, jnp.zeros((LANES - CAP * RANK_ROWS, slots), jnp.float32)], axis=0
        )
        to_owner = (owner == lax.broadcasted_iota(jnp.int32, (devices, slots), 0)).astype(
            jnp.float32
        )
        send_ref[...] = lax.dot_general(
            to_owner, ranked, NT, precision=lax.Precision.HIGHEST, preferred_element_type=jnp.float32
        )

    operands = [ssh_coef, obs_count, returned, kappa, sea_mask, sigma, beta,
                owner_row, tile_index, obs_frac, owner_col] + extra
    outs = [
        jax.ShapeDtypeStruct((2, levels, rows, cols), jnp.float32),
        jax.ShapeDtypeStruct((rows, cols), jnp.float32),
        jax.ShapeDtypeStruct((devices, LANES), jnp.float32),
    ]
    moved = sum(a.size * a.dtype.itemsize for a in operands + outs)
    return pl.pallas_call(
        kernel,
        out_shape=outs,
        in_specs=[pl.BlockSpec(memory_space=pltpu.SMEM)] * 2
        + [pl.BlockSpec(memory_space=pltpu.VMEM)] * (len(operands) - 2),
        out_specs=[pl.BlockSpec(memory_space=pltpu.VMEM)] * 3,
        scratch_shapes=[pltpu.VMEM((records, rows, cols), jnp.float32)],
        compiler_params=pltpu.CompilerParams(vmem_limit_bytes=32 * 2**20),
        cost_estimate=pl.CostEstimate(flops=10**7, bytes_accessed=moved, transcendentals=0),
    )(*operands)


def receive(arrived, records):
    devices = arrived.shape[0]

    def kernel(in_ref, out_ref):
        turned = jnp.transpose(in_ref[...])
        for r in range(CAP):
            out_ref[r] = turned[r * RANK_ROWS : r * RANK_ROWS + records, :]

    return call(kernel, jax.ShapeDtypeStruct((CAP, records, devices), jnp.float32), [arrived])


def body(gx_count, gy_count, control, sigma, kappa, beta, sea_mask, x_inverse, y_inverse, ssh_coef,
         obs_owner, tile_index, obs_frac, obs_count):
    _, kinds, levels, rows, cols = control.shape
    devices = gx_count * gy_count
    plan = Plan(levels, rows, cols, gy_count)
    chunks = kinds
    if not plan.fits:
        plan, chunks = Plan(kinds * levels, rows, cols, gy_count), 1
    me = lax.axis_index("gx").astype(jnp.int32).reshape(1)
    x_high, x_low = prepare_x(x_inverse)
    fields = list(control.reshape(chunks, plan.fields, rows, cols))
    y_parts = None
    result = None
    for step in range(STEPS):
        sent = []
        for chunk in range(chunks):
            held = gather_pieces(fields[chunk], "gx", gx_count)
            packed = zonal(
                plan, [m for m, _ in held], [p for _, p in held], me, x_high, x_low, sea_mask
            )
            sent.append(lax.all_to_all(packed, "gy", split_axis=0, concat_axis=0, tiled=True))
        if y_parts is None:
            held = gather_pieces(y_inverse, "gx", gx_count)
            y_parts = prepare_y([m for m, _ in held], [p for _, p in held], me)
        for chunk in range(chunks):
            solved = meridional(plan, sent[chunk], *y_parts)
            returned = lax.all_to_all(solved, "gy", split_axis=0, concat_axis=0, tiled=True)
            if step < STEPS - 1 or chunk < chunks - 1:
                fields[chunk] = vertical(plan, returned, kappa, sea_mask, levels)
            else:
                obs = (
                    obs_owner.reshape(1, -1),
                    tile_index.reshape(1, -1),
                    obs_frac,
                    obs_count,
                    obs_owner,
                )
                result = finish(
                    plan, returned, fields[0] if chunks > 1 else None, kappa, sea_mask, sigma,
                    beta, ssh_coef, obs, devices,
                )
    increments, height, outgoing = result
    arrived = lax.all_to_all(outgoing, ("gx", "gy"), split_axis=0, concat_axis=0, tiled=True)
    return increments[None], height[None], receive(arrived, kinds * levels + 1)


def solution(mesh):
    return jax.shard_map(
        functools.partial(body, mesh.shape["gx"], mesh.shape["gy"]),
        mesh=mesh,
        in_specs=(
            P(None, None, None, "gy", "gx"),
            P(None, None, "gy", "gx"),
            P(None, "gy", "gx"),
            P(None, "gy", "gx"),
            P("gy", "gx"),
            P("gx", None),
            P("gx", None),
            P(),
            P(("gx", "gy"), None),
            P(("gx", "gy")),
            P(None, ("gx", "gy")),
            P(("gx", "gy")),
        ),
        out_specs=(
            P(None, None, None, "gy", "gx"),
            P(None, "gy", "gx"),
            P(None, None, ("gx", "gy")),
        ),
        check_vma=False,
    )
```

```python
import functools

import jax
import jax.numpy as jnp
from jax import lax
from jax.experimental import pallas as pl
from jax.experimental.pallas import tpu as pltpu
from jax.sharding import PartitionSpec as P

STEPS = 2
CAP = 2
LANES = 128
SUB = 8
RANK_ROWS = 16
NN = (((1,), (0,)), ((), ()))
NT = (((1,), (1,)), ((), ()))


class Plan:
    def __init__(self, fields, rows, cols, parts):
        self.fields, self.rows, self.cols, self.parts = fields, rows, cols, parts
        self.blocks = cols // LANES
        tiles = fields * self.blocks
        share = fields * cols // parts
        self.full = share // LANES
        self.rest = share % LANES
        self.sides = LANES // self.rest if self.rest else 0
        self.groups = rows // SUB
        self.packs = -(-self.groups // self.sides) if self.rest else 0
        self.width = self.full * rows + self.packs * SUB
        self.columns = (self.full + (1 if self.rest else 0)) * LANES
        self.fits = (
            cols % LANES == 0
            and rows % SUB == 0
            and fields * cols % parts == 0
            and (self.rest == 0 or LANES % self.rest == 0)
            and tiles - self.full * parts == (parts // self.sides if self.rest else 0)
        )

    def moved(self, side, place):
        return ((side - place) * self.rest) % LANES

    def pack_rest(self, tile, place):
        lane_side = lax.broadcasted_iota(jnp.int32, (SUB, LANES), 1) // self.rest
        out = []
        for pack in range(self.packs):
            joined = None
            for side in range(self.sides):
                group = pack * self.sides + side
                if group >= self.groups:
                    break
                piece = turn(tile[group * SUB : (group + 1) * SUB, :], self.moved(side, place))
                joined = piece if joined is None else jnp.where(lane_side == side, piece, joined)
            out.append(joined)
        return out

    def unpack_rest(self, ref, place):
        pieces = []
        for group in range(self.groups):
            pack, side = divmod(group, self.sides)
            start = self.full * self.rows + pack * SUB
            pieces.append(turn(ref[start : start + SUB, :], self.moved(place, side)))
        return jnp.concatenate(pieces, axis=0)

    def store_rest(self, ref, packs):
        for pack, value in enumerate(packs):
            start = self.full * self.rows + pack * SUB
            ref[start : start + SUB, :] = value

    def send_tiles(self, tiles_ref, device, out_ref):
        for i in range(self.full):
            out_ref[i * self.rows : (i + 1) * self.rows, :] = tiles_ref[device * self.full + i]
        if self.rest:
            tile = tiles_ref[self.parts * self.full + device // self.sides]
            self.store_rest(out_ref, self.pack_rest(tile, device % self.sides))

    def take_tiles(self, in_ref, device, tiles_ref):
        for i in range(self.full):
            tiles_ref[device * self.full + i] = in_ref[i * self.rows : (i + 1) * self.rows, :]
        if self.rest:
            place = device % self.sides
            index = self.parts * self.full + device // self.sides
            lane_side = lax.broadcasted_iota(jnp.int32, (self.rows, LANES), 1) // self.rest
            tiles_ref[index] = jnp.where(
                lane_side == place, self.unpack_rest(in_ref, place), tiles_ref[index]
            )

    @property
    def tiles(self):
        return pltpu.VMEM((self.fields * self.blocks, self.rows, LANES), jnp.float32)

    @property
    def lines(self):
        return pltpu.VMEM((self.parts * self.rows, self.columns), jnp.float32)

    @property
    def blocks_out(self):
        shape = jax.ShapeDtypeStruct((self.width, LANES), jnp.float32)
        return [shape] * self.parts


def turn(value, shift):
    if isinstance(shift, int) and shift == 0:
        return value
    return pltpu.roll(value, shift, axis=1)


def split(value):
    high = value.astype(jnp.bfloat16)
    low = (value - high.astype(jnp.float32)).astype(jnp.bfloat16)
    return high, low


def dot(a, b, dims=NN):
    return lax.dot_general(a, b, dims, preferred_element_type=jnp.float32)


def dot_split(a, b):
    return dot(a[0], b[0]) + (dot(a[0], b[1]) + dot(a[1], b[0]))


def call(kernel, out_shape, operands, scalars=(), flops=0, scratch=()):
    outs = out_shape if isinstance(out_shape, (list, tuple)) else [out_shape]
    moved = sum(a.size * a.dtype.itemsize for a in list(operands) + list(outs))
    specs = [
        pl.BlockSpec(memory_space=pltpu.SMEM if i in scalars else pltpu.VMEM)
        for i in range(len(operands))
    ]
    out_spec = pl.BlockSpec(memory_space=pltpu.VMEM)
    many = isinstance(out_shape, (list, tuple))
    return pl.pallas_call(
        kernel,
        out_shape=out_shape,
        in_specs=specs,
        out_specs=[out_spec] * len(outs) if many else out_spec,
        scratch_shapes=list(scratch),
        compiler_params=pltpu.CompilerParams(vmem_limit_bytes=min(48, 6 + 3 * moved // 2**20) * 2**20),
        cost_estimate=pl.CostEstimate(flops=flops, bytes_accessed=moved, transcendentals=0),
    )(*operands)


def gather_pieces(block, axis, count):
    held = [(0, block)]
    bit = count // 2
    while bit:
        pairs = [(i, i ^ bit) for i in range(count)]
        held = held + [(mask ^ bit, lax.ppermute(piece, axis, pairs)) for mask, piece in held]
        bit //= 2
    return held


def exchange(blocks, axis, count):
    out = [blocks[0]] + [None] * (count - 1)
    for mask in range(count - 1, 0, -1):
        out[mask] = lax.ppermute(blocks[mask], axis, [(i, i ^ mask) for i in range(count)])
    return out


def prepare_x(x_inverse):
    rows, cols = x_inverse.shape

    def kernel(x_ref, high_ref, low_ref):
        for start in range(0, cols, rows):
            high, low = split(jnp.transpose(x_ref[:, start : start + rows]))
            high_ref[start : start + rows, :] = high
            low_ref[start : start + rows, :] = low

    shape = jax.ShapeDtypeStruct((cols, rows), jnp.bfloat16)
    return call(kernel, [shape, shape], [x_inverse])


def prepare_y(masks, pieces, me):
    rows, cols = pieces[0].shape

    def kernel(me_ref, *refs):
        high_ref, low_ref = refs[-2:]
        for mask, ref in zip(masks, refs):
            start = pl.multiple_of((me_ref[0] ^ mask) * rows, rows)
            high, low = split(ref[...])
            high_ref[pl.ds(start, rows), :] = high
            low_ref[pl.ds(start, rows), :] = low

    shape = jax.ShapeDtypeStruct((cols, cols), jnp.bfloat16)
    return call(kernel, [shape, shape], [me] + pieces, scalars=(0,))


def zonal(plan, masks, pieces, me, x_high, x_low, sea_mask):
    fields, rows, cols, parts = plan.fields, plan.rows, plan.cols, plan.parts

    def kernel(me_ref, high_ref, low_ref, sea_ref, *refs):
        out_refs, tiles_ref = refs[-parts - 1 : -1], refs[-1]
        total = None
        for mask, ref in zip(masks, refs):
            start = pl.multiple_of((me_ref[0] ^ mask) * cols, cols)
            values = split(ref[...].reshape(fields * rows, cols))
            weights = (high_ref[pl.ds(start, cols), :], low_ref[pl.ds(start, cols), :])
            part = dot_split(values, weights)
            total = part if total is None else total + part
        total = total.reshape(fields, rows, cols)
        sea = sea_ref[...].astype(jnp.float32)
        for block in range(plan.blocks):
            lanes = slice(block * LANES, (block + 1) * LANES)
            for field in range(fields):
                tiles_ref[field * plan.blocks + block] = sea[:, lanes] * total[field, :, lanes]
        for mask in range(parts):
            plan.send_tiles(tiles_ref, me_ref[1] ^ mask, out_refs[mask])

    return call(
        kernel,
        plan.blocks_out,
        [me, x_high, x_low, sea_mask] + pieces,
        scalars=(0,),
        flops=6 * fields * rows * cols * cols * len(pieces),
        scratch=[plan.tiles],
    )


def meridional(plan, me, lines, y_high, y_low):
    rows, parts = plan.rows, plan.parts

    def kernel(me_ref, high_ref, low_ref, *refs):
        in_refs, out_refs, lines_ref = refs[:parts], refs[parts : 2 * parts], refs[-1]
        for mask in range(parts):
            place = pl.ds(pl.multiple_of((me_ref[1] ^ mask) * rows, rows), rows)
            for i in range(plan.full):
                lanes = slice(i * LANES, (i + 1) * LANES)
                lines_ref[place, lanes] = in_refs[mask][i * rows : (i + 1) * rows, :]
            if plan.rest:
                lines_ref[place, plan.full * LANES :] = plan.unpack_rest(in_refs[mask], 0)
        lines_ref[...] = dot_split((high_ref[...], low_ref[...]), split(lines_ref[...]))
        for mask in range(parts):
            place = pl.ds(pl.multiple_of((me_ref[1] ^ mask) * rows, rows), rows)
            for i in range(plan.full):
                lanes = slice(i * LANES, (i + 1) * LANES)
                out_refs[mask][i * rows : (i + 1) * rows, :] = lines_ref[place, lanes]
            if plan.rest:
                last = lines_ref[place, plan.full * LANES :]
                plan.store_rest(out_refs[mask], plan.pack_rest(last, 0))

    return call(
        kernel,
        plan.blocks_out,
        [me, y_high, y_low] + lines,
        scalars=(0,),
        flops=6 * (parts * rows) ** 2 * plan.columns,
        scratch=[plan.lines],
    )


def solve_columns(plan, me_ref, in_refs, tiles_ref, kappa_ref, sea_ref, levels, store):
    kinds = plan.fields // levels
    for mask in range(plan.parts):
        plan.take_tiles(in_refs[mask], me_ref[1] ^ mask, tiles_ref)
    for block in range(plan.blocks):
        lanes = slice(block * LANES, (block + 1) * LANES)
        sea = sea_ref[:, lanes].astype(jnp.float32)
        inverse, upper = [], []
        kappa = [kappa_ref[level, :, lanes] for level in range(levels - 1)]
        for level in range(levels):
            below = kappa[level - 1] if level > 0 else 0.0
            above = kappa[level] if level < levels - 1 else 0.0
            pivot = 1.0 + below + above
            if level > 0:
                pivot = pivot + below * upper[-1]
            inverse.append(1.0 / pivot)
            upper.append(-above * inverse[-1])
        for kind in range(kinds):
            forward = []
            for level in range(levels):
                tile = tiles_ref[(kind * levels + level) * plan.blocks + block]
                right = sea * tile
                if level > 0:
                    right = right + kappa[level - 1] * forward[-1]
                forward.append(right * inverse[level])
            value = forward[-1]
            store(kind, levels - 1, lanes, value)
            for level in range(levels - 2, -1, -1):
                value = forward[level] - upper[level] * value
                store(kind, level, lanes, value)


def vertical(plan, me, returned, kappa, sea_mask, levels):
    def kernel(me_ref, kappa_ref, sea_ref, *refs):
        in_refs, (out_ref, tiles_ref) = refs[: plan.parts], refs[plan.parts :]

        def store(kind, level, lanes, value):
            out_ref[kind * levels + level, :, lanes] = value

        solve_columns(plan, me_ref, in_refs, tiles_ref, kappa_ref, sea_ref, levels, store)

    return call(
        kernel,
        jax.ShapeDtypeStruct((plan.fields, plan.rows, plan.cols), jnp.float32),
        [me, kappa, sea_mask] + returned,
        scalars=(0,),
        scratch=[plan.tiles],
    )


def finish(plan, me, returned, temper_field, kappa, sea_mask, sigma, beta, ssh_coef, obs, devices):
    levels = sigma.shape[1]
    rows, cols = plan.rows, plan.cols
    records = 2 * levels + 1
    owner_row, tile_index, obs_frac, obs_count, owner_col = obs
    slots = owner_row.shape[1]
    extra = [] if temper_field is None else [temper_field]

    def kernel(me_ref, ssh_ref, count_ref, kappa_ref, sea_ref, sigma_ref, beta_ref,
               owner_ref, tile_ref, frac_ref, column_ref, *refs):
        inc_ref, height_ref, send_ref, profile_ref, tiles_ref = refs[-5:]

        def store(kind, level, lanes, value):
            profile_ref[(kind + len(extra)) * levels + level, :, lanes] = value

        solve_columns(
            plan, me_ref, refs[len(extra) :], tiles_ref, kappa_ref, sea_ref, levels, store
        )
        for block in range(plan.blocks):
            lanes = slice(block * LANES, (block + 1) * LANES)
            height = None
            for level in range(levels):
                source = refs[0] if extra else profile_ref
                temper = sigma_ref[0, level, :, lanes] * source[level, :, lanes]
                saline = (
                    sigma_ref[1, level, :, lanes] * profile_ref[levels + level, :, lanes]
                    + beta_ref[level, :, lanes] * temper
                )
                term = ssh_ref[0, level] * temper + ssh_ref[1, level] * saline
                height = term if height is None else height + term
                profile_ref[level, :, lanes] = temper
                profile_ref[levels + level, :, lanes] = saline
                inc_ref[0, level, :, lanes] = temper
                inc_ref[1, level, :, lanes] = saline
            profile_ref[2 * levels, :, lanes] = height
            height_ref[:, lanes] = height

        cell = tile_ref[...]
        row, col = cell // cols, cell % cols
        frac_x, frac_y = frac_ref[0:1, :], frac_ref[1:2, :]
        along = lax.broadcasted_iota(jnp.int32, (cols, slots), 0)
        weight_x = jnp.where(along == col, 1.0 - frac_x, jnp.where(along == col + 1, frac_x, 0.0))
        across = lax.broadcasted_iota(jnp.int32, (rows, slots), 0)
        weight_y = jnp.where(across == row, 1.0 - frac_y, jnp.where(across == row + 1, frac_y, 0.0))
        partial = lax.dot_general(
            profile_ref[...].reshape(records * rows, cols),
            weight_x,
            NN,
            precision=lax.Precision.HIGHEST,
            preferred_element_type=jnp.float32,
        ).reshape(records, rows, slots)
        interp = jnp.sum(partial * weight_y[None], axis=1)
        slot = lax.broadcasted_iota(jnp.int32, (1, slots), 1)
        interp = interp * (slot < count_ref[0]).astype(jnp.float32)
        earlier = lax.broadcasted_iota(jnp.int32, (slots, slots), 0) < lax.broadcasted_iota(
            jnp.int32, (slots, slots), 1
        )
        owner = owner_ref[...]
        same = jnp.where((column_ref[...] == owner) & earlier, 1.0, 0.0)
        rank = jnp.sum(same, axis=0, keepdims=True).astype(jnp.int32)
        padded = jnp.concatenate(
            [interp, jnp.zeros((RANK_ROWS - records, slots), jnp.float32)], axis=0
        )
        ranked = jnp.concatenate(
            [jnp.where(rank == r, padded, 0.0) for r in range(CAP)], axis=0
        )
        ranked = jnp.concatenate(
            [ranked, jnp.zeros((LANES - CAP * RANK_ROWS, slots), jnp.float32)], axis=0
        )
        to_owner = (owner == lax.broadcasted_iota(jnp.int32, (devices, slots), 0)).astype(
            jnp.float32
        )
        send_ref[...] = lax.dot_general(
            to_owner, ranked, NT, precision=lax.Precision.HIGHEST, preferred_element_type=jnp.float32
        )

    operands = [me, ssh_coef, obs_count, kappa, sea_mask, sigma, beta,
                owner_row, tile_index, obs_frac, owner_col] + extra + returned
    outs = [
        jax.ShapeDtypeStruct((2, levels, rows, cols), jnp.float32),
        jax.ShapeDtypeStruct((rows, cols), jnp.float32),
        jax.ShapeDtypeStruct((devices, LANES), jnp.float32),
    ]
    moved = sum(a.size * a.dtype.itemsize for a in operands + outs)
    return pl.pallas_call(
        kernel,
        out_shape=outs,
        in_specs=[pl.BlockSpec(memory_space=pltpu.SMEM)] * 3
        + [pl.BlockSpec(memory_space=pltpu.VMEM)] * (len(operands) - 3),
        out_specs=[pl.BlockSpec(memory_space=pltpu.VMEM)] * 3,
        scratch_shapes=[pltpu.VMEM((records, rows, cols), jnp.float32), plan.tiles],
        compiler_params=pltpu.CompilerParams(vmem_limit_bytes=32 * 2**20),
        cost_estimate=pl.CostEstimate(flops=10**7, bytes_accessed=moved, transcendentals=0),
    )(*operands)


def receive(arrived, records):
    devices = arrived.shape[0]

    def kernel(in_ref, out_ref):
        turned = jnp.transpose(in_ref[...])
        for r in range(CAP):
            out_ref[r] = turned[r * RANK_ROWS : r * RANK_ROWS + records, :]

    return call(kernel, jax.ShapeDtypeStruct((CAP, records, devices), jnp.float32), [arrived])


def body(gx_count, gy_count, control, sigma, kappa, beta, sea_mask, x_inverse, y_inverse, ssh_coef,
         obs_owner, tile_index, obs_frac, obs_count):
    _, kinds, levels, rows, cols = control.shape
    devices = gx_count * gy_count
    plan = Plan(levels, rows, cols, gy_count)
    chunks = kinds
    if not plan.fits:
        plan, chunks = Plan(kinds * levels, rows, cols, gy_count), 1
    me = jnp.stack([lax.axis_index("gx"), lax.axis_index("gy")]).astype(jnp.int32)
    x_high, x_low = prepare_x(x_inverse)
    fields = list(control.reshape(chunks, plan.fields, rows, cols))
    y_parts = None
    result = None
    for step in range(STEPS):
        sent = []
        for chunk in range(chunks):
            held = gather_pieces(fields[chunk], "gx", gx_count)
            masks, pieces = [m for m, _ in held], [p for _, p in held]
            if y_parts is None:
                pieces[1], y_inverse = lax.optimization_barrier((pieces[1], y_inverse))
                held = gather_pieces(y_inverse, "gx", gx_count)
                y_parts = prepare_y([m for m, _ in held], [p for _, p in held], me)
            packed = zonal(plan, masks, pieces, me, x_high, x_low, sea_mask)
            sent.append(exchange(packed, "gy", gy_count))
        for chunk in range(chunks):
            solved = meridional(plan, me, sent[chunk], *y_parts)
            returned = exchange(solved, "gy", gy_count)
            if step < STEPS - 1 or chunk < chunks - 1:
                fields[chunk] = vertical(plan, me, returned, kappa, sea_mask, levels)
            else:
                obs = (
                    obs_owner.reshape(1, -1),
                    tile_index.reshape(1, -1),
                    obs_frac,
                    obs_count,
                    obs_owner,
                )
                result = finish(
                    plan, me, returned, fields[0] if chunks > 1 else None, kappa, sea_mask, sigma,
                    beta, ssh_coef, obs, devices,
                )
    increments, height, outgoing = result
    arrived = lax.all_to_all(outgoing, ("gx", "gy"), split_axis=0, concat_axis=0, tiled=True)
    return increments[None], height[None], receive(arrived, kinds * levels + 1)


def solution(mesh):
    return jax.shard_map(
        functools.partial(body, mesh.shape["gx"], mesh.shape["gy"]),
        mesh=mesh,
        in_specs=(
            P(None, None, None, "gy", "gx"),
            P(None, None, "gy", "gx"),
            P(None, "gy", "gx"),
            P(None, "gy", "gx"),
            P("gy", "gx"),
            P("gx", None),
            P("gx", None),
            P(),
            P(("gx", "gy"), None),
            P(("gx", "gy")),
            P(None, ("gx", "gy")),
            P(("gx", "gy")),
        ),
        out_specs=(
            P(None, None, None, "gy", "gx"),
            P(None, "gy", "gx"),
            P(None, None, ("gx", "gy")),
        ),
        check_vma=False,
    )
```

```python
import functools

import jax
import jax.numpy as jnp
from jax import lax
from jax.experimental import pallas as pl
from jax.experimental.pallas import tpu as pltpu
from jax.sharding import PartitionSpec as P

STEPS = 2
CAP = 2
LANES = 128
SUB = 8
RANK_ROWS = 16
NN = (((1,), (0,)), ((), ()))
NT = (((1,), (1,)), ((), ()))


class Plan:
    def __init__(self, fields, rows, cols, parts):
        self.fields, self.rows, self.cols, self.parts = fields, rows, cols, parts
        self.blocks = cols // LANES
        tiles = fields * self.blocks
        share = fields * cols // parts
        self.full = share // LANES
        self.rest = share % LANES
        self.sides = LANES // self.rest if self.rest else 0
        self.groups = rows // SUB
        self.packs = -(-self.groups // self.sides) if self.rest else 0
        self.width = self.full * rows + self.packs * SUB
        self.columns = (self.full + (1 if self.rest else 0)) * LANES
        self.fits = (
            cols % LANES == 0
            and rows % SUB == 0
            and fields * cols % parts == 0
            and (self.rest == 0 or LANES % self.rest == 0)
            and tiles - self.full * parts == (parts // self.sides if self.rest else 0)
        )

    def moved(self, side, place):
        return ((side - place) * self.rest) % LANES

    def pack_rest(self, tile, place):
        lane_side = lax.broadcasted_iota(jnp.int32, (SUB, LANES), 1) // self.rest
        out = []
        for pack in range(self.packs):
            joined = None
            for side in range(self.sides):
                group = pack * self.sides + side
                if group >= self.groups:
                    break
                piece = turn(tile[group * SUB : (group + 1) * SUB, :], self.moved(side, place))
                joined = piece if joined is None else jnp.where(lane_side == side, piece, joined)
            out.append(joined)
        return out

    def unpack_rest(self, ref, place):
        pieces = []
        for group in range(self.groups):
            pack, side = divmod(group, self.sides)
            start = self.full * self.rows + pack * SUB
            pieces.append(turn(ref[start : start + SUB, :], self.moved(place, side)))
        return jnp.concatenate(pieces, axis=0)

    def store_rest(self, ref, packs):
        for pack, value in enumerate(packs):
            start = self.full * self.rows + pack * SUB
            ref[start : start + SUB, :] = value

    def send_tiles(self, tiles_ref, device, out_ref):
        for i in range(self.full):
            out_ref[i * self.rows : (i + 1) * self.rows, :] = tiles_ref[device * self.full + i]
        if self.rest:
            tile = tiles_ref[self.parts * self.full + device // self.sides]
            self.store_rest(out_ref, self.pack_rest(tile, device % self.sides))

    def take_tiles(self, in_ref, device, tiles_ref):
        for i in range(self.full):
            tiles_ref[device * self.full + i] = in_ref[i * self.rows : (i + 1) * self.rows, :]
        if self.rest:
            place = device % self.sides
            index = self.parts * self.full + device // self.sides
            lane_side = lax.broadcasted_iota(jnp.int32, (self.rows, LANES), 1) // self.rest
            tiles_ref[index] = jnp.where(
                lane_side == place, self.unpack_rest(in_ref, place), tiles_ref[index]
            )

    @property
    def tiles(self):
        return pltpu.VMEM((self.fields * self.blocks, self.rows, LANES), jnp.float32)

    @property
    def blocks_out(self):
        shape = jax.ShapeDtypeStruct((self.width, LANES), jnp.float32)
        return [shape] * self.parts


def part_of(me_ref, mask):
    return (me_ref[1] // 2) ^ mask


def turn(value, shift):
    if isinstance(shift, int) and shift == 0:
        return value
    return pltpu.roll(value, shift, axis=1)


def split(value):
    high = value.astype(jnp.bfloat16)
    low = (value - high.astype(jnp.float32)).astype(jnp.bfloat16)
    return high, low


def dot(a, b, dims=NN):
    return lax.dot_general(a, b, dims, preferred_element_type=jnp.float32)


def dot_split(a, b):
    return dot(a[0], b[0]) + (dot(a[0], b[1]) + dot(a[1], b[0]))


def call(kernel, out_shape, operands, scalars=(), flops=0, scratch=()):
    outs = out_shape if isinstance(out_shape, (list, tuple)) else [out_shape]
    moved = sum(a.size * a.dtype.itemsize for a in list(operands) + list(outs))
    specs = [
        pl.BlockSpec(memory_space=pltpu.SMEM if i in scalars else pltpu.VMEM)
        for i in range(len(operands))
    ]
    out_spec = pl.BlockSpec(memory_space=pltpu.VMEM)
    many = isinstance(out_shape, (list, tuple))
    return pl.pallas_call(
        kernel,
        out_shape=out_shape,
        in_specs=specs,
        out_specs=[out_spec] * len(outs) if many else out_spec,
        scratch_shapes=list(scratch),
        compiler_params=pltpu.CompilerParams(vmem_limit_bytes=min(48, 6 + 3 * moved // 2**20) * 2**20),
        cost_estimate=pl.CostEstimate(flops=flops, bytes_accessed=moved, transcendentals=0),
    )(*operands)


def after(value, *others):
    return lax.optimization_barrier((value,) + others)[0]


def gather_pieces(block, axis, count, hold=None):
    held = [(0, block)]
    bit = count // 2
    if bit > 1 and hold is not None:
        first = lax.ppermute(block, axis, [(i, i ^ bit) for i in range(count)])
        held = held + [(bit, after(first, *hold))]
        bit //= 2
    while bit:
        pairs = [(i, i ^ bit) for i in range(count)]
        held = held + [(mask ^ bit, lax.ppermute(piece, axis, pairs)) for mask, piece in held]
        bit //= 2
    return held


def exchange(blocks, axis, count):
    out = [blocks[0]] + [None] * (len(blocks) - 1)
    for mask in range(len(blocks) - 1, 0, -1):
        pairs = [(i, i ^ (2 * mask)) for i in range(count)]
        out[mask] = lax.ppermute(blocks[mask], axis, pairs)
    return out


def prepare_x(x_inverse):
    rows, cols = x_inverse.shape

    def kernel(x_ref, high_ref, low_ref):
        for start in range(0, cols, rows):
            high, low = split(jnp.transpose(x_ref[:, start : start + rows]))
            high_ref[start : start + rows, :] = high
            low_ref[start : start + rows, :] = low

    shape = jax.ShapeDtypeStruct((cols, rows), jnp.bfloat16)
    return call(kernel, [shape, shape], [x_inverse])


def prepare_y(masks, pieces, me, rows):
    owned, half = pieces[0].shape

    def kernel(me_ref, *refs):
        high_ref, low_ref, whole_ref = refs[-3:]
        side = lax.rem(me_ref[1], 2)
        for mask, ref in zip(masks, refs):
            start = pl.multiple_of((me_ref[0] ^ mask) * owned, owned)
            whole_ref[pl.ds(start, owned), :] = ref[...]
        for other in range(2):
            for part in range(half // rows):
                start = pl.multiple_of((2 * part + (side ^ other)) * rows, rows)
                high, low = split(whole_ref[pl.ds(start, rows), :])
                out = other * half + part * rows
                high_ref[out : out + rows, :] = high
                low_ref[out : out + rows, :] = low

    shape = jax.ShapeDtypeStruct((2 * half, half), jnp.bfloat16)
    return call(
        kernel,
        [shape, shape],
        [me] + pieces,
        scalars=(0,),
        scratch=[pltpu.VMEM((2 * half, half), jnp.float32)],
    )


def zonal(plan, masks, pieces, me, x_high, x_low, sea_mask):
    fields, rows, cols, parts = plan.fields, plan.rows, plan.cols, plan.parts

    def kernel(me_ref, high_ref, low_ref, sea_ref, *refs):
        out_refs, tiles_ref = refs[-parts - 1 : -1], refs[-1]
        total = None
        for mask, ref in zip(masks, refs):
            start = pl.multiple_of((me_ref[0] ^ mask) * cols, cols)
            values = split(ref[...].reshape(fields * rows, cols))
            weights = (high_ref[pl.ds(start, cols), :], low_ref[pl.ds(start, cols), :])
            part = dot_split(values, weights)
            total = part if total is None else total + part
        total = total.reshape(fields, rows, cols)
        sea = sea_ref[...].astype(jnp.float32)
        for block in range(plan.blocks):
            lanes = slice(block * LANES, (block + 1) * LANES)
            for field in range(fields):
                tiles_ref[field * plan.blocks + block] = sea[:, lanes] * total[field, :, lanes]
        for mask in range(parts):
            plan.send_tiles(tiles_ref, part_of(me_ref, mask), out_refs[mask])

    return call(
        kernel,
        plan.blocks_out,
        [me, x_high, x_low, sea_mask] + pieces,
        scalars=(0,),
        flops=6 * fields * rows * cols * cols * len(pieces),
        scratch=[plan.tiles],
    )


def meridional(plan, me, lines, y_high, y_low):
    rows, parts = plan.rows, plan.parts

    def kernel(me_ref, high_ref, low_ref, *refs):
        in_refs, out_refs, lines_ref, solved_ref = refs[:parts], refs[parts:-2], refs[-2], refs[-1]
        for mask in range(parts):
            place = pl.ds(pl.multiple_of(part_of(me_ref, mask) * rows, rows), rows)
            for i in range(plan.full):
                lanes = slice(i * LANES, (i + 1) * LANES)
                lines_ref[place, lanes] = in_refs[mask][i * rows : (i + 1) * rows, :]
            if plan.rest:
                lines_ref[place, plan.full * LANES :] = plan.unpack_rest(in_refs[mask], 0)
        solved_ref[...] = dot_split((high_ref[...], low_ref[...]), split(lines_ref[...]))
        for other in range(2):
            for part in range(parts):
                start = (other * parts + part) * rows
                for i in range(plan.full):
                    lanes = slice(i * LANES, (i + 1) * LANES)
                    out_refs[other][part, i * rows : (i + 1) * rows, :] = solved_ref[
                        start : start + rows, lanes
                    ]
                if plan.rest:
                    last = solved_ref[start : start + rows, plan.full * LANES :]
                    plan.store_rest(out_refs[other].at[part], plan.pack_rest(last, 0))

    shape = jax.ShapeDtypeStruct((parts, plan.width, LANES), jnp.float32)
    return call(
        kernel,
        [shape, shape],
        [me, y_high, y_low] + lines,
        scalars=(0,),
        flops=12 * (parts * rows) ** 2 * plan.columns,
        scratch=[
            pltpu.VMEM((parts * rows, plan.columns), jnp.float32),
            pltpu.VMEM((2 * parts * rows, plan.columns), jnp.float32),
        ],
    )


def add_sides(plan, me, own, other):
    def kernel(me_ref, own_ref, other_ref, *out_refs):
        for mask in range(plan.parts):
            part = part_of(me_ref, mask)
            out_refs[mask][...] = own_ref[part] + other_ref[part]

    return call(kernel, plan.blocks_out, [me, own, other], scalars=(0,))


def solve_columns(plan, me_ref, in_refs, tiles_ref, kappa_ref, sea_ref, levels, store):
    kinds = plan.fields // levels
    for mask in range(plan.parts):
        plan.take_tiles(in_refs[mask], part_of(me_ref, mask), tiles_ref)
    for block in range(plan.blocks):
        lanes = slice(block * LANES, (block + 1) * LANES)
        sea = sea_ref[:, lanes].astype(jnp.float32)
        inverse, upper = [], []
        kappa = [kappa_ref[level, :, lanes] for level in range(levels - 1)]
        for level in range(levels):
            below = kappa[level - 1] if level > 0 else 0.0
            above = kappa[level] if level < levels - 1 else 0.0
            pivot = 1.0 + below + above
            if level > 0:
                pivot = pivot + below * upper[-1]
            inverse.append(1.0 / pivot)
            upper.append(-above * inverse[-1])
        for kind in range(kinds):
            forward = []
            for level in range(levels):
                tile = tiles_ref[(kind * levels + level) * plan.blocks + block]
                right = sea * tile
                if level > 0:
                    right = right + kappa[level - 1] * forward[-1]
                forward.append(right * inverse[level])
            value = forward[-1]
            store(kind, levels - 1, lanes, value)
            for level in range(levels - 2, -1, -1):
                value = forward[level] - upper[level] * value
                store(kind, level, lanes, value)


def vertical(plan, me, returned, kappa, sea_mask, levels):
    def kernel(me_ref, kappa_ref, sea_ref, *refs):
        in_refs, (out_ref, tiles_ref) = refs[: plan.parts], refs[plan.parts :]

        def store(kind, level, lanes, value):
            out_ref[kind * levels + level, :, lanes] = value

        solve_columns(plan, me_ref, in_refs, tiles_ref, kappa_ref, sea_ref, levels, store)

    return call(
        kernel,
        jax.ShapeDtypeStruct((plan.fields, plan.rows, plan.cols), jnp.float32),
        [me, kappa, sea_mask] + returned,
        scalars=(0,),
        scratch=[plan.tiles],
    )


def finish(plan, me, returned, temper_field, kappa, sea_mask, sigma, beta, ssh_coef, obs, devices):
    levels = sigma.shape[1]
    rows, cols = plan.rows, plan.cols
    records = 2 * levels + 1
    owner_row, tile_index, obs_frac, obs_count, owner_col = obs
    slots = owner_row.shape[1]
    extra = [] if temper_field is None else [temper_field]

    def kernel(me_ref, ssh_ref, count_ref, kappa_ref, sea_ref, sigma_ref, beta_ref,
               owner_ref, tile_ref, frac_ref, column_ref, *refs):
        inc_ref, height_ref, send_ref, profile_ref, tiles_ref = refs[-5:]

        def store(kind, level, lanes, value):
            profile_ref[(kind + len(extra)) * levels + level, :, lanes] = value

        solve_columns(
            plan, me_ref, refs[len(extra) :], tiles_ref, kappa_ref, sea_ref, levels, store
        )
        for block in range(plan.blocks):
            lanes = slice(block * LANES, (block + 1) * LANES)
            height = None
            for level in range(levels):
                source = refs[0] if extra else profile_ref
                temper = sigma_ref[0, level, :, lanes] * source[level, :, lanes]
                saline = (
                    sigma_ref[1, level, :, lanes] * profile_ref[levels + level, :, lanes]
                    + beta_ref[level, :, lanes] * temper
                )
                term = ssh_ref[0, level] * temper + ssh_ref[1, level] * saline
                height = term if height is None else height + term
                profile_ref[level, :, lanes] = temper
                profile_ref[levels + level, :, lanes] = saline
                inc_ref[0, level, :, lanes] = temper
                inc_ref[1, level, :, lanes] = saline
            profile_ref[2 * levels, :, lanes] = height
            height_ref[:, lanes] = height

        cell = tile_ref[...]
        row, col = cell // cols, cell % cols
        frac_x, frac_y = frac_ref[0:1, :], frac_ref[1:2, :]
        along = lax.broadcasted_iota(jnp.int32, (cols, slots), 0)
        weight_x = jnp.where(along == col, 1.0 - frac_x, jnp.where(along == col + 1, frac_x, 0.0))
        across = lax.broadcasted_iota(jnp.int32, (rows, slots), 0)
        weight_y = jnp.where(across == row, 1.0 - frac_y, jnp.where(across == row + 1, frac_y, 0.0))
        partial = lax.dot_general(
            profile_ref[...].reshape(records * rows, cols),
            weight_x,
            NN,
            precision=lax.Precision.HIGHEST,
            preferred_element_type=jnp.float32,
        ).reshape(records, rows, slots)
        interp = jnp.sum(partial * weight_y[None], axis=1)
        slot = lax.broadcasted_iota(jnp.int32, (1, slots), 1)
        interp = interp * (slot < count_ref[0]).astype(jnp.float32)
        earlier = lax.broadcasted_iota(jnp.int32, (slots, slots), 0) < lax.broadcasted_iota(
            jnp.int32, (slots, slots), 1
        )
        owner = owner_ref[...]
        same = jnp.where((column_ref[...] == owner) & earlier, 1.0, 0.0)
        rank = jnp.sum(same, axis=0, keepdims=True).astype(jnp.int32)
        padded = jnp.concatenate(
            [interp, jnp.zeros((RANK_ROWS - records, slots), jnp.float32)], axis=0
        )
        ranked = jnp.concatenate(
            [jnp.where(rank == r, padded, 0.0) for r in range(CAP)], axis=0
        )
        ranked = jnp.concatenate(
            [ranked, jnp.zeros((LANES - CAP * RANK_ROWS, slots), jnp.float32)], axis=0
        )
        to_owner = (owner == lax.broadcasted_iota(jnp.int32, (devices, slots), 0)).astype(
            jnp.float32
        )
        send_ref[...] = lax.dot_general(
            to_owner, ranked, NT, precision=lax.Precision.HIGHEST, preferred_element_type=jnp.float32
        )

    operands = [me, ssh_coef, obs_count, kappa, sea_mask, sigma, beta,
                owner_row, tile_index, obs_frac, owner_col] + extra + returned
    outs = [
        jax.ShapeDtypeStruct((2, levels, rows, cols), jnp.float32),
        jax.ShapeDtypeStruct((rows, cols), jnp.float32),
        jax.ShapeDtypeStruct((devices, LANES), jnp.float32),
    ]
    moved = sum(a.size * a.dtype.itemsize for a in operands + outs)
    return pl.pallas_call(
        kernel,
        out_shape=outs,
        in_specs=[pl.BlockSpec(memory_space=pltpu.SMEM)] * 3
        + [pl.BlockSpec(memory_space=pltpu.VMEM)] * (len(operands) - 3),
        out_specs=[pl.BlockSpec(memory_space=pltpu.VMEM)] * 3,
        scratch_shapes=[pltpu.VMEM((records, rows, cols), jnp.float32), plan.tiles],
        compiler_params=pltpu.CompilerParams(vmem_limit_bytes=32 * 2**20),
        cost_estimate=pl.CostEstimate(flops=10**7, bytes_accessed=moved, transcendentals=0),
    )(*operands)


def receive(arrived, records):
    devices = arrived.shape[0]

    def kernel(in_ref, out_ref):
        turned = jnp.transpose(in_ref[...])
        for r in range(CAP):
            out_ref[:, r, :] = turned[r * RANK_ROWS : r * RANK_ROWS + records, :]

    out = call(kernel, jax.ShapeDtypeStruct((records, CAP, devices), jnp.float32), [arrived])
    return jnp.swapaxes(out, 0, 1)


def body(gx_count, gy_count, control, sigma, kappa, beta, sea_mask, x_inverse, y_inverse, ssh_coef,
         obs_owner, tile_index, obs_frac, obs_count):
    _, kinds, levels, rows, cols = control.shape
    devices = gx_count * gy_count
    plan = Plan(levels, rows, cols, gy_count // 2)
    chunks = kinds
    if not plan.fits:
        plan, chunks = Plan(kinds * levels, rows, cols, gy_count // 2), 1
    me = jnp.stack([lax.axis_index("gx"), lax.axis_index("gy")]).astype(jnp.int32)
    x_high, x_low = prepare_x(x_inverse)
    fields = list(control.reshape(chunks, plan.fields, rows, cols))
    y_columns = y_inverse.reshape(y_inverse.shape[0], gy_count // 2, 2, rows)
    y_columns = jnp.where(me[1] % 2 == 0, y_columns[:, :, 0], y_columns[:, :, 1])
    y_columns = y_columns.reshape(y_inverse.shape[0], -1)
    y_parts = first_pieces = result = None
    for step in range(STEPS):
        sent = []
        for chunk in range(chunks):
            hold = None
            if first_pieces is not None and step == 0:
                fields[chunk] = after(fields[chunk], *first_pieces)
                hold = sent[0][plan.parts // 2 :]
            held = gather_pieces(fields[chunk], "gx", gx_count, hold)
            masks, pieces = [m for m, _ in held], [p for _, p in held]
            packed = zonal(plan, masks, pieces, me, x_high, x_low, sea_mask)
            sent.append(exchange(packed, "gy", gy_count))
            if y_parts is None:
                held = gather_pieces(y_columns, "gx", gx_count)
                first_pieces = [pieces[1], held[1][1]]
                y_parts = prepare_y([m for m, _ in held], [p for _, p in held], me, rows)
        for chunk in range(chunks):
            own, other = meridional(plan, me, sent[chunk], *y_parts)
            other = lax.ppermute(other, "gy", [(i, i ^ 1) for i in range(gy_count)])
            returned = exchange(add_sides(plan, me, own, other), "gy", gy_count)
            if step < STEPS - 1 or chunk < chunks - 1:
                fields[chunk] = vertical(plan, me, returned, kappa, sea_mask, levels)
            else:
                obs = (
                    obs_owner.reshape(1, -1),
                    tile_index.reshape(1, -1),
                    obs_frac,
                    obs_count,
                    obs_owner,
                )
                result = finish(
                    plan, me, returned, fields[0] if chunks > 1 else None, kappa, sea_mask, sigma,
                    beta, ssh_coef, obs, devices,
                )
    increments, height, outgoing = result
    arrived = lax.all_to_all(outgoing, ("gx", "gy"), split_axis=0, concat_axis=0, tiled=True)
    return increments[None], height[None], receive(arrived, kinds * levels + 1)


def solution(mesh):
    return jax.shard_map(
        functools.partial(body, mesh.shape["gx"], mesh.shape["gy"]),
        mesh=mesh,
        in_specs=(
            P(None, None, None, "gy", "gx"),
            P(None, None, "gy", "gx"),
            P(None, "gy", "gx"),
            P(None, "gy", "gx"),
            P("gy", "gx"),
            P("gx", None),
            P("gx", None),
            P(),
            P(("gx", "gy"), None),
            P(("gx", "gy")),
            P(None, ("gx", "gy")),
            P(("gx", "gy")),
        ),
        out_specs=(
            P(None, None, None, "gy", "gx"),
            P(None, "gy", "gx"),
            P(None, None, ("gx", "gy")),
        ),
        check_vma=False,
    )
```

```python
import functools

import jax
import jax.numpy as jnp
from jax import lax
from jax.experimental import pallas as pl
from jax.experimental.pallas import tpu as pltpu
from jax.sharding import PartitionSpec as P

STEPS = 2
CAP = 2
LANES = 128
SUB = 8
RANK_ROWS = 16
NN = (((1,), (0,)), ((), ()))
NT = (((1,), (1,)), ((), ()))


class Plan:
    def __init__(self, fields, rows, cols, parts):
        self.fields, self.rows, self.cols, self.parts = fields, rows, cols, parts
        self.blocks = cols // LANES
        tiles = fields * self.blocks
        share = fields * cols // parts
        self.full = share // LANES
        self.rest = share % LANES
        self.sides = LANES // self.rest if self.rest else 0
        self.groups = rows // SUB
        self.packs = -(-self.groups // self.sides) if self.rest else 0
        self.width = self.full * rows + self.packs * SUB
        self.columns = (self.full + (1 if self.rest else 0)) * LANES
        self.fits = (
            cols % LANES == 0
            and rows % SUB == 0
            and fields * cols % parts == 0
            and (self.rest == 0 or LANES % self.rest == 0)
            and tiles - self.full * parts == (parts // self.sides if self.rest else 0)
        )

    def moved(self, side, place):
        return ((side - place) * self.rest) % LANES

    def pack_rest(self, tile, place):
        lane_side = lax.broadcasted_iota(jnp.int32, (SUB, LANES), 1) // self.rest
        out = []
        for pack in range(self.packs):
            joined = None
            for side in range(self.sides):
                group = pack * self.sides + side
                if group >= self.groups:
                    break
                piece = turn(tile[group * SUB : (group + 1) * SUB, :], self.moved(side, place))
                joined = piece if joined is None else jnp.where(lane_side == side, piece, joined)
            out.append(joined)
        return out

    def unpack_rest(self, ref, place):
        pieces = []
        for group in range(self.groups):
            pack, side = divmod(group, self.sides)
            start = self.full * self.rows + pack * SUB
            pieces.append(turn(ref[start : start + SUB, :], self.moved(place, side)))
        return jnp.concatenate(pieces, axis=0)

    def store_rest(self, ref, packs):
        for pack, value in enumerate(packs):
            start = self.full * self.rows + pack * SUB
            ref[start : start + SUB, :] = value

    def send_tiles(self, tiles_ref, device, out_ref):
        for i in range(self.full):
            out_ref[i * self.rows : (i + 1) * self.rows, :] = tiles_ref[device * self.full + i]
        if self.rest:
            tile = tiles_ref[self.parts * self.full + device // self.sides]
            self.store_rest(out_ref, self.pack_rest(tile, device % self.sides))

    def take_tiles(self, in_ref, device, tiles_ref):
        for i in range(self.full):
            tiles_ref[device * self.full + i] = in_ref[i * self.rows : (i + 1) * self.rows, :]
        if self.rest:
            place = device % self.sides
            index = self.parts * self.full + device // self.sides
            lane_side = lax.broadcasted_iota(jnp.int32, (self.rows, LANES), 1) // self.rest
            tiles_ref[index] = jnp.where(
                lane_side == place, self.unpack_rest(in_ref, place), tiles_ref[index]
            )

    @property
    def tiles(self):
        return pltpu.VMEM((self.fields * self.blocks, self.rows, LANES), jnp.float32)

    @property
    def blocks_out(self):
        shape = jax.ShapeDtypeStruct((self.width, LANES), jnp.float32)
        return [shape] * self.parts


def part_of(me_ref, mask):
    return (me_ref[1] // 2) ^ mask


def turn(value, shift):
    if isinstance(shift, int) and shift == 0:
        return value
    return pltpu.roll(value, shift, axis=1)


def split(value):
    high = value.astype(jnp.bfloat16)
    low = (value - high.astype(jnp.float32)).astype(jnp.bfloat16)
    return high, low


def dot(a, b, dims=NN):
    return lax.dot_general(a, b, dims, preferred_element_type=jnp.float32)


def dot_split(a, b):
    return dot(a[0], b[0]) + (dot(a[0], b[1]) + dot(a[1], b[0]))


def call(kernel, out_shape, operands, scalars=(), flops=0, scratch=()):
    outs = out_shape if isinstance(out_shape, (list, tuple)) else [out_shape]
    moved = sum(a.size * a.dtype.itemsize for a in list(operands) + list(outs))
    specs = [
        pl.BlockSpec(memory_space=pltpu.SMEM if i in scalars else pltpu.VMEM)
        for i in range(len(operands))
    ]
    out_spec = pl.BlockSpec(memory_space=pltpu.VMEM)
    many = isinstance(out_shape, (list, tuple))
    return pl.pallas_call(
        kernel,
        out_shape=out_shape,
        in_specs=specs,
        out_specs=[out_spec] * len(outs) if many else out_spec,
        scratch_shapes=list(scratch),
        compiler_params=pltpu.CompilerParams(vmem_limit_bytes=min(48, 6 + 3 * moved // 2**20) * 2**20),
        cost_estimate=pl.CostEstimate(flops=1, bytes_accessed=1, transcendentals=0),
    )(*operands)


def after(value, *others):
    return lax.optimization_barrier((value,) + others)[0]


def gather_near(block, axis, count):
    pairs = [(i, i ^ 1) for i in range(count)]
    return [(0, block), (1, lax.ppermute(block, axis, pairs))]


def gather_far(block, axis, count, hold=()):
    held = [(0, block)]
    bit = count // 2
    while bit:
        pairs = [(i, i ^ bit) for i in range(count)]
        sources = held if bit > 1 else held[1:]
        brought = [(mask ^ bit, lax.ppermute(piece, axis, pairs)) for mask, piece in sources]
        if hold and bit == count // 2 and bit > 1:
            brought = [(mask, after(piece, *hold)) for mask, piece in brought]
        held = held + brought
        bit //= 2
    return held[1:]


def exchange(blocks, axis, count):
    out = [blocks[0]] + [None] * (len(blocks) - 1)
    for mask in range(len(blocks) - 1, 0, -1):
        pairs = [(i, i ^ (2 * mask)) for i in range(count)]
        out[mask] = lax.ppermute(blocks[mask], axis, pairs)
    return out


def prepare_x(x_inverse):
    rows, cols = x_inverse.shape

    def kernel(x_ref, high_ref, low_ref):
        for start in range(0, cols, rows):
            high, low = split(jnp.transpose(x_ref[:, start : start + rows]))
            high_ref[start : start + rows, :] = high
            low_ref[start : start + rows, :] = low

    shape = jax.ShapeDtypeStruct((cols, rows), jnp.bfloat16)
    return call(kernel, [shape, shape], [x_inverse])


def prepare_y(masks, pieces, me, rows):
    owned, half = pieces[0].shape

    def kernel(me_ref, *refs):
        high_ref, low_ref, whole_ref = refs[-3:]
        side = lax.rem(me_ref[1], 2)
        for mask, ref in zip(masks, refs):
            start = pl.multiple_of((me_ref[0] ^ mask) * owned, owned)
            whole_ref[pl.ds(start, owned), :] = ref[...]
        for other in range(2):
            for part in range(half // rows):
                start = pl.multiple_of((2 * part + (side ^ other)) * rows, rows)
                high, low = split(whole_ref[pl.ds(start, rows), :])
                out = other * half + part * rows
                high_ref[out : out + rows, :] = high
                low_ref[out : out + rows, :] = low

    shape = jax.ShapeDtypeStruct((2 * half, half), jnp.bfloat16)
    return call(
        kernel,
        [shape, shape],
        [me] + pieces,
        scalars=(0,),
        scratch=[pltpu.VMEM((2 * half, half), jnp.float32)],
    )


def add_zonal(total, masks, me_ref, high_ref, low_ref, refs):
    for mask, ref in zip(masks, refs):
        fields, rows, cols = ref.shape
        start = pl.multiple_of((me_ref[0] ^ mask) * cols, cols)
        values = split(ref[...].reshape(fields * rows, cols))
        weights = (high_ref[pl.ds(start, cols), :], low_ref[pl.ds(start, cols), :])
        part = dot_split(values, weights)
        total = part if total is None else total + part
    return total


def zonal_start(plan, held, me, x_high, x_low):
    masks, pieces = [m for m, _ in held], [p for _, p in held]

    def kernel(me_ref, high_ref, low_ref, *refs):
        refs[-1][...] = add_zonal(None, masks, me_ref, high_ref, low_ref, refs)

    return call(
        kernel,
        jax.ShapeDtypeStruct((plan.fields * plan.rows, plan.cols), jnp.float32),
        [me, x_high, x_low] + pieces,
        scalars=(0,),
        flops=6 * plan.fields * plan.rows * plan.cols**2 * len(pieces),
    )


def zonal_end(plan, total, held, me, x_high, x_low, sea_mask):
    fields, rows, cols, parts = plan.fields, plan.rows, plan.cols, plan.parts
    masks, pieces = [m for m, _ in held], [p for _, p in held]

    def kernel(me_ref, high_ref, low_ref, sea_ref, total_ref, *refs):
        out_refs, tiles_ref = refs[-parts - 1 : -1], refs[-1]
        result = add_zonal(total_ref[...], masks, me_ref, high_ref, low_ref, refs)
        result = result.reshape(fields, rows, cols)
        sea = sea_ref[...].astype(jnp.float32)
        for block in range(plan.blocks):
            lanes = slice(block * LANES, (block + 1) * LANES)
            for field in range(fields):
                tiles_ref[field * plan.blocks + block] = sea[:, lanes] * result[field, :, lanes]
        for mask in range(parts):
            plan.send_tiles(tiles_ref, part_of(me_ref, mask), out_refs[mask])

    return call(
        kernel,
        plan.blocks_out,
        [me, x_high, x_low, sea_mask, total] + pieces,
        scalars=(0,),
        flops=6 * fields * rows * cols**2 * len(pieces),
        scratch=[plan.tiles],
    )


def meridional(plan, me, lines, y_high, y_low):
    rows, parts = plan.rows, plan.parts

    def kernel(me_ref, high_ref, low_ref, *refs):
        in_refs, out_refs, lines_ref, solved_ref = refs[:parts], refs[parts:-2], refs[-2], refs[-1]
        for mask in range(parts):
            place = pl.ds(pl.multiple_of(part_of(me_ref, mask) * rows, rows), rows)
            for i in range(plan.full):
                lanes = slice(i * LANES, (i + 1) * LANES)
                lines_ref[place, lanes] = in_refs[mask][i * rows : (i + 1) * rows, :]
            if plan.rest:
                lines_ref[place, plan.full * LANES :] = plan.unpack_rest(in_refs[mask], 0)
        solved_ref[...] = dot_split((high_ref[...], low_ref[...]), split(lines_ref[...]))
        for other in range(2):
            for part in range(parts):
                start = (other * parts + part) * rows
                for i in range(plan.full):
                    lanes = slice(i * LANES, (i + 1) * LANES)
                    out_refs[other][part, i * rows : (i + 1) * rows, :] = solved_ref[
                        start : start + rows, lanes
                    ]
                if plan.rest:
                    last = solved_ref[start : start + rows, plan.full * LANES :]
                    plan.store_rest(out_refs[other].at[part], plan.pack_rest(last, 0))

    shape = jax.ShapeDtypeStruct((parts, plan.width, LANES), jnp.float32)
    return call(
        kernel,
        [shape, shape],
        [me, y_high, y_low] + lines,
        scalars=(0,),
        flops=12 * (parts * rows) ** 2 * plan.columns,
        scratch=[
            pltpu.VMEM((parts * rows, plan.columns), jnp.float32),
            pltpu.VMEM((2 * parts * rows, plan.columns), jnp.float32),
        ],
    )


def add_sides(plan, me, own, other):
    def kernel(me_ref, own_ref, other_ref, *out_refs):
        for mask in range(plan.parts):
            part = part_of(me_ref, mask)
            out_refs[mask][...] = own_ref[part] + other_ref[part]

    return call(kernel, plan.blocks_out, [me, own, other], scalars=(0,))


def solve_columns(plan, me_ref, in_refs, tiles_ref, kappa_ref, sea_ref, levels, store):
    kinds = plan.fields // levels
    for mask in range(plan.parts):
        plan.take_tiles(in_refs[mask], part_of(me_ref, mask), tiles_ref)
    for block in range(plan.blocks):
        lanes = slice(block * LANES, (block + 1) * LANES)
        sea = sea_ref[:, lanes].astype(jnp.float32)
        inverse, upper = [], []
        kappa = [kappa_ref[level, :, lanes] for level in range(levels - 1)]
        for level in range(levels):
            below = kappa[level - 1] if level > 0 else 0.0
            above = kappa[level] if level < levels - 1 else 0.0
            pivot = 1.0 + below + above
            if level > 0:
                pivot = pivot + below * upper[-1]
            inverse.append(1.0 / pivot)
            upper.append(-above * inverse[-1])
        for kind in range(kinds):
            forward = []
            for level in range(levels):
                tile = tiles_ref[(kind * levels + level) * plan.blocks + block]
                right = sea * tile
                if level > 0:
                    right = right + kappa[level - 1] * forward[-1]
                forward.append(right * inverse[level])
            value = forward[-1]
            store(kind, levels - 1, lanes, value)
            for level in range(levels - 2, -1, -1):
                value = forward[level] - upper[level] * value
                store(kind, level, lanes, value)


def vertical(plan, me, returned, kappa, sea_mask, levels):
    def kernel(me_ref, kappa_ref, sea_ref, *refs):
        in_refs, (out_ref, tiles_ref) = refs[: plan.parts], refs[plan.parts :]

        def store(kind, level, lanes, value):
            out_ref[kind * levels + level, :, lanes] = value

        solve_columns(plan, me_ref, in_refs, tiles_ref, kappa_ref, sea_ref, levels, store)

    return call(
        kernel,
        jax.ShapeDtypeStruct((plan.fields, plan.rows, plan.cols), jnp.float32),
        [me, kappa, sea_mask] + returned,
        scalars=(0,),
        scratch=[plan.tiles],
    )


def finish(plan, me, returned, temper_field, kappa, sea_mask, sigma, beta, ssh_coef, obs, devices):
    levels = sigma.shape[1]
    rows, cols = plan.rows, plan.cols
    records = 2 * levels + 1
    owner_row, tile_index, obs_frac, obs_count, owner_col = obs
    slots = owner_row.shape[1]
    extra = [] if temper_field is None else [temper_field]

    def kernel(me_ref, ssh_ref, count_ref, kappa_ref, sea_ref, sigma_ref, beta_ref,
               owner_ref, tile_ref, frac_ref, column_ref, *refs):
        inc_ref, height_ref, send_ref, profile_ref, tiles_ref = refs[-5:]

        def store(kind, level, lanes, value):
            profile_ref[(kind + len(extra)) * levels + level, :, lanes] = value

        solve_columns(
            plan, me_ref, refs[len(extra) :], tiles_ref, kappa_ref, sea_ref, levels, store
        )
        for block in range(plan.blocks):
            lanes = slice(block * LANES, (block + 1) * LANES)
            height = None
            for level in range(levels):
                source = refs[0] if extra else profile_ref
                temper = sigma_ref[0, level, :, lanes] * source[level, :, lanes]
                saline = (
                    sigma_ref[1, level, :, lanes] * profile_ref[levels + level, :, lanes]
                    + beta_ref[level, :, lanes] * temper
                )
                term = ssh_ref[0, level] * temper + ssh_ref[1, level] * saline
                height = term if height is None else height + term
                profile_ref[level, :, lanes] = temper
                profile_ref[levels + level, :, lanes] = saline
                inc_ref[0, level, :, lanes] = temper
                inc_ref[1, level, :, lanes] = saline
            profile_ref[2 * levels, :, lanes] = height
            height_ref[:, lanes] = height

        cell = tile_ref[...]
        row, col = cell // cols, cell % cols
        frac_x, frac_y = frac_ref[0:1, :], frac_ref[1:2, :]
        along = lax.broadcasted_iota(jnp.int32, (cols, slots), 0)
        weight_x = jnp.where(along == col, 1.0 - frac_x, jnp.where(along == col + 1, frac_x, 0.0))
        across = lax.broadcasted_iota(jnp.int32, (rows, slots), 0)
        weight_y = jnp.where(across == row, 1.0 - frac_y, jnp.where(across == row + 1, frac_y, 0.0))
        partial = lax.dot_general(
            profile_ref[...].reshape(records * rows, cols),
            weight_x,
            NN,
            precision=lax.Precision.HIGHEST,
            preferred_element_type=jnp.float32,
        ).reshape(records, rows, slots)
        interp = jnp.sum(partial * weight_y[None], axis=1)
        slot = lax.broadcasted_iota(jnp.int32, (1, slots), 1)
        interp = interp * (slot < count_ref[0]).astype(jnp.float32)
        earlier = lax.broadcasted_iota(jnp.int32, (slots, slots), 0) < lax.broadcasted_iota(
            jnp.int32, (slots, slots), 1
        )
        owner = owner_ref[...]
        same = jnp.where((column_ref[...] == owner) & earlier, 1.0, 0.0)
        rank = jnp.sum(same, axis=0, keepdims=True).astype(jnp.int32)
        padded = jnp.concatenate(
            [interp, jnp.zeros((RANK_ROWS - records, slots), jnp.float32)], axis=0
        )
        ranked = jnp.concatenate(
            [jnp.where(rank == r, padded, 0.0) for r in range(CAP)], axis=0
        )
        ranked = jnp.concatenate(
            [ranked, jnp.zeros((LANES - CAP * RANK_ROWS, slots), jnp.float32)], axis=0
        )
        to_owner = (owner == lax.broadcasted_iota(jnp.int32, (devices, slots), 0)).astype(
            jnp.float32
        )
        send_ref[...] = lax.dot_general(
            to_owner, ranked, NT, precision=lax.Precision.HIGHEST, preferred_element_type=jnp.float32
        )

    operands = [me, ssh_coef, obs_count, kappa, sea_mask, sigma, beta,
                owner_row, tile_index, obs_frac, owner_col] + extra + returned
    outs = [
        jax.ShapeDtypeStruct((2, levels, rows, cols), jnp.float32),
        jax.ShapeDtypeStruct((rows, cols), jnp.float32),
        jax.ShapeDtypeStruct((devices, LANES), jnp.float32),
    ]
    moved = sum(a.size * a.dtype.itemsize for a in operands + outs)
    return pl.pallas_call(
        kernel,
        out_shape=outs,
        in_specs=[pl.BlockSpec(memory_space=pltpu.SMEM)] * 3
        + [pl.BlockSpec(memory_space=pltpu.VMEM)] * (len(operands) - 3),
        out_specs=[pl.BlockSpec(memory_space=pltpu.VMEM)] * 3,
        scratch_shapes=[pltpu.VMEM((records, rows, cols), jnp.float32), plan.tiles],
        compiler_params=pltpu.CompilerParams(vmem_limit_bytes=32 * 2**20),
        cost_estimate=pl.CostEstimate(flops=1, bytes_accessed=1, transcendentals=0),
    )(*operands)


def receive(arrived, records):
    devices = arrived.shape[0]

    def kernel(in_ref, out_ref):
        turned = jnp.transpose(in_ref[...])
        for r in range(CAP):
            out_ref[:, r, :] = turned[r * RANK_ROWS : r * RANK_ROWS + records, :]

    out = call(kernel, jax.ShapeDtypeStruct((records, CAP, devices), jnp.float32), [arrived])
    return jnp.swapaxes(out, 0, 1)


def body(gx_count, gy_count, control, sigma, kappa, beta, sea_mask, x_inverse, y_inverse, ssh_coef,
         obs_owner, tile_index, obs_frac, obs_count):
    _, kinds, levels, rows, cols = control.shape
    devices = gx_count * gy_count
    plan = Plan(levels, rows, cols, gy_count // 2)
    chunks = kinds
    if not plan.fits:
        plan, chunks = Plan(kinds * levels, rows, cols, gy_count // 2), 1
    me = jnp.stack([lax.axis_index("gx"), lax.axis_index("gy")]).astype(jnp.int32)
    x_parts = prepare_x(x_inverse)
    fields = [control[0, 0] if chunks > 1 else control.reshape(plan.fields, rows, cols)]
    if chunks > 1:
        control = after(control, fields[0])
        fields += [control[0, kind] for kind in range(1, kinds)]
    y_columns = y_inverse.reshape(y_inverse.shape[0], gy_count // 2, 2, rows)
    y_columns = jnp.where(me[1] % 2 == 0, y_columns[:, :, 0], y_columns[:, :, 1])
    y_columns = y_columns.reshape(y_inverse.shape[0], -1)
    y_far = gather_far(y_columns, "gx", gx_count)
    y_held = gather_near(y_columns, "gx", gx_count) + y_far
    y_parts = prepare_y([m for m, _ in y_held], [p for _, p in y_held], me, rows)
    side_pairs = [(i, i ^ 1) for i in range(gy_count)]
    result = None
    for step in range(STEPS):
        own, other, sent = [], [], []
        for chunk in range(chunks):
            near = gather_near(fields[chunk], "gx", gx_count)
            total = zonal_start(plan, near, me, *x_parts)
            if sent:
                hold = sent[-1]
            elif step == 0:
                hold = [total, y_far[0][1]] + fields[1:]
            else:
                hold = [total] + returned
            far = gather_far(fields[chunk], "gx", gx_count, hold)
            if own:
                total = after(total, own[-1])
            packed = zonal_end(plan, total, far, me, *x_parts, sea_mask)
            sent.append(exchange(packed, "gy", gy_count))
            lines = sent[chunk]
            if other:
                lines = [after(line, other[-1]) for line in lines]
            for_own, for_other = meridional(plan, me, lines, *y_parts)
            own.append(for_own)
            other.append(lax.ppermute(for_other, "gy", side_pairs))
        for chunk in range(chunks):
            if chunk == 0:
                own[chunk] = after(own[chunk], own[-1])
            elif step < STEPS - 1:
                own[chunk] = after(own[chunk], fields[chunk - 1])
            returned = exchange(add_sides(plan, me, own[chunk], other[chunk]), "gy", gy_count)
            if chunk < chunks - 1:
                returned = [after(block, other[-1]) for block in returned]
            if step < STEPS - 1 or chunk < chunks - 1:
                fields[chunk] = vertical(plan, me, returned, kappa, sea_mask, levels)
            else:
                obs = (
                    obs_owner.reshape(1, -1),
                    tile_index.reshape(1, -1),
                    obs_frac,
                    obs_count,
                    obs_owner,
                )
                result = finish(
                    plan, me, returned, fields[0] if chunks > 1 else None, kappa, sea_mask, sigma,
                    beta, ssh_coef, obs, devices,
                )
    increments, height, outgoing = result
    arrived = lax.all_to_all(outgoing, ("gx", "gy"), split_axis=0, concat_axis=0, tiled=True)
    return increments[None], height[None], receive(arrived, kinds * levels + 1)


def solution(mesh):
    return jax.shard_map(
        functools.partial(body, mesh.shape["gx"], mesh.shape["gy"]),
        mesh=mesh,
        in_specs=(
            P(None, None, None, "gy", "gx"),
            P(None, None, "gy", "gx"),
            P(None, "gy", "gx"),
            P(None, "gy", "gx"),
            P("gy", "gx"),
            P("gx", None),
            P("gx", None),
            P(),
            P(("gx", "gy"), None),
            P(("gx", "gy")),
            P(None, ("gx", "gy")),
            P(("gx", "gy")),
        ),
        out_specs=(
            P(None, None, None, "gy", "gx"),
            P(None, "gy", "gx"),
            P(None, None, ("gx", "gy")),
        ),
        check_vma=False,
    )
```

```python
import functools

import jax
import jax.numpy as jnp
from jax import lax
from jax.experimental import pallas as pl
from jax.experimental.pallas import tpu as pltpu
from jax.sharding import PartitionSpec as P

STEPS = 2
CAP = 2
LANES = 128
SUB = 8
RANK_ROWS = 16
NN = (((1,), (0,)), ((), ()))
NT = (((1,), (1,)), ((), ()))


class Plan:
    def __init__(self, fields, rows, cols, parts):
        self.fields, self.rows, self.cols, self.parts = fields, rows, cols, parts
        self.blocks = cols // LANES
        tiles = fields * self.blocks
        share = fields * cols // parts
        self.full = share // LANES
        self.rest = share % LANES
        self.sides = LANES // self.rest if self.rest else 0
        self.groups = rows // SUB
        self.packs = -(-self.groups // self.sides) if self.rest else 0
        self.width = self.full * rows + self.packs * SUB
        self.columns = (self.full + (1 if self.rest else 0)) * LANES
        self.fits = (
            cols % LANES == 0
            and rows % SUB == 0
            and fields * cols % parts == 0
            and (self.rest == 0 or LANES % self.rest == 0)
            and tiles - self.full * parts == (parts // self.sides if self.rest else 0)
        )

    def moved(self, side, place):
        return ((side - place) * self.rest) % LANES

    def pack_rest(self, tile, place):
        lane_side = lax.broadcasted_iota(jnp.int32, (SUB, LANES), 1) // self.rest
        out = []
        for pack in range(self.packs):
            joined = None
            for side in range(self.sides):
                group = pack * self.sides + side
                if group >= self.groups:
                    break
                piece = turn(tile[group * SUB : (group + 1) * SUB, :], self.moved(side, place))
                joined = piece if joined is None else jnp.where(lane_side == side, piece, joined)
            out.append(joined)
        return out

    def unpack_rest(self, ref, place):
        pieces = []
        for group in range(self.groups):
            pack, side = divmod(group, self.sides)
            start = self.full * self.rows + pack * SUB
            pieces.append(turn(ref[start : start + SUB, :], self.moved(place, side)))
        return jnp.concatenate(pieces, axis=0)

    def store_rest(self, ref, packs):
        for pack, value in enumerate(packs):
            start = self.full * self.rows + pack * SUB
            ref[start : start + SUB, :] = value

    def send_tiles(self, tiles_ref, device, out_ref):
        for i in range(self.full):
            out_ref[i * self.rows : (i + 1) * self.rows, :] = tiles_ref[device * self.full + i]
        if self.rest:
            tile = tiles_ref[self.parts * self.full + device // self.sides]
            self.store_rest(out_ref, self.pack_rest(tile, device % self.sides))

    def take_tiles(self, in_ref, device, tiles_ref):
        for i in range(self.full):
            tiles_ref[device * self.full + i] = in_ref[i * self.rows : (i + 1) * self.rows, :]
        if self.rest:
            place = device % self.sides
            index = self.parts * self.full + device // self.sides
            lane_side = lax.broadcasted_iota(jnp.int32, (self.rows, LANES), 1) // self.rest
            tiles_ref[index] = jnp.where(
                lane_side == place, self.unpack_rest(in_ref, place), tiles_ref[index]
            )

    @property
    def tiles(self):
        return pltpu.VMEM((self.fields * self.blocks, self.rows, LANES), jnp.float32)

    @property
    def blocks_out(self):
        shape = jax.ShapeDtypeStruct((self.width, LANES), jnp.float32)
        return [shape] * self.parts


def part_of(me_ref, mask):
    return (me_ref[1] // 2) ^ mask


def turn(value, shift):
    if isinstance(shift, int) and shift == 0:
        return value
    return pltpu.roll(value, shift, axis=1)


def split(value):
    high = value.astype(jnp.bfloat16)
    low = (value - high.astype(jnp.float32)).astype(jnp.bfloat16)
    return high, low


def dot(a, b, dims=NN):
    return lax.dot_general(a, b, dims, preferred_element_type=jnp.float32)


def dot_split(a, b):
    return dot(a[0], b[0]) + (dot(a[0], b[1]) + dot(a[1], b[0]))


def call(kernel, out_shape, operands, scalars=(), flops=0, scratch=()):
    outs = out_shape if isinstance(out_shape, (list, tuple)) else [out_shape]
    moved = sum(a.size * a.dtype.itemsize for a in list(operands) + list(outs))
    specs = [
        pl.BlockSpec(memory_space=pltpu.SMEM if i in scalars else pltpu.VMEM)
        for i in range(len(operands))
    ]
    out_spec = pl.BlockSpec(memory_space=pltpu.VMEM)
    many = isinstance(out_shape, (list, tuple))
    return pl.pallas_call(
        kernel,
        out_shape=out_shape,
        in_specs=specs,
        out_specs=[out_spec] * len(outs) if many else out_spec,
        scratch_shapes=list(scratch),
        compiler_params=pltpu.CompilerParams(vmem_limit_bytes=min(48, 6 + 3 * moved // 2**20) * 2**20),
        cost_estimate=pl.CostEstimate(flops=1, bytes_accessed=1, transcendentals=0),
    )(*operands)


def after(value, *others):
    return lax.optimization_barrier((value,) + others)[0]


def gather_near(block, axis, count):
    pairs = [(i, i ^ 1) for i in range(count)]
    return [(0, block), (1, lax.ppermute(block, axis, pairs))]


def gather_far(block, axis, count, hold=()):
    held = [(0, block)]
    bit = count // 2
    while bit:
        pairs = [(i, i ^ bit) for i in range(count)]
        sources = held if bit > 1 else held[1:]
        brought = [(mask ^ bit, lax.ppermute(piece, axis, pairs)) for mask, piece in sources]
        if hold and bit == count // 2 and bit > 1:
            brought = [(mask, after(piece, *hold)) for mask, piece in brought]
        held = held + brought
        bit //= 2
    return held[1:]


def exchange(blocks, axis, count):
    out = [blocks[0]] + [None] * (len(blocks) - 1)
    for mask in range(1, len(blocks)):
        pairs = [(i, i ^ (2 * mask)) for i in range(count)]
        out[mask] = lax.ppermute(blocks[mask], axis, pairs)
    return out


def prepare_x(x_inverse):
    rows, cols = x_inverse.shape

    def kernel(x_ref, high_ref, low_ref):
        for start in range(0, cols, rows):
            high, low = split(jnp.transpose(x_ref[:, start : start + rows]))
            high_ref[start : start + rows, :] = high
            low_ref[start : start + rows, :] = low

    shape = jax.ShapeDtypeStruct((cols, rows), jnp.bfloat16)
    return call(kernel, [shape, shape], [x_inverse])


def prepare_y(masks, pieces, me, rows):
    owned, half = pieces[0].shape

    def kernel(me_ref, *refs):
        high_ref, low_ref, whole_ref = refs[-3:]
        side = lax.rem(me_ref[1], 2)
        for mask, ref in zip(masks, refs):
            start = pl.multiple_of((me_ref[0] ^ mask) * owned, owned)
            whole_ref[pl.ds(start, owned), :] = ref[...]
        for other in range(2):
            for part in range(half // rows):
                start = pl.multiple_of((2 * part + (side ^ other)) * rows, rows)
                high, low = split(whole_ref[pl.ds(start, rows), :])
                out = other * half + part * rows
                high_ref[out : out + rows, :] = high
                low_ref[out : out + rows, :] = low

    shape = jax.ShapeDtypeStruct((2 * half, half), jnp.bfloat16)
    return call(
        kernel,
        [shape, shape],
        [me] + pieces,
        scalars=(0,),
        scratch=[pltpu.VMEM((2 * half, half), jnp.float32)],
    )


def add_zonal(total, masks, me_ref, high_ref, low_ref, refs):
    for mask, ref in zip(masks, refs):
        fields, rows, cols = ref.shape
        start = pl.multiple_of((me_ref[0] ^ mask) * cols, cols)
        values = split(ref[...].reshape(fields * rows, cols))
        weights = (high_ref[pl.ds(start, cols), :], low_ref[pl.ds(start, cols), :])
        part = dot_split(values, weights)
        total = part if total is None else total + part
    return total


def zonal_start(plan, held, me, x_high, x_low):
    masks, pieces = [m for m, _ in held], [p for _, p in held]

    def kernel(me_ref, high_ref, low_ref, *refs):
        refs[-1][...] = add_zonal(None, masks, me_ref, high_ref, low_ref, refs)

    return call(
        kernel,
        jax.ShapeDtypeStruct((plan.fields * plan.rows, plan.cols), jnp.float32),
        [me, x_high, x_low] + pieces,
        scalars=(0,),
        flops=6 * plan.fields * plan.rows * plan.cols**2 * len(pieces),
    )


def zonal_end(plan, total, held, me, x_high, x_low, sea_mask):
    fields, rows, cols, parts = plan.fields, plan.rows, plan.cols, plan.parts
    masks, pieces = [m for m, _ in held], [p for _, p in held]

    def kernel(me_ref, high_ref, low_ref, sea_ref, total_ref, *refs):
        out_refs, tiles_ref = refs[-parts - 1 : -1], refs[-1]
        result = add_zonal(total_ref[...], masks, me_ref, high_ref, low_ref, refs)
        result = result.reshape(fields, rows, cols)
        sea = sea_ref[...].astype(jnp.float32)
        for block in range(plan.blocks):
            lanes = slice(block * LANES, (block + 1) * LANES)
            for field in range(fields):
                tiles_ref[field * plan.blocks + block] = sea[:, lanes] * result[field, :, lanes]
        for mask in range(parts):
            plan.send_tiles(tiles_ref, part_of(me_ref, mask), out_refs[mask])

    return call(
        kernel,
        plan.blocks_out,
        [me, x_high, x_low, sea_mask, total] + pieces,
        scalars=(0,),
        flops=6 * fields * rows * cols**2 * len(pieces),
        scratch=[plan.tiles],
    )


def meridional(plan, me, lines, y_high, y_low):
    rows, parts = plan.rows, plan.parts

    def kernel(me_ref, high_ref, low_ref, *refs):
        in_refs, out_refs, lines_ref, solved_ref = refs[:parts], refs[parts:-2], refs[-2], refs[-1]
        for mask in range(parts):
            place = pl.ds(pl.multiple_of(part_of(me_ref, mask) * rows, rows), rows)
            for i in range(plan.full):
                lanes = slice(i * LANES, (i + 1) * LANES)
                lines_ref[place, lanes] = in_refs[mask][i * rows : (i + 1) * rows, :]
            if plan.rest:
                lines_ref[place, plan.full * LANES :] = plan.unpack_rest(in_refs[mask], 0)
        solved_ref[...] = dot_split((high_ref[...], low_ref[...]), split(lines_ref[...]))
        for other in range(2):
            for part in range(parts):
                start = (other * parts + part) * rows
                for i in range(plan.full):
                    lanes = slice(i * LANES, (i + 1) * LANES)
                    out_refs[other][part, i * rows : (i + 1) * rows, :] = solved_ref[
                        start : start + rows, lanes
                    ]
                if plan.rest:
                    last = solved_ref[start : start + rows, plan.full * LANES :]
                    plan.store_rest(out_refs[other].at[part], plan.pack_rest(last, 0))

    shape = jax.ShapeDtypeStruct((parts, plan.width, LANES), jnp.float32)
    return call(
        kernel,
        [shape, shape],
        [me, y_high, y_low] + lines,
        scalars=(0,),
        flops=12 * (parts * rows) ** 2 * plan.columns,
        scratch=[
            pltpu.VMEM((parts * rows, plan.columns), jnp.float32),
            pltpu.VMEM((2 * parts * rows, plan.columns), jnp.float32),
        ],
    )


def add_sides(plan, me, own, other):
    def kernel(me_ref, own_ref, other_ref, *out_refs):
        for mask in range(plan.parts):
            part = part_of(me_ref, mask)
            out_refs[mask][...] = own_ref[part] + other_ref[part]

    return call(kernel, plan.blocks_out, [me, own, other], scalars=(0,))


def solve_columns(plan, me_ref, in_refs, tiles_ref, kappa_ref, sea_ref, levels, store):
    kinds = plan.fields // levels
    for mask in range(plan.parts):
        plan.take_tiles(in_refs[mask], part_of(me_ref, mask), tiles_ref)
    for block in range(plan.blocks):
        lanes = slice(block * LANES, (block + 1) * LANES)
        sea = sea_ref[:, lanes].astype(jnp.float32)
        inverse, upper = [], []
        kappa = [kappa_ref[level, :, lanes] for level in range(levels - 1)]
        for level in range(levels):
            below = kappa[level - 1] if level > 0 else 0.0
            above = kappa[level] if level < levels - 1 else 0.0
            pivot = 1.0 + below + above
            if level > 0:
                pivot = pivot + below * upper[-1]
            inverse.append(1.0 / pivot)
            upper.append(-above * inverse[-1])
        for kind in range(kinds):
            forward = []
            for level in range(levels):
                tile = tiles_ref[(kind * levels + level) * plan.blocks + block]
                right = sea * tile
                if level > 0:
                    right = right + kappa[level - 1] * forward[-1]
                forward.append(right * inverse[level])
            value = forward[-1]
            store(kind, levels - 1, lanes, value)
            for level in range(levels - 2, -1, -1):
                value = forward[level] - upper[level] * value
                store(kind, level, lanes, value)


def vertical(plan, me, returned, kappa, sea_mask, levels):
    def kernel(me_ref, kappa_ref, sea_ref, *refs):
        in_refs, (out_ref, tiles_ref) = refs[: plan.parts], refs[plan.parts :]

        def store(kind, level, lanes, value):
            out_ref[kind * levels + level, :, lanes] = value

        solve_columns(plan, me_ref, in_refs, tiles_ref, kappa_ref, sea_ref, levels, store)

    return call(
        kernel,
        jax.ShapeDtypeStruct((plan.fields, plan.rows, plan.cols), jnp.float32),
        [me, kappa, sea_mask] + returned,
        scalars=(0,),
        scratch=[plan.tiles],
    )


def finish(plan, me, returned, temper_field, kappa, sea_mask, sigma, beta, ssh_coef, obs, devices):
    levels = sigma.shape[1]
    rows, cols = plan.rows, plan.cols
    records = 2 * levels + 1
    owner_row, tile_index, obs_frac, obs_count, owner_col = obs
    slots = owner_row.shape[1]
    extra = [] if temper_field is None else [temper_field]

    def kernel(me_ref, ssh_ref, count_ref, kappa_ref, sea_ref, sigma_ref, beta_ref,
               owner_ref, tile_ref, frac_ref, column_ref, *refs):
        inc_ref, height_ref, send_ref, profile_ref, tiles_ref = refs[-5:]

        def store(kind, level, lanes, value):
            profile_ref[(kind + len(extra)) * levels + level, :, lanes] = value

        solve_columns(
            plan, me_ref, refs[len(extra) :], tiles_ref, kappa_ref, sea_ref, levels, store
        )
        for block in range(plan.blocks):
            lanes = slice(block * LANES, (block + 1) * LANES)
            height = None
            for level in range(levels):
                source = refs[0] if extra else profile_ref
                temper = sigma_ref[0, level, :, lanes] * source[level, :, lanes]
                saline = (
                    sigma_ref[1, level, :, lanes] * profile_ref[levels + level, :, lanes]
                    + beta_ref[level, :, lanes] * temper
                )
                term = ssh_ref[0, level] * temper + ssh_ref[1, level] * saline
                height = term if height is None else height + term
                profile_ref[level, :, lanes] = temper
                profile_ref[levels + level, :, lanes] = saline
                inc_ref[0, level, :, lanes] = temper
                inc_ref[1, level, :, lanes] = saline
            profile_ref[2 * levels, :, lanes] = height
            height_ref[:, lanes] = height

        cell = tile_ref[...]
        row, col = cell // cols, cell % cols
        frac_x, frac_y = frac_ref[0:1, :], frac_ref[1:2, :]
        along = lax.broadcasted_iota(jnp.int32, (cols, slots), 0)
        weight_x = jnp.where(along == col, 1.0 - frac_x, jnp.where(along == col + 1, frac_x, 0.0))
        across = lax.broadcasted_iota(jnp.int32, (rows, slots), 0)
        weight_y = jnp.where(across == row, 1.0 - frac_y, jnp.where(across == row + 1, frac_y, 0.0))
        partial = lax.dot_general(
            profile_ref[...].reshape(records * rows, cols),
            weight_x,
            NN,
            precision=lax.Precision.HIGHEST,
            preferred_element_type=jnp.float32,
        ).reshape(records, rows, slots)
        interp = jnp.sum(partial * weight_y[None], axis=1)
        slot = lax.broadcasted_iota(jnp.int32, (1, slots), 1)
        interp = interp * (slot < count_ref[0]).astype(jnp.float32)
        earlier = lax.broadcasted_iota(jnp.int32, (slots, slots), 0) < lax.broadcasted_iota(
            jnp.int32, (slots, slots), 1
        )
        owner = owner_ref[...]
        same = jnp.where((column_ref[...] == owner) & earlier, 1.0, 0.0)
        rank = jnp.sum(same, axis=0, keepdims=True).astype(jnp.int32)
        padded = jnp.concatenate(
            [interp, jnp.zeros((RANK_ROWS - records, slots), jnp.float32)], axis=0
        )
        ranked = jnp.concatenate(
            [jnp.where(rank == r, padded, 0.0) for r in range(CAP)], axis=0
        )
        ranked = jnp.concatenate(
            [ranked, jnp.zeros((LANES - CAP * RANK_ROWS, slots), jnp.float32)], axis=0
        )
        to_owner = (owner == lax.broadcasted_iota(jnp.int32, (devices, slots), 0)).astype(
            jnp.float32
        )
        send_ref[...] = lax.dot_general(
            to_owner, ranked, NT, precision=lax.Precision.HIGHEST, preferred_element_type=jnp.float32
        )

    operands = [me, ssh_coef, obs_count, kappa, sea_mask, sigma, beta,
                owner_row, tile_index, obs_frac, owner_col] + extra + returned
    outs = [
        jax.ShapeDtypeStruct((2, levels, rows, cols), jnp.float32),
        jax.ShapeDtypeStruct((rows, cols), jnp.float32),
        jax.ShapeDtypeStruct((devices, LANES), jnp.float32),
    ]
    moved = sum(a.size * a.dtype.itemsize for a in operands + outs)
    return pl.pallas_call(
        kernel,
        out_shape=outs,
        in_specs=[pl.BlockSpec(memory_space=pltpu.SMEM)] * 3
        + [pl.BlockSpec(memory_space=pltpu.VMEM)] * (len(operands) - 3),
        out_specs=[pl.BlockSpec(memory_space=pltpu.VMEM)] * 3,
        scratch_shapes=[pltpu.VMEM((records, rows, cols), jnp.float32), plan.tiles],
        compiler_params=pltpu.CompilerParams(vmem_limit_bytes=32 * 2**20),
        cost_estimate=pl.CostEstimate(flops=1, bytes_accessed=1, transcendentals=0),
    )(*operands)


def receive(arrived, records):
    devices = arrived.shape[0]

    def kernel(in_ref, out_ref):
        turned = jnp.transpose(in_ref[...])
        for r in range(CAP):
            out_ref[:, r, :] = turned[r * RANK_ROWS : r * RANK_ROWS + records, :]

    out = call(kernel, jax.ShapeDtypeStruct((records, CAP, devices), jnp.float32), [arrived])
    return jnp.swapaxes(out, 0, 1)


def body(gx_count, gy_count, control, sigma, kappa, beta, sea_mask, x_inverse, y_inverse, ssh_coef,
         obs_owner, tile_index, obs_frac, obs_count):
    _, kinds, levels, rows, cols = control.shape
    devices = gx_count * gy_count
    plan = Plan(levels, rows, cols, gy_count // 2)
    chunks = kinds
    if not plan.fits:
        plan, chunks = Plan(kinds * levels, rows, cols, gy_count // 2), 1
    me = jnp.stack([lax.axis_index("gx"), lax.axis_index("gy")]).astype(jnp.int32)
    x_parts = prepare_x(x_inverse)
    fields = [control[0, 0] if chunks > 1 else control.reshape(plan.fields, rows, cols)]
    if chunks > 1:
        control = after(control, fields[0])
        fields += [control[0, kind] for kind in range(1, kinds)]
    y_columns = y_inverse.reshape(y_inverse.shape[0], gy_count // 2, 2, rows)
    y_columns = jnp.where(me[1] % 2 == 0, y_columns[:, :, 0], y_columns[:, :, 1])
    y_columns = y_columns.reshape(y_inverse.shape[0], -1)
    y_far = gather_far(y_columns, "gx", gx_count)
    y_held = gather_near(y_columns, "gx", gx_count) + y_far
    y_parts = prepare_y([m for m, _ in y_held], [p for _, p in y_held], me, rows)
    side_pairs = [(i, i ^ 1) for i in range(gy_count)]
    result = None
    for step in range(STEPS):
        own, other, sent = [], [], []
        for chunk in range(chunks):
            near = gather_near(fields[chunk], "gx", gx_count)
            total = zonal_start(plan, near, me, *x_parts)
            if sent:
                hold = [total, y_parts[0]] + lines
            elif step == 0:
                hold = [total, y_far[0][1]] + fields[1:]
            else:
                hold = [total] + returned[::-1]
            far = gather_far(fields[chunk], "gx", gx_count, hold)
            if own:
                total = after(total, own[-1])
            packed = zonal_end(plan, total, far, me, *x_parts, sea_mask)
            sent.append(exchange(packed, "gy", gy_count))
            ready = other[-1] if other else y_parts[0]
            lines = [after(line, ready) for line in sent[chunk]]
            for_own, for_other = meridional(plan, me, lines, *y_parts)
            own.append(for_own)
            other.append(lax.ppermute(for_other, "gy", side_pairs))
        for chunk in range(chunks):
            if chunk == 0:
                own[chunk] = after(own[chunk], own[-1])
            elif step < STEPS - 1:
                own[chunk] = after(own[chunk], fields[chunk - 1])
            returned = exchange(add_sides(plan, me, own[chunk], other[chunk]), "gy", gy_count)
            if chunk < chunks - 1:
                returned = [after(block, other[-1]) for block in returned]
            if step < STEPS - 1 or chunk < chunks - 1:
                fields[chunk] = vertical(plan, me, returned, kappa, sea_mask, levels)
            else:
                returned = [after(block, *fields[:chunk]) for block in returned]
                obs = (
                    obs_owner.reshape(1, -1),
                    tile_index.reshape(1, -1),
                    obs_frac,
                    obs_count,
                    obs_owner,
                )
                result = finish(
                    plan, me, returned, fields[0] if chunks > 1 else None, kappa, sea_mask, sigma,
                    beta, ssh_coef, obs, devices,
                )
    increments, height, outgoing = result
    arrived = lax.all_to_all(outgoing, ("gx", "gy"), split_axis=0, concat_axis=0, tiled=True)
    return increments[None], height[None], receive(arrived, kinds * levels + 1)


def solution(mesh):
    return jax.shard_map(
        functools.partial(body, mesh.shape["gx"], mesh.shape["gy"]),
        mesh=mesh,
        in_specs=(
            P(None, None, None, "gy", "gx"),
            P(None, None, "gy", "gx"),
            P(None, "gy", "gx"),
            P(None, "gy", "gx"),
            P("gy", "gx"),
            P("gx", None),
            P("gx", None),
            P(),
            P(("gx", "gy"), None),
            P(("gx", "gy")),
            P(None, ("gx", "gy")),
            P(("gx", "gy")),
        ),
        out_specs=(
            P(None, None, None, "gy", "gx"),
            P(None, "gy", "gx"),
            P(None, None, ("gx", "gy")),
        ),
        check_vma=False,
    )
```

```python
import functools

import jax
import jax.numpy as jnp
from jax import lax
from jax.experimental import pallas as pl
from jax.experimental.pallas import tpu as pltpu
from jax.sharding import PartitionSpec as P

STEPS = 2
CAP = 2
LANES = 128
SUB = 8
RANK_ROWS = 16
NN = (((1,), (0,)), ((), ()))
NT = (((1,), (1,)), ((), ()))


class Plan:
    def __init__(self, fields, rows, cols, parts):
        self.fields, self.rows, self.cols, self.parts = fields, rows, cols, parts
        self.blocks = cols // LANES
        tiles = fields * self.blocks
        share = fields * cols // parts
        self.full = share // LANES
        self.rest = share % LANES
        self.sides = LANES // self.rest if self.rest else 0
        self.groups = rows // SUB
        self.packs = -(-self.groups // self.sides) if self.rest else 0
        self.width = self.full * rows + self.packs * SUB
        self.columns = (self.full + (1 if self.rest else 0)) * LANES
        self.fits = (
            cols % LANES == 0
            and rows % SUB == 0
            and fields * cols % parts == 0
            and (self.rest == 0 or LANES % self.rest == 0)
            and tiles - self.full * parts == (parts // self.sides if self.rest else 0)
        )

    def moved(self, side, place):
        return ((side - place) * self.rest) % LANES

    def pack_rest(self, tile, place):
        lane_side = lax.broadcasted_iota(jnp.int32, (SUB, LANES), 1) // self.rest
        out = []
        for pack in range(self.packs):
            joined = None
            for side in range(self.sides):
                group = pack * self.sides + side
                if group >= self.groups:
                    break
                piece = turn(tile[group * SUB : (group + 1) * SUB, :], self.moved(side, place))
                joined = piece if joined is None else jnp.where(lane_side == side, piece, joined)
            out.append(joined)
        return out

    def unpack_rest(self, ref, place, base=0):
        pieces = []
        for group in range(self.groups):
            pack, side = divmod(group, self.sides)
            start = base + self.full * self.rows + pack * SUB
            pieces.append(turn(ref[start : start + SUB, :], self.moved(place, side)))
        return jnp.concatenate(pieces, axis=0)

    def store_rest(self, ref, packs, base=0):
        for pack, value in enumerate(packs):
            start = base + self.full * self.rows + pack * SUB
            ref[start : start + SUB, :] = value

    def send_tiles(self, tiles_ref, device, out_ref):
        for i in range(self.full):
            out_ref[i * self.rows : (i + 1) * self.rows, :] = tiles_ref[device * self.full + i]
        if self.rest:
            tile = tiles_ref[self.parts * self.full + device // self.sides]
            self.store_rest(out_ref, self.pack_rest(tile, device % self.sides))

    def take_tiles(self, in_ref, device, tiles_ref, base, tile_base):
        for i in range(self.full):
            start = base + i * self.rows
            tiles_ref[tile_base + device * self.full + i] = in_ref[start : start + self.rows, :]
        if self.rest:
            place = device % self.sides
            index = tile_base + self.parts * self.full + device // self.sides
            lane_side = lax.broadcasted_iota(jnp.int32, (self.rows, LANES), 1) // self.rest
            tiles_ref[index] = jnp.where(
                lane_side == place, self.unpack_rest(in_ref, place, base), tiles_ref[index]
            )

    @property
    def tiles(self):
        return pltpu.VMEM((self.fields * self.blocks, self.rows, LANES), jnp.float32)

    @property
    def blocks_out(self):
        shape = jax.ShapeDtypeStruct((self.width, LANES), jnp.float32)
        return [shape] * self.parts


class Stack:
    def __init__(self, plans):
        self.rows, self.cols, self.parts = plans[0].rows, plans[0].cols, plans[0].parts
        self.blocks = plans[0].blocks
        self.members = []
        self.fields = self.width = self.columns = 0
        for plan in plans:
            self.members.append((plan, self.width, self.fields * self.blocks, self.columns))
            self.fields += plan.fields
            self.width += plan.width
            self.columns += plan.columns

    def take_tiles(self, in_ref, device, tiles_ref):
        for plan, base, tile_base, _ in self.members:
            plan.take_tiles(in_ref, device, tiles_ref, base, tile_base)

    tiles = Plan.tiles
    blocks_out = Plan.blocks_out


def part_of(me_ref, mask):
    return (me_ref[1] // 2) ^ mask


def turn(value, shift):
    if isinstance(shift, int) and shift == 0:
        return value
    return pltpu.roll(value, shift, axis=1)


def split(value):
    high = value.astype(jnp.bfloat16)
    low = (value - high.astype(jnp.float32)).astype(jnp.bfloat16)
    return high, low


def dot(a, b, dims=NN):
    return lax.dot_general(a, b, dims, preferred_element_type=jnp.float32)


def dot_split(a, b):
    return dot(a[0], b[0]) + (dot(a[0], b[1]) + dot(a[1], b[0]))


def call(kernel, out_shape, operands, scalars=(), flops=0, scratch=()):
    outs = out_shape if isinstance(out_shape, (list, tuple)) else [out_shape]
    moved = sum(a.size * a.dtype.itemsize for a in list(operands) + list(outs))
    specs = [
        pl.BlockSpec(memory_space=pltpu.SMEM if i in scalars else pltpu.VMEM)
        for i in range(len(operands))
    ]
    out_spec = pl.BlockSpec(memory_space=pltpu.VMEM)
    many = isinstance(out_shape, (list, tuple))
    return pl.pallas_call(
        kernel,
        out_shape=out_shape,
        in_specs=specs,
        out_specs=[out_spec] * len(outs) if many else out_spec,
        scratch_shapes=list(scratch),
        compiler_params=pltpu.CompilerParams(vmem_limit_bytes=min(48, 6 + 3 * moved // 2**20) * 2**20),
        cost_estimate=pl.CostEstimate(flops=1, bytes_accessed=1, transcendentals=0),
    )(*operands)


def after(value, *others):
    return lax.optimization_barrier((value,) + others)[0]


def gather_near(block, axis, count):
    pairs = [(i, i ^ 1) for i in range(count)]
    return [(0, block), (1, lax.ppermute(block, axis, pairs))]


def gather_far(block, axis, count, hold=()):
    held = [(0, block)]
    bit = count // 2
    while bit:
        pairs = [(i, i ^ bit) for i in range(count)]
        sources = held if bit > 1 else held[1:]
        brought = [(mask ^ bit, lax.ppermute(piece, axis, pairs)) for mask, piece in sources]
        if hold and bit == count // 2 and bit > 1:
            brought = [(mask, after(piece, *hold)) for mask, piece in brought]
        held = held + brought
        bit //= 2
    return held[1:]


def exchange(blocks, axis, count):
    out = [blocks[0]] + [None] * (len(blocks) - 1)
    for mask in range(1, len(blocks)):
        pairs = [(i, i ^ (2 * mask)) for i in range(count)]
        out[mask] = lax.ppermute(blocks[mask], axis, pairs)
    return out


def prepare_x(x_inverse):
    rows, cols = x_inverse.shape

    def kernel(x_ref, high_ref, low_ref):
        for start in range(0, cols, rows):
            high, low = split(jnp.transpose(x_ref[:, start : start + rows]))
            high_ref[start : start + rows, :] = high
            low_ref[start : start + rows, :] = low

    shape = jax.ShapeDtypeStruct((cols, rows), jnp.bfloat16)
    return call(kernel, [shape, shape], [x_inverse])


def prepare_y(masks, pieces, me, rows):
    owned, half = pieces[0].shape

    def kernel(me_ref, *refs):
        high_ref, low_ref, whole_ref = refs[-3:]
        side = lax.rem(me_ref[1], 2)
        for mask, ref in zip(masks, refs):
            start = pl.multiple_of((me_ref[0] ^ mask) * owned, owned)
            whole_ref[pl.ds(start, owned), :] = ref[...]
        for other in range(2):
            for part in range(half // rows):
                start = pl.multiple_of((2 * part + (side ^ other)) * rows, rows)
                high, low = split(whole_ref[pl.ds(start, rows), :])
                out = other * half + part * rows
                high_ref[out : out + rows, :] = high
                low_ref[out : out + rows, :] = low

    shape = jax.ShapeDtypeStruct((2 * half, half), jnp.bfloat16)
    return call(
        kernel,
        [shape, shape],
        [me] + pieces,
        scalars=(0,),
        scratch=[pltpu.VMEM((2 * half, half), jnp.float32)],
    )


def add_zonal(total, masks, me_ref, high_ref, low_ref, refs):
    for mask, ref in zip(masks, refs):
        fields, rows, cols = ref.shape
        start = pl.multiple_of((me_ref[0] ^ mask) * cols, cols)
        values = split(ref[...].reshape(fields * rows, cols))
        weights = (high_ref[pl.ds(start, cols), :], low_ref[pl.ds(start, cols), :])
        part = dot_split(values, weights)
        total = part if total is None else total + part
    return total


def zonal_start(plan, held, me, x_high, x_low):
    masks, pieces = [m for m, _ in held], [p for _, p in held]

    def kernel(me_ref, high_ref, low_ref, *refs):
        refs[-1][...] = add_zonal(None, masks, me_ref, high_ref, low_ref, refs)

    return call(
        kernel,
        jax.ShapeDtypeStruct((plan.fields * plan.rows, plan.cols), jnp.float32),
        [me, x_high, x_low] + pieces,
        scalars=(0,),
        flops=6 * plan.fields * plan.rows * plan.cols**2 * len(pieces),
    )


def zonal_end(plan, total, held, me, x_high, x_low, sea_mask):
    fields, rows, cols, parts = plan.fields, plan.rows, plan.cols, plan.parts
    masks, pieces = [m for m, _ in held], [p for _, p in held]

    def kernel(me_ref, high_ref, low_ref, sea_ref, total_ref, *refs):
        out_refs, tiles_ref = refs[-parts - 1 : -1], refs[-1]
        result = add_zonal(total_ref[...], masks, me_ref, high_ref, low_ref, refs)
        result = result.reshape(fields, rows, cols)
        sea = sea_ref[...].astype(jnp.float32)
        for block in range(plan.blocks):
            lanes = slice(block * LANES, (block + 1) * LANES)
            for field in range(fields):
                tiles_ref[field * plan.blocks + block] = sea[:, lanes] * result[field, :, lanes]
        for mask in range(parts):
            plan.send_tiles(tiles_ref, part_of(me_ref, mask), out_refs[mask])

    return call(
        kernel,
        plan.blocks_out,
        [me, x_high, x_low, sea_mask, total] + pieces,
        scalars=(0,),
        flops=6 * fields * rows * cols**2 * len(pieces),
        scratch=[plan.tiles],
    )


def meridional(stack, me, lines, y_high, y_low):
    rows, parts = stack.rows, stack.parts

    def kernel(me_ref, high_ref, low_ref, *refs):
        in_refs, out_refs = refs[: len(lines)], refs[len(lines) : -2]
        lines_ref, solved_ref = refs[-2:]
        for number, (plan, _, _, first) in enumerate(stack.members):
            for mask in range(parts):
                ref = in_refs[number * parts + mask]
                place = pl.ds(pl.multiple_of(part_of(me_ref, mask) * rows, rows), rows)
                for i in range(plan.full):
                    lanes = slice(first + i * LANES, first + (i + 1) * LANES)
                    lines_ref[place, lanes] = ref[i * rows : (i + 1) * rows, :]
                if plan.rest:
                    lanes = slice(first + plan.full * LANES, first + plan.columns)
                    lines_ref[place, lanes] = plan.unpack_rest(ref, 0)
        solved_ref[...] = dot_split((high_ref[...], low_ref[...]), split(lines_ref[...]))
        for plan, base, _, first in stack.members:
            for other in range(2):
                for part in range(parts):
                    start = (other * parts + part) * rows
                    for i in range(plan.full):
                        out = base + i * rows
                        out_refs[other][part, out : out + rows, :] = solved_ref[
                            start : start + rows, first + i * LANES : first + (i + 1) * LANES
                        ]
                    if plan.rest:
                        last = solved_ref[
                            start : start + rows, first + plan.full * LANES : first + plan.columns
                        ]
                        packs = plan.pack_rest(last, 0)
                        plan.store_rest(out_refs[other].at[part], packs, base)

    shape = jax.ShapeDtypeStruct((parts, stack.width, LANES), jnp.float32)
    return call(
        kernel,
        [shape, shape],
        [me, y_high, y_low] + lines,
        scalars=(0,),
        flops=12 * (parts * rows) ** 2 * stack.columns,
        scratch=[
            pltpu.VMEM((parts * rows, stack.columns), jnp.float32),
            pltpu.VMEM((2 * parts * rows, stack.columns), jnp.float32),
        ],
    )


def add_sides(plan, me, own, other):
    def kernel(me_ref, own_ref, other_ref, *out_refs):
        for mask in range(plan.parts):
            part = part_of(me_ref, mask)
            out_refs[mask][...] = own_ref[part] + other_ref[part]

    return call(kernel, plan.blocks_out, [me, own, other], scalars=(0,))


def solve_columns(plan, me_ref, in_refs, tiles_ref, kappa_ref, sea_ref, levels, store):
    kinds = plan.fields // levels
    for mask in range(plan.parts):
        plan.take_tiles(in_refs[mask], part_of(me_ref, mask), tiles_ref)
    for block in range(plan.blocks):
        lanes = slice(block * LANES, (block + 1) * LANES)
        sea = sea_ref[:, lanes].astype(jnp.float32)
        inverse, upper = [], []
        kappa = [kappa_ref[level, :, lanes] for level in range(levels - 1)]
        for level in range(levels):
            below = kappa[level - 1] if level > 0 else 0.0
            above = kappa[level] if level < levels - 1 else 0.0
            pivot = 1.0 + below + above
            if level > 0:
                pivot = pivot + below * upper[-1]
            inverse.append(1.0 / pivot)
            upper.append(-above * inverse[-1])
        for kind in range(kinds):
            forward = []
            for level in range(levels):
                tile = tiles_ref[(kind * levels + level) * plan.blocks + block]
                right = sea * tile
                if level > 0:
                    right = right + kappa[level - 1] * forward[-1]
                forward.append(right * inverse[level])
            value = forward[-1]
            store(kind, levels - 1, lanes, value)
            for level in range(levels - 2, -1, -1):
                value = forward[level] - upper[level] * value
                store(kind, level, lanes, value)


def vertical(plan, me, returned, kappa, sea_mask, levels):
    def kernel(me_ref, kappa_ref, sea_ref, *refs):
        in_refs, (out_ref, tiles_ref) = refs[: plan.parts], refs[plan.parts :]

        def store(kind, level, lanes, value):
            out_ref[kind * levels + level, :, lanes] = value

        solve_columns(plan, me_ref, in_refs, tiles_ref, kappa_ref, sea_ref, levels, store)

    return call(
        kernel,
        jax.ShapeDtypeStruct((plan.fields, plan.rows, plan.cols), jnp.float32),
        [me, kappa, sea_mask] + returned,
        scalars=(0,),
        scratch=[plan.tiles],
    )


def finish(plan, me, returned, temper_field, kappa, sea_mask, sigma, beta, ssh_coef, obs, devices):
    levels = sigma.shape[1]
    rows, cols = plan.rows, plan.cols
    records = 2 * levels + 1
    owner_row, tile_index, obs_frac, obs_count, owner_col = obs
    slots = owner_row.shape[1]
    extra = [] if temper_field is None else [temper_field]

    def kernel(me_ref, ssh_ref, count_ref, kappa_ref, sea_ref, sigma_ref, beta_ref,
               owner_ref, tile_ref, frac_ref, column_ref, *refs):
        inc_ref, height_ref, send_ref, profile_ref, tiles_ref = refs[-5:]

        def store(kind, level, lanes, value):
            profile_ref[(kind + len(extra)) * levels + level, :, lanes] = value

        solve_columns(
            plan, me_ref, refs[len(extra) :], tiles_ref, kappa_ref, sea_ref, levels, store
        )
        for block in range(plan.blocks):
            lanes = slice(block * LANES, (block + 1) * LANES)
            height = None
            for level in range(levels):
                source = refs[0] if extra else profile_ref
                temper = sigma_ref[0, level, :, lanes] * source[level, :, lanes]
                saline = (
                    sigma_ref[1, level, :, lanes] * profile_ref[levels + level, :, lanes]
                    + beta_ref[level, :, lanes] * temper
                )
                term = ssh_ref[0, level] * temper + ssh_ref[1, level] * saline
                height = term if height is None else height + term
                profile_ref[level, :, lanes] = temper
                profile_ref[levels + level, :, lanes] = saline
                inc_ref[0, level, :, lanes] = temper
                inc_ref[1, level, :, lanes] = saline
            profile_ref[2 * levels, :, lanes] = height
            height_ref[:, lanes] = height

        cell = tile_ref[...]
        row, col = cell // cols, cell % cols
        frac_x, frac_y = frac_ref[0:1, :], frac_ref[1:2, :]
        along = lax.broadcasted_iota(jnp.int32, (cols, slots), 0)
        weight_x = jnp.where(along == col, 1.0 - frac_x, jnp.where(along == col + 1, frac_x, 0.0))
        across = lax.broadcasted_iota(jnp.int32, (rows, slots), 0)
        weight_y = jnp.where(across == row, 1.0 - frac_y, jnp.where(across == row + 1, frac_y, 0.0))
        partial = lax.dot_general(
            profile_ref[...].reshape(records * rows, cols),
            weight_x,
            NN,
            precision=lax.Precision.HIGHEST,
            preferred_element_type=jnp.float32,
        ).reshape(records, rows, slots)
        interp = jnp.sum(partial * weight_y[None], axis=1)
        slot = lax.broadcasted_iota(jnp.int32, (1, slots), 1)
        interp = interp * (slot < count_ref[0]).astype(jnp.float32)
        earlier = lax.broadcasted_iota(jnp.int32, (slots, slots), 0) < lax.broadcasted_iota(
            jnp.int32, (slots, slots), 1
        )
        owner = owner_ref[...]
        same = jnp.where((column_ref[...] == owner) & earlier, 1.0, 0.0)
        rank = jnp.sum(same, axis=0, keepdims=True).astype(jnp.int32)
        padded = jnp.concatenate(
            [interp, jnp.zeros((RANK_ROWS - records, slots), jnp.float32)], axis=0
        )
        ranked = jnp.concatenate(
            [jnp.where(rank == r, padded, 0.0) for r in range(CAP)], axis=0
        )
        ranked = jnp.concatenate(
            [ranked, jnp.zeros((LANES - CAP * RANK_ROWS, slots), jnp.float32)], axis=0
        )
        to_owner = (owner == lax.broadcasted_iota(jnp.int32, (devices, slots), 0)).astype(
            jnp.float32
        )
        send_ref[...] = lax.dot_general(
            to_owner, ranked, NT, precision=lax.Precision.HIGHEST, preferred_element_type=jnp.float32
        )

    operands = [me, ssh_coef, obs_count, kappa, sea_mask, sigma, beta,
                owner_row, tile_index, obs_frac, owner_col] + extra + returned
    outs = [
        jax.ShapeDtypeStruct((2, levels, rows, cols), jnp.float32),
        jax.ShapeDtypeStruct((rows, cols), jnp.float32),
        jax.ShapeDtypeStruct((devices, LANES), jnp.float32),
    ]
    moved = sum(a.size * a.dtype.itemsize for a in operands + outs)
    return pl.pallas_call(
        kernel,
        out_shape=outs,
        in_specs=[pl.BlockSpec(memory_space=pltpu.SMEM)] * 3
        + [pl.BlockSpec(memory_space=pltpu.VMEM)] * (len(operands) - 3),
        out_specs=[pl.BlockSpec(memory_space=pltpu.VMEM)] * 3,
        scratch_shapes=[pltpu.VMEM((records, rows, cols), jnp.float32), plan.tiles],
        compiler_params=pltpu.CompilerParams(vmem_limit_bytes=32 * 2**20),
        cost_estimate=pl.CostEstimate(flops=1, bytes_accessed=1, transcendentals=0),
    )(*operands)


def receive(arrived, records):
    devices = arrived.shape[0]

    def kernel(in_ref, out_ref):
        turned = jnp.transpose(in_ref[...])
        for r in range(CAP):
            out_ref[:, r, :] = turned[r * RANK_ROWS : r * RANK_ROWS + records, :]

    out = call(kernel, jax.ShapeDtypeStruct((records, CAP, devices), jnp.float32), [arrived])
    return jnp.swapaxes(out, 0, 1)


def body(gx_count, gy_count, control, sigma, kappa, beta, sea_mask, x_inverse, y_inverse, ssh_coef,
         obs_owner, tile_index, obs_frac, obs_count):
    _, kinds, levels, rows, cols = control.shape
    devices = gx_count * gy_count
    plan = Plan(levels, rows, cols, gy_count // 2)
    chunks = kinds
    if not plan.fits:
        plan, chunks = Plan(kinds * levels, rows, cols, gy_count // 2), 1
    plans = [[plan] for _ in range(chunks)]
    half = Plan(plan.fields // 2, rows, cols, gy_count // 2)
    if plan.fields % 2 == 0 and half.fits and half.full:
        plans[0] = [half, half]
    me = jnp.stack([lax.axis_index("gx"), lax.axis_index("gy")]).astype(jnp.int32)
    x_parts = prepare_x(x_inverse)
    y_columns = y_inverse.reshape(y_inverse.shape[0], gy_count // 2, 2, rows)
    y_columns = jnp.where(me[1] % 2 == 0, y_columns[:, :, 0], y_columns[:, :, 1])
    y_columns = y_columns.reshape(y_inverse.shape[0], -1)
    y_far = gather_far(y_columns, "gx", gx_count)
    whole = control.reshape(kinds * levels, rows, cols)
    fields = [[]]
    for part in plans[0]:
        fields[0].append(whole[len(fields[0]) * part.fields : (len(fields[0]) + 1) * part.fields])
        whole = after(whole, fields[0][-1])
    y_held = gather_near(y_columns, "gx", gx_count) + y_far
    y_parts = prepare_y([m for m, _ in y_held], [p for _, p in y_held], me, rows)
    side_pairs = [(i, i ^ 1) for i in range(gy_count)]
    result = None
    for step in range(STEPS):
        own, other, lines = [], [], []
        for chunk in range(chunks):
            held_back, lines, totals = lines, [], []
            for part, piece in zip(plans[chunk], fields[chunk]):
                near = gather_near(piece, "gx", gx_count)
                totals.append(zonal_start(part, near, me, *x_parts))
            for number, (part, piece) in enumerate(zip(plans[chunk], fields[chunk])):
                total = totals[number]
                hold = [total]
                if chunk > 0:
                    hold += [y_parts[0]] + held_back
                elif step > 0:
                    hold += returned[::-1]
                else:
                    hold += lines
                    if number > 0:
                        hold += [y_far[0][1]] + [pieces[0] for pieces in fields[1:]]
                far = gather_far(piece, "gx", gx_count, hold)
                if own:
                    total = after(total, own[-1])
                packed = zonal_end(part, total, far, me, *x_parts, sea_mask)
                if step == 0 and len(fields) < chunks:
                    whole = after(whole, packed[0], y_far[0][1])
                    for later in range(1, chunks):
                        start = later * plan.fields
                        fields.append([whole[start : start + plan.fields]])
                ready = other[-1] if other else y_parts[0] if number else totals[-1]
                lines += [after(line, ready) for line in exchange(packed, "gy", gy_count)]
            stack = Stack(plans[chunk])
            for_own, for_other = meridional(stack, me, lines, *y_parts)
            own.append(for_own)
            other.append(lax.ppermute(for_other, "gy", side_pairs))
        for chunk in range(chunks):
            stack = Stack(plans[chunk])
            if chunk == 0:
                own[chunk] = after(own[chunk], own[-1])
            elif step < STEPS - 1:
                own[chunk] = after(own[chunk], *fields[chunk - 1])
            returned = exchange(add_sides(stack, me, own[chunk], other[chunk]), "gy", gy_count)
            if chunk < chunks - 1:
                returned = [after(block, other[-1]) for block in returned]
            if step < STEPS - 1 or chunk < chunks - 1:
                fields[chunk] = [vertical(stack, me, returned, kappa, sea_mask, levels)]
            else:
                tempers = [pieces[0] for pieces in fields[:chunk]]
                returned = [after(block, *tempers) for block in returned]
                obs = (
                    obs_owner.reshape(1, -1),
                    tile_index.reshape(1, -1),
                    obs_frac,
                    obs_count,
                    obs_owner,
                )
                result = finish(
                    stack, me, returned, tempers[0] if chunks > 1 else None, kappa, sea_mask,
                    sigma, beta, ssh_coef, obs, devices,
                )
        plans = [[plan] for _ in range(chunks)]
    increments, height, outgoing = result
    arrived = lax.all_to_all(outgoing, ("gx", "gy"), split_axis=0, concat_axis=0, tiled=True)
    return increments[None], height[None], receive(arrived, kinds * levels + 1)


def solution(mesh):
    return jax.shard_map(
        functools.partial(body, mesh.shape["gx"], mesh.shape["gy"]),
        mesh=mesh,
        in_specs=(
            P(None, None, None, "gy", "gx"),
            P(None, None, "gy", "gx"),
            P(None, "gy", "gx"),
            P(None, "gy", "gx"),
            P("gy", "gx"),
            P("gx", None),
            P("gx", None),
            P(),
            P(("gx", "gy"), None),
            P(("gx", "gy")),
            P(None, ("gx", "gy")),
            P(("gx", "gy")),
        ),
        out_specs=(
            P(None, None, None, "gy", "gx"),
            P(None, "gy", "gx"),
            P(None, None, ("gx", "gy")),
        ),
        check_vma=False,
    )
```

```python
import functools

import jax
import jax.numpy as jnp
from jax import lax
from jax.experimental import pallas as pl
from jax.experimental.pallas import tpu as pltpu
from jax.sharding import PartitionSpec as P

STEPS = 2
CAP = 2
LANES = 128
SUB = 8
RANK_ROWS = 16
NN = (((1,), (0,)), ((), ()))
NT = (((1,), (1,)), ((), ()))


class Plan:
    def __init__(self, fields, rows, cols, parts):
        self.fields, self.rows, self.cols, self.parts = fields, rows, cols, parts
        self.blocks = cols // LANES
        tiles = fields * self.blocks
        share = fields * cols // parts
        self.full = share // LANES
        self.rest = share % LANES
        self.sides = LANES // self.rest if self.rest else 0
        self.groups = rows // SUB
        self.packs = -(-self.groups // self.sides) if self.rest else 0
        self.width = self.full * rows + self.packs * SUB
        self.columns = (self.full + (1 if self.rest else 0)) * LANES
        self.fits = (
            cols % LANES == 0
            and rows % SUB == 0
            and fields * cols % parts == 0
            and (self.rest == 0 or LANES % self.rest == 0)
            and tiles - self.full * parts == (parts // self.sides if self.rest else 0)
        )

    def moved(self, side, place):
        return ((side - place) * self.rest) % LANES

    def pack_rest(self, tile, place):
        lane_side = lax.broadcasted_iota(jnp.int32, (SUB, LANES), 1) // self.rest
        out = []
        for pack in range(self.packs):
            joined = None
            for side in range(self.sides):
                group = pack * self.sides + side
                if group >= self.groups:
                    break
                piece = turn(tile[group * SUB : (group + 1) * SUB, :], self.moved(side, place))
                joined = piece if joined is None else jnp.where(lane_side == side, piece, joined)
            out.append(joined)
        return out

    def unpack_rest(self, ref, place):
        pieces = []
        for group in range(self.groups):
            pack, side = divmod(group, self.sides)
            start = self.full * self.rows + pack * SUB
            pieces.append(turn(ref[start : start + SUB, :], self.moved(place, side)))
        return jnp.concatenate(pieces, axis=0)

    def store_rest(self, ref, packs):
        for pack, value in enumerate(packs):
            start = self.full * self.rows + pack * SUB
            ref[start : start + SUB, :] = value

    def send_tiles(self, tiles_ref, device, out_ref):
        for i in range(self.full):
            out_ref[i * self.rows : (i + 1) * self.rows, :] = tiles_ref[device * self.full + i]
        if self.rest:
            tile = tiles_ref[self.parts * self.full + device // self.sides]
            self.store_rest(out_ref, self.pack_rest(tile, device % self.sides))

    def take_tiles(self, in_ref, device, tiles_ref):
        for i in range(self.full):
            tiles_ref[device * self.full + i] = in_ref[i * self.rows : (i + 1) * self.rows, :]
        if self.rest:
            place = device % self.sides
            index = self.parts * self.full + device // self.sides
            lane_side = lax.broadcasted_iota(jnp.int32, (self.rows, LANES), 1) // self.rest
            tiles_ref[index] = jnp.where(
                lane_side == place, self.unpack_rest(in_ref, place), tiles_ref[index]
            )

    @property
    def tiles(self):
        return pltpu.VMEM((self.fields * self.blocks, self.rows, LANES), jnp.float32)

    @property
    def blocks_out(self):
        shape = jax.ShapeDtypeStruct((self.width, LANES), jnp.float32)
        return [shape] * self.parts


def part_of(me_ref, mask):
    return (me_ref[1] // 2) ^ mask


def turn(value, shift):
    if isinstance(shift, int) and shift == 0:
        return value
    return pltpu.roll(value, shift, axis=1)


def split(value):
    high = value.astype(jnp.bfloat16)
    low = (value - high.astype(jnp.float32)).astype(jnp.bfloat16)
    return high, low


def dot(a, b, dims=NN):
    return lax.dot_general(a, b, dims, preferred_element_type=jnp.float32)


def wide_left(value):
    high, low = split(value)
    return jnp.concatenate([high, high, low], axis=1)


def wide_right(value):
    high, low = split(value)
    return jnp.concatenate([high, low, high], axis=0)


def call(kernel, out_shape, operands, scalars=(), flops=0, scratch=()):
    outs = out_shape if isinstance(out_shape, (list, tuple)) else [out_shape]
    moved = sum(a.size * a.dtype.itemsize for a in list(operands) + list(outs))
    specs = [
        pl.BlockSpec(memory_space=pltpu.SMEM if i in scalars else pltpu.VMEM)
        for i in range(len(operands))
    ]
    out_spec = pl.BlockSpec(memory_space=pltpu.VMEM)
    many = isinstance(out_shape, (list, tuple))
    return pl.pallas_call(
        kernel,
        out_shape=out_shape,
        in_specs=specs,
        out_specs=[out_spec] * len(outs) if many else out_spec,
        scratch_shapes=list(scratch),
        compiler_params=pltpu.CompilerParams(vmem_limit_bytes=min(48, 6 + 3 * moved // 2**20) * 2**20),
        cost_estimate=pl.CostEstimate(flops=1, bytes_accessed=1, transcendentals=0),
    )(*operands)


def after(value, *others):
    return lax.optimization_barrier((value,) + others)[0]


def gather_near(block, axis, count):
    pairs = [(i, i ^ 1) for i in range(count)]
    return [(0, block), (1, lax.ppermute(block, axis, pairs))]


def gather_far(block, axis, count, hold=()):
    held = [(0, block)]
    bit = count // 2
    while bit:
        pairs = [(i, i ^ bit) for i in range(count)]
        sources = held if bit > 1 else held[1:]
        brought = [(mask ^ bit, lax.ppermute(piece, axis, pairs)) for mask, piece in sources]
        if hold and bit == count // 2 and bit > 1:
            brought = [(mask, after(piece, *hold)) for mask, piece in brought]
        held = held + brought
        bit //= 2
    return held[1:]


def exchange(blocks, axis, count):
    out = [blocks[0]] + [None] * (len(blocks) - 1)
    for mask in range(1, len(blocks)):
        pairs = [(i, i ^ (2 * mask)) for i in range(count)]
        out[mask] = lax.ppermute(blocks[mask], axis, pairs)
    return out


def prepare_x(x_inverse):
    rows, cols = x_inverse.shape

    def kernel(x_ref, out_ref):
        for owner in range(cols // rows):
            block = jnp.transpose(x_ref[:, owner * rows : (owner + 1) * rows])
            out_ref[3 * owner * rows : 3 * (owner + 1) * rows, :] = wide_right(block)

    return call(kernel, jax.ShapeDtypeStruct((3 * cols, rows), jnp.bfloat16), [x_inverse])


def prepare_y(masks, pieces, me, rows):
    owned, half = pieces[0].shape

    def kernel(me_ref, *refs):
        out_ref, whole_ref = refs[-2:]
        side = lax.rem(me_ref[1], 2)
        for mask, ref in zip(masks, refs):
            start = pl.multiple_of((me_ref[0] ^ mask) * owned, owned)
            whole_ref[pl.ds(start, owned), :] = ref[...]
        for other in range(2):
            for part in range(half // rows):
                start = pl.multiple_of((2 * part + (side ^ other)) * rows, rows)
                out = other * half + part * rows
                out_ref[out : out + rows, :] = wide_left(whole_ref[pl.ds(start, rows), :])

    return call(
        kernel,
        jax.ShapeDtypeStruct((2 * half, 3 * half), jnp.bfloat16),
        [me] + pieces,
        scalars=(0,),
        scratch=[pltpu.VMEM((2 * half, half), jnp.float32)],
    )


def add_zonal(total, masks, me_ref, x_ref, refs):
    for mask, ref in zip(masks, refs):
        fields, rows, cols = ref.shape
        start = pl.multiple_of((me_ref[0] ^ mask) * (3 * cols), 3 * cols)
        values = wide_left(ref[...].reshape(fields * rows, cols))
        part = dot(values, x_ref[pl.ds(start, 3 * cols), :])
        total = part if total is None else total + part
    return total


def zonal_start(plan, held, me, x_wide):
    masks, pieces = [m for m, _ in held], [p for _, p in held]

    def kernel(me_ref, x_ref, *refs):
        refs[-1][...] = add_zonal(None, masks, me_ref, x_ref, refs)

    return call(
        kernel,
        jax.ShapeDtypeStruct((plan.fields * plan.rows, plan.cols), jnp.float32),
        [me, x_wide] + pieces,
        scalars=(0,),
        flops=6 * plan.fields * plan.rows * plan.cols**2 * len(pieces),
    )


def zonal_end(plan, total, held, me, x_wide, sea_mask):
    fields, rows, cols, parts = plan.fields, plan.rows, plan.cols, plan.parts
    masks, pieces = [m for m, _ in held], [p for _, p in held]

    def kernel(me_ref, x_ref, sea_ref, total_ref, *refs):
        out_refs, tiles_ref = refs[-parts - 1 : -1], refs[-1]
        result = add_zonal(total_ref[...], masks, me_ref, x_ref, refs)
        result = result.reshape(fields, rows, cols)
        sea = sea_ref[...].astype(jnp.float32)
        for block in range(plan.blocks):
            lanes = slice(block * LANES, (block + 1) * LANES)
            for field in range(fields):
                tiles_ref[field * plan.blocks + block] = sea[:, lanes] * result[field, :, lanes]
        for mask in range(parts):
            plan.send_tiles(tiles_ref, part_of(me_ref, mask), out_refs[mask])

    return call(
        kernel,
        plan.blocks_out,
        [me, x_wide, sea_mask, total] + pieces,
        scalars=(0,),
        flops=6 * fields * rows * cols**2 * len(pieces),
        scratch=[plan.tiles],
    )


def meridional(plan, me, lines, y_wide):
    rows, parts = plan.rows, plan.parts

    def kernel(me_ref, y_ref, *refs):
        in_refs, out_refs, lines_ref = refs[:parts], refs[parts:-1], refs[-1]
        for mask in range(parts):
            place = pl.ds(pl.multiple_of(part_of(me_ref, mask) * rows, rows), rows)
            for i in range(plan.full):
                lanes = slice(i * LANES, (i + 1) * LANES)
                lines_ref[place, lanes] = in_refs[mask][i * rows : (i + 1) * rows, :]
            if plan.rest:
                lines_ref[place, plan.full * LANES :] = plan.unpack_rest(in_refs[mask], 0)
        solved = dot(y_ref[...], wide_right(lines_ref[...]))
        for other in range(2):
            for part in range(parts):
                start = (other * parts + part) * rows
                for i in range(plan.full):
                    lanes = slice(i * LANES, (i + 1) * LANES)
                    out_refs[other][part, i * rows : (i + 1) * rows, :] = solved[
                        start : start + rows, lanes
                    ]
                if plan.rest:
                    last = solved[start : start + rows, plan.full * LANES :]
                    plan.store_rest(out_refs[other].at[part], plan.pack_rest(last, 0))

    shape = jax.ShapeDtypeStruct((parts, plan.width, LANES), jnp.float32)
    return call(
        kernel,
        [shape, shape],
        [me, y_wide] + lines,
        scalars=(0,),
        flops=12 * (parts * rows) ** 2 * plan.columns,
        scratch=[pltpu.VMEM((parts * rows, plan.columns), jnp.float32)],
    )


def add_sides(plan, me, own, other):
    def kernel(me_ref, own_ref, other_ref, *out_refs):
        for mask in range(plan.parts):
            part = part_of(me_ref, mask)
            out_refs[mask][...] = own_ref[part] + other_ref[part]

    return call(kernel, plan.blocks_out, [me, own, other], scalars=(0,))


def solve_columns(plan, me_ref, in_refs, tiles_ref, kappa_ref, sea_ref, levels, store):
    kinds = plan.fields // levels
    for mask in range(plan.parts):
        plan.take_tiles(in_refs[mask], part_of(me_ref, mask), tiles_ref)
    for block in range(plan.blocks):
        lanes = slice(block * LANES, (block + 1) * LANES)
        sea = sea_ref[:, lanes].astype(jnp.float32)
        inverse, upper = [], []
        kappa = [kappa_ref[level, :, lanes] for level in range(levels - 1)]
        for level in range(levels):
            below = kappa[level - 1] if level > 0 else 0.0
            above = kappa[level] if level < levels - 1 else 0.0
            pivot = 1.0 + below + above
            if level > 0:
                pivot = pivot + below * upper[-1]
            inverse.append(1.0 / pivot)
            upper.append(-above * inverse[-1])
        for kind in range(kinds):
            forward = []
            for level in range(levels):
                tile = tiles_ref[(kind * levels + level) * plan.blocks + block]
                right = sea * tile
                if level > 0:
                    right = right + kappa[level - 1] * forward[-1]
                forward.append(right * inverse[level])
            value = forward[-1]
            store(kind, levels - 1, lanes, value)
            for level in range(levels - 2, -1, -1):
                value = forward[level] - upper[level] * value
                store(kind, level, lanes, value)


def vertical(plan, me, returned, kappa, sea_mask, levels):
    def kernel(me_ref, kappa_ref, sea_ref, *refs):
        in_refs, (out_ref, tiles_ref) = refs[: plan.parts], refs[plan.parts :]

        def store(kind, level, lanes, value):
            out_ref[kind * levels + level, :, lanes] = value

        solve_columns(plan, me_ref, in_refs, tiles_ref, kappa_ref, sea_ref, levels, store)

    return call(
        kernel,
        jax.ShapeDtypeStruct((plan.fields, plan.rows, plan.cols), jnp.float32),
        [me, kappa, sea_mask] + returned,
        scalars=(0,),
        scratch=[plan.tiles],
    )


def finish(plan, me, returned, temper_field, kappa, sea_mask, sigma, beta, ssh_coef, obs, devices):
    levels = sigma.shape[1]
    rows, cols = plan.rows, plan.cols
    records = 2 * levels + 1
    owner_row, tile_index, obs_frac, obs_count, owner_col = obs
    slots = owner_row.shape[1]
    extra = [] if temper_field is None else [temper_field]

    def kernel(me_ref, ssh_ref, count_ref, kappa_ref, sea_ref, sigma_ref, beta_ref,
               owner_ref, tile_ref, frac_ref, column_ref, *refs):
        inc_ref, height_ref, send_ref, profile_ref, tiles_ref = refs[-5:]

        def store(kind, level, lanes, value):
            profile_ref[(kind + len(extra)) * levels + level, :, lanes] = value

        solve_columns(
            plan, me_ref, refs[len(extra) :], tiles_ref, kappa_ref, sea_ref, levels, store
        )
        for block in range(plan.blocks):
            lanes = slice(block * LANES, (block + 1) * LANES)
            height = None
            for level in range(levels):
                source = refs[0] if extra else profile_ref
                temper = sigma_ref[0, level, :, lanes] * source[level, :, lanes]
                saline = (
                    sigma_ref[1, level, :, lanes] * profile_ref[levels + level, :, lanes]
                    + beta_ref[level, :, lanes] * temper
                )
                term = ssh_ref[0, level] * temper + ssh_ref[1, level] * saline
                height = term if height is None else height + term
                profile_ref[level, :, lanes] = temper
                profile_ref[levels + level, :, lanes] = saline
                inc_ref[0, level, :, lanes] = temper
                inc_ref[1, level, :, lanes] = saline
            profile_ref[2 * levels, :, lanes] = height
            height_ref[:, lanes] = height

        cell = tile_ref[...]
        row, col = cell // cols, cell % cols
        frac_x, frac_y = frac_ref[0:1, :], frac_ref[1:2, :]
        along = lax.broadcasted_iota(jnp.int32, (cols, slots), 0)
        weight_x = jnp.where(along == col, 1.0 - frac_x, jnp.where(along == col + 1, frac_x, 0.0))
        across = lax.broadcasted_iota(jnp.int32, (rows, slots), 0)
        weight_y = jnp.where(across == row, 1.0 - frac_y, jnp.where(across == row + 1, frac_y, 0.0))
        partial = lax.dot_general(
            profile_ref[...].reshape(records * rows, cols),
            weight_x,
            NN,
            precision=lax.Precision.HIGHEST,
            preferred_element_type=jnp.float32,
        ).reshape(records, rows, slots)
        interp = jnp.sum(partial * weight_y[None], axis=1)
        slot = lax.broadcasted_iota(jnp.int32, (1, slots), 1)
        interp = interp * (slot < count_ref[0]).astype(jnp.float32)
        earlier = lax.broadcasted_iota(jnp.int32, (slots, slots), 0) < lax.broadcasted_iota(
            jnp.int32, (slots, slots), 1
        )
        owner = owner_ref[...]
        same = jnp.where((column_ref[...] == owner) & earlier, 1.0, 0.0)
        rank = jnp.sum(same, axis=0, keepdims=True).astype(jnp.int32)
        padded = jnp.concatenate(
            [interp, jnp.zeros((RANK_ROWS - records, slots), jnp.float32)], axis=0
        )
        ranked = jnp.concatenate(
            [jnp.where(rank == r, padded, 0.0) for r in range(CAP)], axis=0
        )
        ranked = jnp.concatenate(
            [ranked, jnp.zeros((LANES - CAP * RANK_ROWS, slots), jnp.float32)], axis=0
        )
        to_owner = (owner == lax.broadcasted_iota(jnp.int32, (devices, slots), 0)).astype(
            jnp.float32
        )
        send_ref[...] = lax.dot_general(
            to_owner, ranked, NT, precision=lax.Precision.HIGHEST, preferred_element_type=jnp.float32
        )

    operands = [me, ssh_coef, obs_count, kappa, sea_mask, sigma, beta,
                owner_row, tile_index, obs_frac, owner_col] + extra + returned
    outs = [
        jax.ShapeDtypeStruct((2, levels, rows, cols), jnp.float32),
        jax.ShapeDtypeStruct((rows, cols), jnp.float32),
        jax.ShapeDtypeStruct((devices, LANES), jnp.float32),
    ]
    moved = sum(a.size * a.dtype.itemsize for a in operands + outs)
    return pl.pallas_call(
        kernel,
        out_shape=outs,
        in_specs=[pl.BlockSpec(memory_space=pltpu.SMEM)] * 3
        + [pl.BlockSpec(memory_space=pltpu.VMEM)] * (len(operands) - 3),
        out_specs=[pl.BlockSpec(memory_space=pltpu.VMEM)] * 3,
        scratch_shapes=[pltpu.VMEM((records, rows, cols), jnp.float32), plan.tiles],
        compiler_params=pltpu.CompilerParams(vmem_limit_bytes=32 * 2**20),
        cost_estimate=pl.CostEstimate(flops=1, bytes_accessed=1, transcendentals=0),
    )(*operands)


def receive(arrived, records):
    devices = arrived.shape[0]

    def kernel(in_ref, out_ref):
        turned = jnp.transpose(in_ref[...])
        for r in range(CAP):
            out_ref[:, r, :] = turned[r * RANK_ROWS : r * RANK_ROWS + records, :]

    out = call(kernel, jax.ShapeDtypeStruct((records, CAP, devices), jnp.float32), [arrived])
    return jnp.swapaxes(out, 0, 1)


def body(gx_count, gy_count, control, sigma, kappa, beta, sea_mask, x_inverse, y_inverse, ssh_coef,
         obs_owner, tile_index, obs_frac, obs_count):
    _, kinds, levels, rows, cols = control.shape
    devices = gx_count * gy_count
    plan = Plan(levels, rows, cols, gy_count // 2)
    chunks = kinds
    if not plan.fits:
        plan, chunks = Plan(kinds * levels, rows, cols, gy_count // 2), 1
    me = jnp.stack([lax.axis_index("gx"), lax.axis_index("gy")]).astype(jnp.int32)
    x_wide = prepare_x(x_inverse)
    fields = [control[0, 0] if chunks > 1 else control.reshape(plan.fields, rows, cols)]
    if chunks > 1:
        control = after(control, fields[0])
        fields += [control[0, kind] for kind in range(1, kinds)]
    y_columns = y_inverse.reshape(y_inverse.shape[0], gy_count // 2, 2, rows)
    y_columns = jnp.where(me[1] % 2 == 0, y_columns[:, :, 0], y_columns[:, :, 1])
    y_columns = y_columns.reshape(y_inverse.shape[0], -1)
    y_far = gather_far(y_columns, "gx", gx_count)
    y_held = gather_near(y_columns, "gx", gx_count) + y_far
    y_wide = prepare_y([m for m, _ in y_held], [p for _, p in y_held], me, rows)
    side_pairs = [(i, i ^ 1) for i in range(gy_count)]
    result = None
    for step in range(STEPS):
        own, other, sent = [], [], []
        for chunk in range(chunks):
            near = gather_near(fields[chunk], "gx", gx_count)
            total = zonal_start(plan, near, me, x_wide)
            if sent:
                hold = [total, y_wide] + lines
            elif step == 0:
                hold = [total, y_far[0][1]] + fields[1:]
            else:
                hold = [total] + returned[::-1]
            far = gather_far(fields[chunk], "gx", gx_count, hold)
            if own:
                total = after(total, own[-1])
            packed = zonal_end(plan, total, far, me, x_wide, sea_mask)
            sent.append(exchange(packed, "gy", gy_count))
            if other:
                sums = add_sides(plan, me, own[-1], other[-1])
            ready = sums[0] if other else y_wide
            lines = [after(line, ready) for line in sent[chunk]]
            for_own, for_other = meridional(plan, me, lines, y_wide)
            own.append(for_own)
            other.append(lax.ppermute(for_other, "gy", side_pairs))
        for chunk in range(chunks):
            if chunk == 0 and chunks > 1:
                blocks = [after(block, own[-1]) for block in sums]
            else:
                if chunk > 0 and step < STEPS - 1:
                    own[chunk] = after(own[chunk], fields[chunk - 1])
                blocks = add_sides(plan, me, own[chunk], other[chunk])
            returned = exchange(blocks, "gy", gy_count)
            if chunk < chunks - 1:
                returned = [after(block, other[-1]) for block in returned]
            if step < STEPS - 1 or chunk < chunks - 1:
                fields[chunk] = vertical(plan, me, returned, kappa, sea_mask, levels)
            else:
                returned = [after(block, *fields[:chunk]) for block in returned]
                obs = (
                    obs_owner.reshape(1, -1),
                    tile_index.reshape(1, -1),
                    obs_frac,
                    obs_count,
                    obs_owner,
                )
                result = finish(
                    plan, me, returned, fields[0] if chunks > 1 else None, kappa, sea_mask, sigma,
                    beta, ssh_coef, obs, devices,
                )
    increments, height, outgoing = result
    arrived = lax.all_to_all(outgoing, ("gx", "gy"), split_axis=0, concat_axis=0, tiled=True)
    return increments[None], height[None], receive(arrived, kinds * levels + 1)


def solution(mesh):
    return jax.shard_map(
        functools.partial(body, mesh.shape["gx"], mesh.shape["gy"]),
        mesh=mesh,
        in_specs=(
            P(None, None, None, "gy", "gx"),
            P(None, None, "gy", "gx"),
            P(None, "gy", "gx"),
            P(None, "gy", "gx"),
            P("gy", "gx"),
            P("gx", None),
            P("gx", None),
            P(),
            P(("gx", "gy"), None),
            P(("gx", "gy")),
            P(None, ("gx", "gy")),
            P(("gx", "gy")),
        ),
        out_specs=(
            P(None, None, None, "gy", "gx"),
            P(None, "gy", "gx"),
            P(None, None, ("gx", "gy")),
        ),
        check_vma=False,
    )
```

```python
import functools

import jax
import jax.numpy as jnp
from jax import lax
from jax.experimental import pallas as pl
from jax.experimental.pallas import tpu as pltpu
from jax.sharding import PartitionSpec as P

STEPS = 2
CAP = 2
LANES = 128
SUB = 8
RANK_ROWS = 16
NN = (((1,), (0,)), ((), ()))
NT = (((1,), (1,)), ((), ()))


class Plan:
    def __init__(self, fields, rows, cols, parts):
        self.fields, self.rows, self.cols, self.parts = fields, rows, cols, parts
        self.blocks = cols // LANES
        tiles = fields * self.blocks
        share = fields * cols // parts
        self.full = share // LANES
        self.rest = share % LANES
        self.sides = LANES // self.rest if self.rest else 0
        self.groups = rows // SUB
        self.packs = -(-self.groups // self.sides) if self.rest else 0
        self.width = self.full * rows + self.packs * SUB
        self.columns = (self.full + (1 if self.rest else 0)) * LANES
        self.fits = (
            cols % LANES == 0
            and rows % SUB == 0
            and fields * cols % parts == 0
            and (self.rest == 0 or LANES % self.rest == 0)
            and tiles - self.full * parts == (parts // self.sides if self.rest else 0)
        )

    def moved(self, side, place):
        return ((side - place) * self.rest) % LANES

    def pack_rest(self, tile, place):
        lane_side = lax.broadcasted_iota(jnp.int32, (SUB, LANES), 1) // self.rest
        out = []
        for pack in range(self.packs):
            joined = None
            for side in range(self.sides):
                group = pack * self.sides + side
                if group >= self.groups:
                    break
                piece = turn(tile[group * SUB : (group + 1) * SUB, :], self.moved(side, place))
                joined = piece if joined is None else jnp.where(lane_side == side, piece, joined)
            out.append(joined)
        return out

    def unpack_rest(self, ref, place):
        pieces = []
        for group in range(self.groups):
            pack, side = divmod(group, self.sides)
            start = self.full * self.rows + pack * SUB
            pieces.append(turn(ref[start : start + SUB, :], self.moved(place, side)))
        return jnp.concatenate(pieces, axis=0)

    def store_rest(self, ref, packs):
        for pack, value in enumerate(packs):
            start = self.full * self.rows + pack * SUB
            ref[start : start + SUB, :] = value

    def send_tiles(self, tiles_ref, device, out_ref):
        for i in range(self.full):
            out_ref[i * self.rows : (i + 1) * self.rows, :] = tiles_ref[device * self.full + i]
        if self.rest:
            tile = tiles_ref[self.parts * self.full + device // self.sides]
            self.store_rest(out_ref, self.pack_rest(tile, device % self.sides))

    def take_tiles(self, in_ref, device, tiles_ref):
        for i in range(self.full):
            tiles_ref[device * self.full + i] = in_ref[i * self.rows : (i + 1) * self.rows, :]
        if self.rest:
            place = device % self.sides
            index = self.parts * self.full + device // self.sides
            lane_side = lax.broadcasted_iota(jnp.int32, (self.rows, LANES), 1) // self.rest
            tiles_ref[index] = jnp.where(
                lane_side == place, self.unpack_rest(in_ref, place), tiles_ref[index]
            )

    @property
    def tiles(self):
        return pltpu.VMEM((self.fields * self.blocks, self.rows, LANES), jnp.float32)

    @property
    def blocks_out(self):
        shape = jax.ShapeDtypeStruct((self.width, LANES), jnp.float32)
        return [shape] * self.parts


def part_of(me_ref, mask):
    return (me_ref[1] // 2) ^ mask


def turn(value, shift):
    if isinstance(shift, int) and shift == 0:
        return value
    return pltpu.roll(value, shift, axis=1)


def split(value):
    high = value.astype(jnp.bfloat16)
    low = (value - high.astype(jnp.float32)).astype(jnp.bfloat16)
    return high, low


def dot(a, b, dims=NN):
    return lax.dot_general(a, b, dims, preferred_element_type=jnp.float32)


def dot_split(a, b):
    return dot(a[0], b[0]) + (dot(a[0], b[1]) + dot(a[1], b[0]))


def call(kernel, out_shape, operands, scalars=(), flops=0, scratch=()):
    outs = out_shape if isinstance(out_shape, (list, tuple)) else [out_shape]
    moved = sum(a.size * a.dtype.itemsize for a in list(operands) + list(outs))
    specs = [
        pl.BlockSpec(memory_space=pltpu.SMEM if i in scalars else pltpu.VMEM)
        for i in range(len(operands))
    ]
    out_spec = pl.BlockSpec(memory_space=pltpu.VMEM)
    many = isinstance(out_shape, (list, tuple))
    return pl.pallas_call(
        kernel,
        out_shape=out_shape,
        in_specs=specs,
        out_specs=[out_spec] * len(outs) if many else out_spec,
        scratch_shapes=list(scratch),
        compiler_params=pltpu.CompilerParams(vmem_limit_bytes=min(48, 6 + 3 * moved // 2**20) * 2**20),
        cost_estimate=pl.CostEstimate(flops=1, bytes_accessed=1, transcendentals=0),
    )(*operands)


def after(value, *others):
    return lax.optimization_barrier((value,) + others)[0]


def gather_near(block, axis, count):
    pairs = [(i, i ^ 1) for i in range(count)]
    return [(0, block), (1, lax.ppermute(block, axis, pairs))]


def gather_far(block, axis, count, hold=()):
    held = [(0, block)]
    bit = count // 2
    while bit:
        pairs = [(i, i ^ bit) for i in range(count)]
        sources = held if bit > 1 else held[1:]
        brought = [(mask ^ bit, lax.ppermute(piece, axis, pairs)) for mask, piece in sources]
        if hold and bit == count // 2 and bit > 1:
            brought = [(mask, after(piece, *hold)) for mask, piece in brought]
        held = held + brought
        bit //= 2
    return held[1:]


def exchange(blocks, axis, count):
    out = [blocks[0]] + [None] * (len(blocks) - 1)
    for mask in range(1, len(blocks)):
        pairs = [(i, i ^ (2 * mask)) for i in range(count)]
        out[mask] = lax.ppermute(blocks[mask], axis, pairs)
    return out


def prepare_x(x_inverse):
    rows, cols = x_inverse.shape

    def kernel(x_ref, high_ref, low_ref):
        for start in range(0, cols, rows):
            high, low = split(jnp.transpose(x_ref[:, start : start + rows]))
            high_ref[start : start + rows, :] = high
            low_ref[start : start + rows, :] = low

    shape = jax.ShapeDtypeStruct((cols, rows), jnp.bfloat16)
    return call(kernel, [shape, shape], [x_inverse])


def prepare_y(masks, pieces, me, rows):
    owned, half = pieces[0].shape

    def kernel(me_ref, *refs):
        high_ref, low_ref, whole_ref = refs[-3:]
        side = lax.rem(me_ref[1], 2)
        for mask, ref in zip(masks, refs):
            start = pl.multiple_of((me_ref[0] ^ mask) * owned, owned)
            whole_ref[pl.ds(start, owned), :] = ref[...]
        for other in range(2):
            for part in range(half // rows):
                start = pl.multiple_of((2 * part + (side ^ other)) * rows, rows)
                high, low = split(whole_ref[pl.ds(start, rows), :])
                out = other * half + part * rows
                high_ref[out : out + rows, :] = high
                low_ref[out : out + rows, :] = low

    shape = jax.ShapeDtypeStruct((2 * half, half), jnp.bfloat16)
    return call(
        kernel,
        [shape, shape],
        [me] + pieces,
        scalars=(0,),
        scratch=[pltpu.VMEM((2 * half, half), jnp.float32)],
    )


def add_zonal(total, masks, me_ref, high_ref, low_ref, refs):
    for mask, ref in zip(masks, refs):
        fields, rows, cols = ref.shape
        start = pl.multiple_of((me_ref[0] ^ mask) * cols, cols)
        values = split(ref[...].reshape(fields * rows, cols))
        weights = (high_ref[pl.ds(start, cols), :], low_ref[pl.ds(start, cols), :])
        part = dot_split(values, weights)
        total = part if total is None else total + part
    return total


def zonal_start(plan, held, me, x_high, x_low):
    masks, pieces = [m for m, _ in held], [p for _, p in held]

    def kernel(me_ref, high_ref, low_ref, *refs):
        refs[-1][...] = add_zonal(None, masks, me_ref, high_ref, low_ref, refs)

    return call(
        kernel,
        jax.ShapeDtypeStruct((plan.fields * plan.rows, plan.cols), jnp.float32),
        [me, x_high, x_low] + pieces,
        scalars=(0,),
        flops=6 * plan.fields * plan.rows * plan.cols**2 * len(pieces),
    )


def zonal_end(plan, total, held, me, x_high, x_low, sea_mask):
    fields, rows, cols, parts = plan.fields, plan.rows, plan.cols, plan.parts
    masks, pieces = [m for m, _ in held], [p for _, p in held]

    def kernel(me_ref, high_ref, low_ref, sea_ref, total_ref, *refs):
        out_refs, tiles_ref = refs[-parts - 1 : -1], refs[-1]
        result = add_zonal(total_ref[...], masks, me_ref, high_ref, low_ref, refs)
        result = result.reshape(fields, rows, cols)
        sea = sea_ref[...].astype(jnp.float32)
        for block in range(plan.blocks):
            lanes = slice(block * LANES, (block + 1) * LANES)
            for field in range(fields):
                tiles_ref[field * plan.blocks + block] = sea[:, lanes] * result[field, :, lanes]
        for mask in range(parts):
            plan.send_tiles(tiles_ref, part_of(me_ref, mask), out_refs[mask])

    return call(
        kernel,
        plan.blocks_out,
        [me, x_high, x_low, sea_mask, total] + pieces,
        scalars=(0,),
        flops=6 * fields * rows * cols**2 * len(pieces),
        scratch=[plan.tiles],
    )


def meridional(plan, me, lines, y_high, y_low):
    rows, parts = plan.rows, plan.parts

    def kernel(me_ref, high_ref, low_ref, *refs):
        in_refs, out_refs, lines_ref, solved_ref = refs[:parts], refs[parts:-2], refs[-2], refs[-1]
        for mask in range(parts):
            place = pl.ds(pl.multiple_of(part_of(me_ref, mask) * rows, rows), rows)
            for i in range(plan.full):
                lanes = slice(i * LANES, (i + 1) * LANES)
                lines_ref[place, lanes] = in_refs[mask][i * rows : (i + 1) * rows, :]
            if plan.rest:
                lines_ref[place, plan.full * LANES :] = plan.unpack_rest(in_refs[mask], 0)
        solved_ref[...] = dot_split((high_ref[...], low_ref[...]), split(lines_ref[...]))
        for other in range(2):
            for part in range(parts):
                start = (other * parts + part) * rows
                for i in range(plan.full):
                    lanes = slice(i * LANES, (i + 1) * LANES)
                    out_refs[other][part, i * rows : (i + 1) * rows, :] = solved_ref[
                        start : start + rows, lanes
                    ]
                if plan.rest:
                    last = solved_ref[start : start + rows, plan.full * LANES :]
                    plan.store_rest(out_refs[other].at[part], plan.pack_rest(last, 0))

    shape = jax.ShapeDtypeStruct((parts, plan.width, LANES), jnp.float32)
    return call(
        kernel,
        [shape, shape],
        [me, y_high, y_low] + lines,
        scalars=(0,),
        flops=12 * (parts * rows) ** 2 * plan.columns,
        scratch=[
            pltpu.VMEM((parts * rows, plan.columns), jnp.float32),
            pltpu.VMEM((2 * parts * rows, plan.columns), jnp.float32),
        ],
    )


def add_sides(plan, me, own, other):
    def kernel(me_ref, own_ref, other_ref, *out_refs):
        for mask in range(plan.parts):
            part = part_of(me_ref, mask)
            out_refs[mask][...] = own_ref[part] + other_ref[part]

    return call(kernel, plan.blocks_out, [me, own, other], scalars=(0,))


def solve_columns(plan, me_ref, in_refs, tiles_ref, kappa_ref, sea_ref, levels, store):
    kinds = plan.fields // levels
    for mask in range(plan.parts):
        plan.take_tiles(in_refs[mask], part_of(me_ref, mask), tiles_ref)
    for block in range(plan.blocks):
        lanes = slice(block * LANES, (block + 1) * LANES)
        sea = sea_ref[:, lanes].astype(jnp.float32)
        inverse, upper = [], []
        kappa = [kappa_ref[level, :, lanes] for level in range(levels - 1)]
        for level in range(levels):
            below = kappa[level - 1] if level > 0 else 0.0
            above = kappa[level] if level < levels - 1 else 0.0
            pivot = 1.0 + below + above
            if level > 0:
                pivot = pivot + below * upper[-1]
            inverse.append(1.0 / pivot)
            upper.append(-above * inverse[-1])
        for kind in range(kinds):
            forward = []
            for level in range(levels):
                tile = tiles_ref[(kind * levels + level) * plan.blocks + block]
                right = sea * tile
                if level > 0:
                    right = right + kappa[level - 1] * forward[-1]
                forward.append(right * inverse[level])
            value = forward[-1]
            store(kind, levels - 1, lanes, value)
            for level in range(levels - 2, -1, -1):
                value = forward[level] - upper[level] * value
                store(kind, level, lanes, value)


def vertical(plan, me, returned, kappa, sea_mask, levels):
    def kernel(me_ref, kappa_ref, sea_ref, *refs):
        in_refs, (out_ref, tiles_ref) = refs[: plan.parts], refs[plan.parts :]

        def store(kind, level, lanes, value):
            out_ref[kind * levels + level, :, lanes] = value

        solve_columns(plan, me_ref, in_refs, tiles_ref, kappa_ref, sea_ref, levels, store)

    return call(
        kernel,
        jax.ShapeDtypeStruct((plan.fields, plan.rows, plan.cols), jnp.float32),
        [me, kappa, sea_mask] + returned,
        scalars=(0,),
        scratch=[plan.tiles],
    )


def finish(plan, me, returned, temper_field, kappa, sea_mask, sigma, beta, ssh_coef, obs, devices):
    levels = sigma.shape[1]
    rows, cols = plan.rows, plan.cols
    records = 2 * levels + 1
    owner_row, tile_index, obs_frac, obs_count, owner_col = obs
    slots = owner_row.shape[1]
    extra = [] if temper_field is None else [temper_field]

    def kernel(me_ref, ssh_ref, count_ref, kappa_ref, sea_ref, sigma_ref, beta_ref,
               owner_ref, tile_ref, frac_ref, column_ref, *refs):
        inc_ref, height_ref, send_ref, profile_ref, tiles_ref = refs[-5:]

        def store(kind, level, lanes, value):
            profile_ref[(kind + len(extra)) * levels + level, :, lanes] = value

        solve_columns(
            plan, me_ref, refs[len(extra) :], tiles_ref, kappa_ref, sea_ref, levels, store
        )
        for block in range(plan.blocks):
            lanes = slice(block * LANES, (block + 1) * LANES)
            height = None
            for level in range(levels):
                source = refs[0] if extra else profile_ref
                temper = sigma_ref[0, level, :, lanes] * source[level, :, lanes]
                saline = (
                    sigma_ref[1, level, :, lanes] * profile_ref[levels + level, :, lanes]
                    + beta_ref[level, :, lanes] * temper
                )
                term = ssh_ref[0, level] * temper + ssh_ref[1, level] * saline
                height = term if height is None else height + term
                profile_ref[level, :, lanes] = temper
                profile_ref[levels + level, :, lanes] = saline
                inc_ref[0, level, :, lanes] = temper
                inc_ref[1, level, :, lanes] = saline
            profile_ref[2 * levels, :, lanes] = height
            height_ref[:, lanes] = height

        cell = tile_ref[...]
        row, col = cell // cols, cell % cols
        frac_x, frac_y = frac_ref[0:1, :], frac_ref[1:2, :]
        along = lax.broadcasted_iota(jnp.int32, (cols, slots), 0)
        weight_x = jnp.where(along == col, 1.0 - frac_x, jnp.where(along == col + 1, frac_x, 0.0))
        across = lax.broadcasted_iota(jnp.int32, (rows, slots), 0)
        weight_y = jnp.where(across == row, 1.0 - frac_y, jnp.where(across == row + 1, frac_y, 0.0))
        partial = lax.dot_general(
            profile_ref[...].reshape(records * rows, cols),
            weight_x,
            NN,
            precision=lax.Precision.HIGHEST,
            preferred_element_type=jnp.float32,
        ).reshape(records, rows, slots)
        interp = jnp.sum(partial * weight_y[None], axis=1)
        slot = lax.broadcasted_iota(jnp.int32, (1, slots), 1)
        interp = interp * (slot < count_ref[0]).astype(jnp.float32)
        earlier = lax.broadcasted_iota(jnp.int32, (slots, slots), 0) < lax.broadcasted_iota(
            jnp.int32, (slots, slots), 1
        )
        owner = owner_ref[...]
        same = jnp.where((column_ref[...] == owner) & earlier, 1.0, 0.0)
        rank = jnp.sum(same, axis=0, keepdims=True).astype(jnp.int32)
        padded = jnp.concatenate(
            [interp, jnp.zeros((RANK_ROWS - records, slots), jnp.float32)], axis=0
        )
        ranked = jnp.concatenate(
            [jnp.where(rank == r, padded, 0.0) for r in range(CAP)], axis=0
        )
        ranked = jnp.concatenate(
            [ranked, jnp.zeros((LANES - CAP * RANK_ROWS, slots), jnp.float32)], axis=0
        )
        to_owner = (owner == lax.broadcasted_iota(jnp.int32, (devices, slots), 0)).astype(
            jnp.float32
        )
        send_ref[...] = lax.dot_general(
            to_owner, ranked, NT, precision=lax.Precision.HIGHEST, preferred_element_type=jnp.float32
        )

    operands = [me, ssh_coef, obs_count, kappa, sea_mask, sigma, beta,
                owner_row, tile_index, obs_frac, owner_col] + extra + returned
    outs = [
        jax.ShapeDtypeStruct((2, levels, rows, cols), jnp.float32),
        jax.ShapeDtypeStruct((rows, cols), jnp.float32),
        jax.ShapeDtypeStruct((devices, LANES), jnp.float32),
    ]
    moved = sum(a.size * a.dtype.itemsize for a in operands + outs)
    return pl.pallas_call(
        kernel,
        out_shape=outs,
        in_specs=[pl.BlockSpec(memory_space=pltpu.SMEM)] * 3
        + [pl.BlockSpec(memory_space=pltpu.VMEM)] * (len(operands) - 3),
        out_specs=[pl.BlockSpec(memory_space=pltpu.VMEM)] * 3,
        scratch_shapes=[pltpu.VMEM((records, rows, cols), jnp.float32), plan.tiles],
        compiler_params=pltpu.CompilerParams(vmem_limit_bytes=32 * 2**20),
        cost_estimate=pl.CostEstimate(flops=1, bytes_accessed=1, transcendentals=0),
    )(*operands)


def receive(arrived, records):
    devices = arrived.shape[0]

    def kernel(in_ref, out_ref):
        turned = jnp.transpose(in_ref[...])
        for r in range(CAP):
            out_ref[:, r, :] = turned[r * RANK_ROWS : r * RANK_ROWS + records, :]

    out = call(kernel, jax.ShapeDtypeStruct((records, CAP, devices), jnp.float32), [arrived])
    return jnp.swapaxes(out, 0, 1)


def body(gx_count, gy_count, control, sigma, kappa, beta, sea_mask, x_inverse, y_inverse, ssh_coef,
         obs_owner, tile_index, obs_frac, obs_count):
    _, kinds, levels, rows, cols = control.shape
    devices = gx_count * gy_count
    plan = Plan(levels, rows, cols, gy_count // 2)
    chunks = kinds
    if not plan.fits:
        plan, chunks = Plan(kinds * levels, rows, cols, gy_count // 2), 1
    me = jnp.stack([lax.axis_index("gx"), lax.axis_index("gy")]).astype(jnp.int32)
    x_parts = prepare_x(x_inverse)
    fields = [control[0, 0] if chunks > 1 else control.reshape(plan.fields, rows, cols)]
    if chunks > 1:
        control = after(control, fields[0])
        fields += [control[0, kind] for kind in range(1, kinds)]
    y_columns = y_inverse.reshape(y_inverse.shape[0], gy_count // 2, 2, rows)
    y_columns = jnp.where(me[1] % 2 == 0, y_columns[:, :, 0], y_columns[:, :, 1])
    y_columns = y_columns.reshape(y_inverse.shape[0], -1)
    y_far = gather_far(y_columns, "gx", gx_count)
    y_held = gather_near(y_columns, "gx", gx_count) + y_far
    y_parts = prepare_y([m for m, _ in y_held], [p for _, p in y_held], me, rows)
    side_pairs = [(i, i ^ 1) for i in range(gy_count)]
    result = None
    for step in range(STEPS):
        own, other, sent = [], [], []
        for chunk in range(chunks):
            near = gather_near(fields[chunk], "gx", gx_count)
            total = zonal_start(plan, near, me, *x_parts)
            if sent:
                hold = [total, y_parts[0]] + lines
            elif step == 0:
                hold = [total, y_far[0][1]] + fields[1:]
            else:
                hold = [total] + returned[::-1]
            far = gather_far(fields[chunk], "gx", gx_count, hold)
            if own:
                total = after(total, own[-1])
            packed = zonal_end(plan, total, far, me, *x_parts, sea_mask)
            sent.append(exchange(packed, "gy", gy_count))
            if other:
                sums = add_sides(plan, me, own[-1], other[-1])
            ready = sums[0] if other else y_parts[0]
            lines = [after(line, ready) for line in sent[chunk]]
            for_own, for_other = meridional(plan, me, lines, *y_parts)
            own.append(for_own)
            other.append(lax.ppermute(for_other, "gy", side_pairs))
        for chunk in range(chunks):
            if chunk == 0 and chunks > 1:
                blocks = [after(block, own[-1]) for block in sums]
            else:
                if chunk > 0 and step < STEPS - 1:
                    own[chunk] = after(own[chunk], fields[chunk - 1])
                blocks = add_sides(plan, me, own[chunk], other[chunk])
            returned = exchange(blocks, "gy", gy_count)
            if chunk < chunks - 1:
                returned = [after(block, other[-1]) for block in returned]
            if step < STEPS - 1 or chunk < chunks - 1:
                fields[chunk] = vertical(plan, me, returned, kappa, sea_mask, levels)
            else:
                returned = [after(block, *fields[:chunk]) for block in returned]
                obs = (
                    obs_owner.reshape(1, -1),
                    tile_index.reshape(1, -1),
                    obs_frac,
                    obs_count,
                    obs_owner,
                )
                result = finish(
                    plan, me, returned, fields[0] if chunks > 1 else None, kappa, sea_mask, sigma,
                    beta, ssh_coef, obs, devices,
                )
    increments, height, outgoing = result
    arrived = lax.all_to_all(outgoing, ("gx", "gy"), split_axis=0, concat_axis=0, tiled=True)
    return increments[None], height[None], receive(arrived, kinds * levels + 1)


def solution(mesh):
    return jax.shard_map(
        functools.partial(body, mesh.shape["gx"], mesh.shape["gy"]),
        mesh=mesh,
        in_specs=(
            P(None, None, None, "gy", "gx"),
            P(None, None, "gy", "gx"),
            P(None, "gy", "gx"),
            P(None, "gy", "gx"),
            P("gy", "gx"),
            P("gx", None),
            P("gx", None),
            P(),
            P(("gx", "gy"), None),
            P(("gx", "gy")),
            P(None, ("gx", "gy")),
            P(("gx", "gy")),
        ),
        out_specs=(
            P(None, None, None, "gy", "gx"),
            P(None, "gy", "gx"),
            P(None, None, ("gx", "gy")),
        ),
        check_vma=False,
    )
```

```python
import functools

import jax
import jax.numpy as jnp
from jax import lax
from jax.experimental import pallas as pl
from jax.experimental.pallas import tpu as pltpu
from jax.sharding import PartitionSpec as P

STEPS = 2
CAP = 2
LANES = 128
SUB = 8
RANK_ROWS = 16
NN = (((1,), (0,)), ((), ()))
NT = (((1,), (1,)), ((), ()))


class Plan:
    def __init__(self, fields, rows, cols, parts):
        self.fields, self.rows, self.cols, self.parts = fields, rows, cols, parts
        self.blocks = cols // LANES
        tiles = fields * self.blocks
        share = fields * cols // parts
        self.full = share // LANES
        self.rest = share % LANES
        self.sides = LANES // self.rest if self.rest else 0
        self.groups = rows // SUB
        self.packs = -(-self.groups // self.sides) if self.rest else 0
        self.width = self.full * rows + self.packs * SUB
        self.columns = (self.full + (1 if self.rest else 0)) * LANES
        self.fits = (
            cols % LANES == 0
            and rows % SUB == 0
            and fields * cols % parts == 0
            and (self.rest == 0 or LANES % self.rest == 0)
            and tiles - self.full * parts == (parts // self.sides if self.rest else 0)
        )

    def moved(self, side, place):
        return ((side - place) * self.rest) % LANES

    def pack_rest(self, tile, place):
        lane_side = lax.broadcasted_iota(jnp.int32, (SUB, LANES), 1) // self.rest
        out = []
        for pack in range(self.packs):
            joined = None
            for side in range(self.sides):
                group = pack * self.sides + side
                if group >= self.groups:
                    break
                piece = turn(tile[group * SUB : (group + 1) * SUB, :], self.moved(side, place))
                joined = piece if joined is None else jnp.where(lane_side == side, piece, joined)
            out.append(joined)
        return out

    def unpack_rest(self, ref, place):
        pieces = []
        for group in range(self.groups):
            pack, side = divmod(group, self.sides)
            start = self.full * self.rows + pack * SUB
            pieces.append(turn(ref[start : start + SUB, :], self.moved(place, side)))
        return jnp.concatenate(pieces, axis=0)

    def store_rest(self, ref, packs):
        for pack, value in enumerate(packs):
            start = self.full * self.rows + pack * SUB
            ref[start : start + SUB, :] = value

    def send_tiles(self, tiles_ref, device, out_ref):
        for i in range(self.full):
            out_ref[i * self.rows : (i + 1) * self.rows, :] = tiles_ref[device * self.full + i]
        if self.rest:
            tile = tiles_ref[self.parts * self.full + device // self.sides]
            self.store_rest(out_ref, self.pack_rest(tile, device % self.sides))

    def take_tiles(self, in_ref, device, tiles_ref):
        for i in range(self.full):
            tiles_ref[device * self.full + i] = in_ref[i * self.rows : (i + 1) * self.rows, :]
        if self.rest:
            place = device % self.sides
            index = self.parts * self.full + device // self.sides
            lane_side = lax.broadcasted_iota(jnp.int32, (self.rows, LANES), 1) // self.rest
            tiles_ref[index] = jnp.where(
                lane_side == place, self.unpack_rest(in_ref, place), tiles_ref[index]
            )

    @property
    def tiles(self):
        return pltpu.VMEM((self.fields * self.blocks, self.rows, LANES), jnp.float32)

    @property
    def blocks_out(self):
        shape = jax.ShapeDtypeStruct((self.width, LANES), jnp.float32)
        return [shape] * self.parts


def gray(number):
    return number ^ (number >> 1)


def part_of(me_ref, mask):
    return (me_ref[1] // 2) ^ gray(mask)


def turn(value, shift):
    if isinstance(shift, int) and shift == 0:
        return value
    return pltpu.roll(value, shift, axis=1)


def split(value):
    high = value.astype(jnp.bfloat16)
    low = (value - high.astype(jnp.float32)).astype(jnp.bfloat16)
    return high, low


def dot(a, b, dims=NN):
    return lax.dot_general(a, b, dims, preferred_element_type=jnp.float32)


def dot_split(a, b):
    return dot(a[0], b[0]) + (dot(a[0], b[1]) + dot(a[1], b[0]))


def call(kernel, out_shape, operands, scalars=(), flops=0, scratch=()):
    outs = out_shape if isinstance(out_shape, (list, tuple)) else [out_shape]
    moved = sum(a.size * a.dtype.itemsize for a in list(operands) + list(outs))
    specs = [
        pl.BlockSpec(memory_space=pltpu.SMEM if i in scalars else pltpu.VMEM)
        for i in range(len(operands))
    ]
    out_spec = pl.BlockSpec(memory_space=pltpu.VMEM)
    many = isinstance(out_shape, (list, tuple))
    return pl.pallas_call(
        kernel,
        out_shape=out_shape,
        in_specs=specs,
        out_specs=[out_spec] * len(outs) if many else out_spec,
        scratch_shapes=list(scratch),
        compiler_params=pltpu.CompilerParams(vmem_limit_bytes=min(48, 6 + 3 * moved // 2**20) * 2**20),
        cost_estimate=pl.CostEstimate(flops=1, bytes_accessed=1, transcendentals=0),
    )(*operands)


def after(value, *others):
    return lax.optimization_barrier((value,) + others)[0]


def gather_near(block, axis, count):
    pairs = [(i, i ^ 1) for i in range(count)]
    return [(0, block), (1, lax.ppermute(block, axis, pairs))]


def gather_far(block, axis, count, hold=()):
    held = [(0, block)]
    bit = count // 2
    while bit:
        pairs = [(i, i ^ bit) for i in range(count)]
        sources = held if bit > 1 else held[1:]
        brought = [(mask ^ bit, lax.ppermute(piece, axis, pairs)) for mask, piece in sources]
        if hold and bit == count // 2 and bit > 1:
            brought = [(mask, after(piece, *hold)) for mask, piece in brought]
        held = held + brought
        bit //= 2
    return held[1:]


def exchange(blocks, axis, count):
    out = [blocks[0]] + [None] * (len(blocks) - 1)
    for mask in range(1, len(blocks)):
        pairs = [(i, i ^ (2 * gray(mask))) for i in range(count)]
        out[mask] = lax.ppermute(blocks[mask], axis, pairs)
    return out


def prepare_x(x_inverse):
    rows, cols = x_inverse.shape

    def kernel(x_ref, high_ref, low_ref):
        for start in range(0, cols, rows):
            high, low = split(jnp.transpose(x_ref[:, start : start + rows]))
            high_ref[start : start + rows, :] = high
            low_ref[start : start + rows, :] = low

    shape = jax.ShapeDtypeStruct((cols, rows), jnp.bfloat16)
    return call(kernel, [shape, shape], [x_inverse])


def prepare_y(masks, pieces, me, rows):
    owned, half = pieces[0].shape

    def kernel(me_ref, *refs):
        high_ref, low_ref, whole_ref = refs[-3:]
        side = lax.rem(me_ref[1], 2)
        for mask, ref in zip(masks, refs):
            start = pl.multiple_of((me_ref[0] ^ mask) * owned, owned)
            whole_ref[pl.ds(start, owned), :] = ref[...]
        for other in range(2):
            for part in range(half // rows):
                start = pl.multiple_of((2 * part + (side ^ other)) * rows, rows)
                high, low = split(whole_ref[pl.ds(start, rows), :])
                out = other * half + part * rows
                high_ref[out : out + rows, :] = high
                low_ref[out : out + rows, :] = low

    shape = jax.ShapeDtypeStruct((2 * half, half), jnp.bfloat16)
    return call(
        kernel,
        [shape, shape],
        [me] + pieces,
        scalars=(0,),
        scratch=[pltpu.VMEM((2 * half, half), jnp.float32)],
    )


def add_zonal(total, masks, me_ref, high_ref, low_ref, refs):
    for mask, ref in zip(masks, refs):
        fields, rows, cols = ref.shape
        start = pl.multiple_of((me_ref[0] ^ mask) * cols, cols)
        values = split(ref[...].reshape(fields * rows, cols))
        weights = (high_ref[pl.ds(start, cols), :], low_ref[pl.ds(start, cols), :])
        part = dot_split(values, weights)
        total = part if total is None else total + part
    return total


def zonal_start(plan, held, me, x_high, x_low):
    masks, pieces = [m for m, _ in held], [p for _, p in held]

    def kernel(me_ref, high_ref, low_ref, *refs):
        refs[-1][...] = add_zonal(None, masks, me_ref, high_ref, low_ref, refs)

    return call(
        kernel,
        jax.ShapeDtypeStruct((plan.fields * plan.rows, plan.cols), jnp.float32),
        [me, x_high, x_low] + pieces,
        scalars=(0,),
        flops=6 * plan.fields * plan.rows * plan.cols**2 * len(pieces),
    )


def zonal_end(plan, total, held, me, x_high, x_low, sea_mask):
    fields, rows, cols, parts = plan.fields, plan.rows, plan.cols, plan.parts
    masks, pieces = [m for m, _ in held], [p for _, p in held]

    def kernel(me_ref, high_ref, low_ref, sea_ref, total_ref, *refs):
        out_refs, tiles_ref = refs[-parts - 1 : -1], refs[-1]
        result = add_zonal(total_ref[...], masks, me_ref, high_ref, low_ref, refs)
        result = result.reshape(fields, rows, cols)
        sea = sea_ref[...].astype(jnp.float32)
        for block in range(plan.blocks):
            lanes = slice(block * LANES, (block + 1) * LANES)
            for field in range(fields):
                tiles_ref[field * plan.blocks + block] = sea[:, lanes] * result[field, :, lanes]
        for mask in range(parts):
            plan.send_tiles(tiles_ref, part_of(me_ref, mask), out_refs[mask])

    return call(
        kernel,
        plan.blocks_out,
        [me, x_high, x_low, sea_mask, total] + pieces,
        scalars=(0,),
        flops=6 * fields * rows * cols**2 * len(pieces),
        scratch=[plan.tiles],
    )


def meridional(plan, me, lines, y_high, y_low):
    rows, parts = plan.rows, plan.parts

    def kernel(me_ref, high_ref, low_ref, *refs):
        in_refs, out_refs, lines_ref, solved_ref = refs[:parts], refs[parts:-2], refs[-2], refs[-1]
        for mask in range(parts):
            place = pl.ds(pl.multiple_of(part_of(me_ref, mask) * rows, rows), rows)
            for i in range(plan.full):
                lanes = slice(i * LANES, (i + 1) * LANES)
                lines_ref[place, lanes] = in_refs[mask][i * rows : (i + 1) * rows, :]
            if plan.rest:
                lines_ref[place, plan.full * LANES :] = plan.unpack_rest(in_refs[mask], 0)
        solved_ref[...] = dot_split((high_ref[...], low_ref[...]), split(lines_ref[...]))
        for other in range(2):
            for part in range(parts):
                start = (other * parts + part) * rows
                for i in range(plan.full):
                    lanes = slice(i * LANES, (i + 1) * LANES)
                    out_refs[other][part, i * rows : (i + 1) * rows, :] = solved_ref[
                        start : start + rows, lanes
                    ]
                if plan.rest:
                    last = solved_ref[start : start + rows, plan.full * LANES :]
                    plan.store_rest(out_refs[other].at[part], plan.pack_rest(last, 0))

    shape = jax.ShapeDtypeStruct((parts, plan.width, LANES), jnp.float32)
    return call(
        kernel,
        [shape, shape],
        [me, y_high, y_low] + lines,
        scalars=(0,),
        flops=12 * (parts * rows) ** 2 * plan.columns,
        scratch=[
            pltpu.VMEM((parts * rows, plan.columns), jnp.float32),
            pltpu.VMEM((2 * parts * rows, plan.columns), jnp.float32),
        ],
    )


def add_sides(plan, me, own, other):
    def kernel(me_ref, own_ref, other_ref, *out_refs):
        for mask in range(plan.parts):
            part = part_of(me_ref, mask)
            out_refs[mask][...] = own_ref[part] + other_ref[part]

    return call(kernel, plan.blocks_out, [me, own, other], scalars=(0,))


def solve_columns(plan, me_ref, in_refs, tiles_ref, kappa_ref, sea_ref, levels, store):
    kinds = plan.fields // levels
    for mask in range(plan.parts):
        plan.take_tiles(in_refs[mask], part_of(me_ref, mask), tiles_ref)
    for block in range(plan.blocks):
        lanes = slice(block * LANES, (block + 1) * LANES)
        sea = sea_ref[:, lanes].astype(jnp.float32)
        inverse, upper = [], []
        kappa = [kappa_ref[level, :, lanes] for level in range(levels - 1)]
        for level in range(levels):
            below = kappa[level - 1] if level > 0 else 0.0
            above = kappa[level] if level < levels - 1 else 0.0
            pivot = 1.0 + below + above
            if level > 0:
                pivot = pivot + below * upper[-1]
            inverse.append(1.0 / pivot)
            upper.append(-above * inverse[-1])
        for kind in range(kinds):
            forward = []
            for level in range(levels):
                tile = tiles_ref[(kind * levels + level) * plan.blocks + block]
                right = sea * tile
                if level > 0:
                    right = right + kappa[level - 1] * forward[-1]
                forward.append(right * inverse[level])
            value = forward[-1]
            store(kind, levels - 1, lanes, value)
            for level in range(levels - 2, -1, -1):
                value = forward[level] - upper[level] * value
                store(kind, level, lanes, value)


def vertical(plan, me, returned, kappa, sea_mask, levels):
    def kernel(me_ref, kappa_ref, sea_ref, *refs):
        in_refs, (out_ref, tiles_ref) = refs[: plan.parts], refs[plan.parts :]

        def store(kind, level, lanes, value):
            out_ref[kind * levels + level, :, lanes] = value

        solve_columns(plan, me_ref, in_refs, tiles_ref, kappa_ref, sea_ref, levels, store)

    return call(
        kernel,
        jax.ShapeDtypeStruct((plan.fields, plan.rows, plan.cols), jnp.float32),
        [me, kappa, sea_mask] + returned,
        scalars=(0,),
        scratch=[plan.tiles],
    )


def finish(plan, me, returned, temper_field, kappa, sea_mask, sigma, beta, ssh_coef, obs, devices):
    levels = sigma.shape[1]
    rows, cols = plan.rows, plan.cols
    records = 2 * levels + 1
    owner_row, tile_index, obs_frac, obs_count, owner_col = obs
    slots = owner_row.shape[1]
    extra = [] if temper_field is None else [temper_field]

    def kernel(me_ref, ssh_ref, count_ref, kappa_ref, sea_ref, sigma_ref, beta_ref,
               owner_ref, tile_ref, frac_ref, column_ref, *refs):
        inc_ref, height_ref, send_ref, profile_ref, tiles_ref = refs[-5:]

        def store(kind, level, lanes, value):
            profile_ref[(kind + len(extra)) * levels + level, :, lanes] = value

        solve_columns(
            plan, me_ref, refs[len(extra) :], tiles_ref, kappa_ref, sea_ref, levels, store
        )
        for block in range(plan.blocks):
            lanes = slice(block * LANES, (block + 1) * LANES)
            height = None
            for level in range(levels):
                source = refs[0] if extra else profile_ref
                temper = sigma_ref[0, level, :, lanes] * source[level, :, lanes]
                saline = (
                    sigma_ref[1, level, :, lanes] * profile_ref[levels + level, :, lanes]
                    + beta_ref[level, :, lanes] * temper
                )
                term = ssh_ref[0, level] * temper + ssh_ref[1, level] * saline
                height = term if height is None else height + term
                profile_ref[level, :, lanes] = temper
                profile_ref[levels + level, :, lanes] = saline
                inc_ref[0, level, :, lanes] = temper
                inc_ref[1, level, :, lanes] = saline
            profile_ref[2 * levels, :, lanes] = height
            height_ref[:, lanes] = height

        cell = tile_ref[...]
        row, col = cell // cols, cell % cols
        frac_x, frac_y = frac_ref[0:1, :], frac_ref[1:2, :]
        along = lax.broadcasted_iota(jnp.int32, (cols, slots), 0)
        weight_x = jnp.where(along == col, 1.0 - frac_x, jnp.where(along == col + 1, frac_x, 0.0))
        across = lax.broadcasted_iota(jnp.int32, (rows, slots), 0)
        weight_y = jnp.where(across == row, 1.0 - frac_y, jnp.where(across == row + 1, frac_y, 0.0))
        partial = lax.dot_general(
            profile_ref[...].reshape(records * rows, cols),
            weight_x,
            NN,
            precision=lax.Precision.HIGHEST,
            preferred_element_type=jnp.float32,
        ).reshape(records, rows, slots)
        interp = jnp.sum(partial * weight_y[None], axis=1)
        slot = lax.broadcasted_iota(jnp.int32, (1, slots), 1)
        interp = interp * (slot < count_ref[0]).astype(jnp.float32)
        earlier = lax.broadcasted_iota(jnp.int32, (slots, slots), 0) < lax.broadcasted_iota(
            jnp.int32, (slots, slots), 1
        )
        owner = owner_ref[...]
        same = jnp.where((column_ref[...] == owner) & earlier, 1.0, 0.0)
        rank = jnp.sum(same, axis=0, keepdims=True).astype(jnp.int32)
        padded = jnp.concatenate(
            [interp, jnp.zeros((RANK_ROWS - records, slots), jnp.float32)], axis=0
        )
        ranked = jnp.concatenate(
            [jnp.where(rank == r, padded, 0.0) for r in range(CAP)], axis=0
        )
        ranked = jnp.concatenate(
            [ranked, jnp.zeros((LANES - CAP * RANK_ROWS, slots), jnp.float32)], axis=0
        )
        to_owner = (owner == lax.broadcasted_iota(jnp.int32, (devices, slots), 0)).astype(
            jnp.float32
        )
        send_ref[...] = lax.dot_general(
            to_owner, ranked, NT, precision=lax.Precision.HIGHEST, preferred_element_type=jnp.float32
        )

    operands = [me, ssh_coef, obs_count, kappa, sea_mask, sigma, beta,
                owner_row, tile_index, obs_frac, owner_col] + extra + returned
    outs = [
        jax.ShapeDtypeStruct((2, levels, rows, cols), jnp.float32),
        jax.ShapeDtypeStruct((rows, cols), jnp.float32),
        jax.ShapeDtypeStruct((devices, LANES), jnp.float32),
    ]
    moved = sum(a.size * a.dtype.itemsize for a in operands + outs)
    return pl.pallas_call(
        kernel,
        out_shape=outs,
        in_specs=[pl.BlockSpec(memory_space=pltpu.SMEM)] * 3
        + [pl.BlockSpec(memory_space=pltpu.VMEM)] * (len(operands) - 3),
        out_specs=[pl.BlockSpec(memory_space=pltpu.VMEM)] * 3,
        scratch_shapes=[pltpu.VMEM((records, rows, cols), jnp.float32), plan.tiles],
        compiler_params=pltpu.CompilerParams(vmem_limit_bytes=32 * 2**20),
        cost_estimate=pl.CostEstimate(flops=1, bytes_accessed=1, transcendentals=0),
    )(*operands)


def receive(arrived, records):
    devices = arrived.shape[0]

    def kernel(in_ref, out_ref):
        turned = jnp.transpose(in_ref[...])
        for r in range(CAP):
            out_ref[:, r, :] = turned[r * RANK_ROWS : r * RANK_ROWS + records, :]

    out = call(kernel, jax.ShapeDtypeStruct((records, CAP, devices), jnp.float32), [arrived])
    return jnp.swapaxes(out, 0, 1)


def body(gx_count, gy_count, control, sigma, kappa, beta, sea_mask, x_inverse, y_inverse, ssh_coef,
         obs_owner, tile_index, obs_frac, obs_count):
    _, kinds, levels, rows, cols = control.shape
    devices = gx_count * gy_count
    plan = Plan(levels, rows, cols, gy_count // 2)
    chunks = kinds
    if not plan.fits:
        plan, chunks = Plan(kinds * levels, rows, cols, gy_count // 2), 1
    me = jnp.stack([lax.axis_index("gx"), lax.axis_index("gy")]).astype(jnp.int32)
    x_parts = prepare_x(x_inverse)
    fields = [control[0, 0] if chunks > 1 else control.reshape(plan.fields, rows, cols)]
    if chunks > 1:
        control = after(control, fields[0])
        fields += [control[0, kind] for kind in range(1, kinds)]
    y_columns = y_inverse.reshape(y_inverse.shape[0], gy_count // 2, 2, rows)
    y_columns = jnp.where(me[1] % 2 == 0, y_columns[:, :, 0], y_columns[:, :, 1])
    y_columns = y_columns.reshape(y_inverse.shape[0], -1)
    y_far = gather_far(y_columns, "gx", gx_count)
    y_held = gather_near(y_columns, "gx", gx_count) + y_far
    y_parts = prepare_y([m for m, _ in y_held], [p for _, p in y_held], me, rows)
    side_pairs = [(i, i ^ 1) for i in range(gy_count)]
    result = None
    for step in range(STEPS):
        own, other, sent = [], [], []
        for chunk in range(chunks):
            near = gather_near(fields[chunk], "gx", gx_count)
            total = zonal_start(plan, near, me, *x_parts)
            if sent:
                hold = [total, y_parts[0]] + lines
            elif step == 0:
                hold = [total, y_far[0][1]] + fields[1:]
            else:
                hold = [total] + returned[::-1]
            far = gather_far(fields[chunk], "gx", gx_count, hold)
            if own:
                total = after(total, own[-1])
            packed = zonal_end(plan, total, far, me, *x_parts, sea_mask)
            sent.append(exchange(packed, "gy", gy_count))
            if other:
                sums = add_sides(plan, me, own[-1], other[-1])
            ready = sums[0] if other else y_parts[0]
            lines = [after(line, ready) for line in sent[chunk]]
            for_own, for_other = meridional(plan, me, lines, *y_parts)
            own.append(for_own)
            other.append(lax.ppermute(for_other, "gy", side_pairs))
        for chunk in range(chunks):
            if chunk == 0 and chunks > 1:
                blocks = [after(block, own[-1]) for block in sums]
            else:
                if chunk > 0 and step < STEPS - 1:
                    own[chunk] = after(own[chunk], fields[chunk - 1])
                blocks = add_sides(plan, me, own[chunk], other[chunk])
            returned = exchange(blocks, "gy", gy_count)
            if chunk < chunks - 1:
                returned = [after(block, other[-1]) for block in returned]
            if step < STEPS - 1 or chunk < chunks - 1:
                fields[chunk] = vertical(plan, me, returned, kappa, sea_mask, levels)
            else:
                returned = [after(block, *fields[:chunk]) for block in returned]
                obs = (
                    obs_owner.reshape(1, -1),
                    tile_index.reshape(1, -1),
                    obs_frac,
                    obs_count,
                    obs_owner,
                )
                result = finish(
                    plan, me, returned, fields[0] if chunks > 1 else None, kappa, sea_mask, sigma,
                    beta, ssh_coef, obs, devices,
                )
    increments, height, outgoing = result
    arrived = lax.all_to_all(outgoing, ("gx", "gy"), split_axis=0, concat_axis=0, tiled=True)
    return increments[None], height[None], receive(arrived, kinds * levels + 1)


def solution(mesh):
    return jax.shard_map(
        functools.partial(body, mesh.shape["gx"], mesh.shape["gy"]),
        mesh=mesh,
        in_specs=(
            P(None, None, None, "gy", "gx"),
            P(None, None, "gy", "gx"),
            P(None, "gy", "gx"),
            P(None, "gy", "gx"),
            P("gy", "gx"),
            P("gx", None),
            P("gx", None),
            P(),
            P(("gx", "gy"), None),
            P(("gx", "gy")),
            P(None, ("gx", "gy")),
            P(("gx", "gy")),
        ),
        out_specs=(
            P(None, None, None, "gy", "gx"),
            P(None, "gy", "gx"),
            P(None, None, ("gx", "gy")),
        ),
        check_vma=False,
    )
```

```python
import functools

import jax
import jax.numpy as jnp
from jax import lax
from jax.experimental import pallas as pl
from jax.experimental.pallas import tpu as pltpu
from jax.sharding import PartitionSpec as P

STEPS = 2
CAP = 2
LANES = 128
SUB = 8
RANK_ROWS = 16
NN = (((1,), (0,)), ((), ()))
NT = (((1,), (1,)), ((), ()))


class Plan:
    def __init__(self, fields, rows, cols, parts):
        self.fields, self.rows, self.cols, self.parts = fields, rows, cols, parts
        self.blocks = cols // LANES
        tiles = fields * self.blocks
        share = fields * cols // parts
        self.full = share // LANES
        self.rest = share % LANES
        self.sides = LANES // self.rest if self.rest else 0
        self.groups = rows // SUB
        self.packs = -(-self.groups // self.sides) if self.rest else 0
        self.width = self.full * rows + self.packs * SUB
        self.columns = (self.full + (1 if self.rest else 0)) * LANES
        self.fits = (
            cols % LANES == 0
            and rows % SUB == 0
            and fields * cols % parts == 0
            and (self.rest == 0 or LANES % self.rest == 0)
            and tiles - self.full * parts == (parts // self.sides if self.rest else 0)
        )

    def moved(self, side, place):
        return ((side - place) * self.rest) % LANES

    def pack_rest(self, tile, place):
        lane_side = lax.broadcasted_iota(jnp.int32, (SUB, LANES), 1) // self.rest
        out = []
        for pack in range(self.packs):
            joined = None
            for side in range(self.sides):
                group = pack * self.sides + side
                if group >= self.groups:
                    break
                piece = turn(tile[group * SUB : (group + 1) * SUB, :], self.moved(side, place))
                joined = piece if joined is None else jnp.where(lane_side == side, piece, joined)
            out.append(joined)
        return out

    def unpack_rest(self, ref, place):
        pieces = []
        for group in range(self.groups):
            pack, side = divmod(group, self.sides)
            start = self.full * self.rows + pack * SUB
            pieces.append(turn(ref[start : start + SUB, :], self.moved(place, side)))
        return jnp.concatenate(pieces, axis=0)

    def store_rest(self, ref, packs):
        for pack, value in enumerate(packs):
            start = self.full * self.rows + pack * SUB
            ref[start : start + SUB, :] = value

    def send_tiles(self, tiles_ref, device, out_ref):
        for i in range(self.full):
            out_ref[i * self.rows : (i + 1) * self.rows, :] = tiles_ref[device * self.full + i]
        if self.rest:
            tile = tiles_ref[self.parts * self.full + device // self.sides]
            self.store_rest(out_ref, self.pack_rest(tile, device % self.sides))

    def take_tiles(self, in_ref, device, tiles_ref):
        for i in range(self.full):
            tiles_ref[device * self.full + i] = in_ref[i * self.rows : (i + 1) * self.rows, :]
        if self.rest:
            place = device % self.sides
            index = self.parts * self.full + device // self.sides
            lane_side = lax.broadcasted_iota(jnp.int32, (self.rows, LANES), 1) // self.rest
            tiles_ref[index] = jnp.where(
                lane_side == place, self.unpack_rest(in_ref, place), tiles_ref[index]
            )

    @property
    def tiles(self):
        return pltpu.VMEM((self.fields * self.blocks, self.rows, LANES), jnp.float32)

    @property
    def blocks_out(self):
        shape = jax.ShapeDtypeStruct((self.width, LANES), jnp.float32)
        return [shape] * self.parts


def part_of(me_ref, mask):
    return (me_ref[1] // 2) ^ mask


def turn(value, shift):
    if isinstance(shift, int) and shift == 0:
        return value
    return pltpu.roll(value, shift, axis=1)


def split(value):
    high = value.astype(jnp.bfloat16)
    low = (value - high.astype(jnp.float32)).astype(jnp.bfloat16)
    return high, low


def dot(a, b, dims=NN):
    return lax.dot_general(a, b, dims, preferred_element_type=jnp.float32)


def dot_split(a, b):
    return dot(a[0], b[0]) + (dot(a[0], b[1]) + dot(a[1], b[0]))


def call(kernel, out_shape, operands, scalars=(), flops=0, scratch=()):
    outs = out_shape if isinstance(out_shape, (list, tuple)) else [out_shape]
    moved = sum(a.size * a.dtype.itemsize for a in list(operands) + list(outs))
    specs = [
        pl.BlockSpec(memory_space=pltpu.SMEM if i in scalars else pltpu.VMEM)
        for i in range(len(operands))
    ]
    out_spec = pl.BlockSpec(memory_space=pltpu.VMEM)
    many = isinstance(out_shape, (list, tuple))
    return pl.pallas_call(
        kernel,
        out_shape=out_shape,
        in_specs=specs,
        out_specs=[out_spec] * len(outs) if many else out_spec,
        scratch_shapes=list(scratch),
        compiler_params=pltpu.CompilerParams(vmem_limit_bytes=min(48, 6 + 3 * moved // 2**20) * 2**20),
        cost_estimate=pl.CostEstimate(flops=1, bytes_accessed=1, transcendentals=0),
    )(*operands)


def after(value, *others):
    return lax.optimization_barrier((value,) + others)[0]


def gather_near(block, axis, count):
    pairs = [(i, i ^ 1) for i in range(count)]
    return [(0, block), (1, lax.ppermute(block, axis, pairs))]


def gather_far(block, axis, count, hold=()):
    held = [(0, block)]
    bit = count // 2
    while bit:
        pairs = [(i, i ^ bit) for i in range(count)]
        sources = held if bit > 1 else held[1:]
        brought = [(mask ^ bit, lax.ppermute(piece, axis, pairs)) for mask, piece in sources]
        if hold and bit == count // 2 and bit > 1:
            brought = [(mask, after(piece, *hold)) for mask, piece in brought]
        held = held + brought
        bit //= 2
    return held[1:]


def exchange(blocks, axis, count):
    out = [blocks[0]] + [None] * (len(blocks) - 1)
    for mask in range(1, len(blocks)):
        pairs = [(i, i ^ (2 * mask)) for i in range(count)]
        out[mask] = lax.ppermute(blocks[mask], axis, pairs)
    return out


def prepare_x(x_inverse):
    rows, cols = x_inverse.shape

    def kernel(x_ref, high_ref, low_ref):
        for start in range(0, cols, rows):
            high, low = split(jnp.transpose(x_ref[:, start : start + rows]))
            high_ref[start : start + rows, :] = high
            low_ref[start : start + rows, :] = low

    shape = jax.ShapeDtypeStruct((cols, rows), jnp.bfloat16)
    return call(kernel, [shape, shape], [x_inverse])


def prepare_y(masks, pieces, me, rows):
    owned, half = pieces[0].shape

    def kernel(me_ref, *refs):
        high_ref, low_ref, whole_ref = refs[-3:]
        side = lax.rem(me_ref[1], 2)
        for mask, ref in zip(masks, refs):
            start = pl.multiple_of((me_ref[0] ^ mask) * owned, owned)
            whole_ref[pl.ds(start, owned), :] = ref[...]
        for other in range(2):
            for part in range(half // rows):
                start = pl.multiple_of((2 * part + (side ^ other)) * rows, rows)
                high, low = split(whole_ref[pl.ds(start, rows), :])
                out = other * half + part * rows
                high_ref[out : out + rows, :] = high
                low_ref[out : out + rows, :] = low

    shape = jax.ShapeDtypeStruct((2 * half, half), jnp.bfloat16)
    return call(
        kernel,
        [shape, shape],
        [me] + pieces,
        scalars=(0,),
        scratch=[pltpu.VMEM((2 * half, half), jnp.float32)],
    )


def add_zonal(total, masks, me_ref, high_ref, low_ref, refs):
    for mask, ref in zip(masks, refs):
        fields, rows, cols = ref.shape
        start = pl.multiple_of((me_ref[0] ^ mask) * cols, cols)
        values = split(ref[...].reshape(fields * rows, cols))
        weights = (high_ref[pl.ds(start, cols), :], low_ref[pl.ds(start, cols), :])
        part = dot_split(values, weights)
        total = part if total is None else total + part
    return total


def zonal_start(plan, held, me, x_high, x_low):
    masks, pieces = [m for m, _ in held], [p for _, p in held]

    def kernel(me_ref, high_ref, low_ref, *refs):
        refs[-1][...] = add_zonal(None, masks, me_ref, high_ref, low_ref, refs)

    return call(
        kernel,
        jax.ShapeDtypeStruct((plan.fields * plan.rows, plan.cols), jnp.float32),
        [me, x_high, x_low] + pieces,
        scalars=(0,),
        flops=6 * plan.fields * plan.rows * plan.cols**2 * len(pieces),
    )


def zonal_end(plan, total, held, me, x_high, x_low, sea_mask):
    fields, rows, cols, parts = plan.fields, plan.rows, plan.cols, plan.parts
    masks, pieces = [m for m, _ in held], [p for _, p in held]

    def kernel(me_ref, high_ref, low_ref, sea_ref, total_ref, *refs):
        out_refs, tiles_ref = refs[-parts - 1 : -1], refs[-1]
        result = add_zonal(total_ref[...], masks, me_ref, high_ref, low_ref, refs)
        result = result.reshape(fields, rows, cols)
        sea = sea_ref[...].astype(jnp.float32)
        for block in range(plan.blocks):
            lanes = slice(block * LANES, (block + 1) * LANES)
            for field in range(fields):
                tiles_ref[field * plan.blocks + block] = sea[:, lanes] * result[field, :, lanes]
        for mask in range(parts):
            plan.send_tiles(tiles_ref, part_of(me_ref, mask), out_refs[mask])

    return call(
        kernel,
        plan.blocks_out,
        [me, x_high, x_low, sea_mask, total] + pieces,
        scalars=(0,),
        flops=6 * fields * rows * cols**2 * len(pieces),
        scratch=[plan.tiles],
    )


def meridional(plan, me, lines, y_high, y_low):
    rows, parts = plan.rows, plan.parts

    def kernel(me_ref, high_ref, low_ref, *refs):
        in_refs, out_refs, lines_ref, solved_ref = refs[:parts], refs[parts:-2], refs[-2], refs[-1]
        for mask in range(parts):
            place = pl.ds(pl.multiple_of(part_of(me_ref, mask) * rows, rows), rows)
            for i in range(plan.full):
                lanes = slice(i * LANES, (i + 1) * LANES)
                lines_ref[place, lanes] = in_refs[mask][i * rows : (i + 1) * rows, :]
            if plan.rest:
                lines_ref[place, plan.full * LANES :] = plan.unpack_rest(in_refs[mask], 0)
        solved_ref[...] = dot_split((high_ref[...], low_ref[...]), split(lines_ref[...]))
        for other in range(2):
            for part in range(parts):
                start = (other * parts + part) * rows
                for i in range(plan.full):
                    lanes = slice(i * LANES, (i + 1) * LANES)
                    out_refs[other][part, i * rows : (i + 1) * rows, :] = solved_ref[
                        start : start + rows, lanes
                    ]
                if plan.rest:
                    last = solved_ref[start : start + rows, plan.full * LANES :]
                    plan.store_rest(out_refs[other].at[part], plan.pack_rest(last, 0))

    shape = jax.ShapeDtypeStruct((parts, plan.width, LANES), jnp.float32)
    return call(
        kernel,
        [shape, shape],
        [me, y_high, y_low] + lines,
        scalars=(0,),
        flops=12 * (parts * rows) ** 2 * plan.columns,
        scratch=[
            pltpu.VMEM((parts * rows, plan.columns), jnp.float32),
            pltpu.VMEM((2 * parts * rows, plan.columns), jnp.float32),
        ],
    )


def add_sides(plan, me, own, other):
    def kernel(me_ref, own_ref, other_ref, *out_refs):
        for mask in range(plan.parts):
            part = part_of(me_ref, mask)
            out_refs[mask][...] = own_ref[part] + other_ref[part]

    return call(kernel, plan.blocks_out, [me, own, other], scalars=(0,))


def solve_columns(plan, me_ref, in_refs, tiles_ref, kappa_ref, sea_ref, levels, store):
    kinds = plan.fields // levels
    for mask in range(plan.parts):
        plan.take_tiles(in_refs[mask], part_of(me_ref, mask), tiles_ref)
    for block in range(plan.blocks):
        lanes = slice(block * LANES, (block + 1) * LANES)
        sea = sea_ref[:, lanes].astype(jnp.float32)
        inverse, upper = [], []
        kappa = [kappa_ref[level, :, lanes] for level in range(levels - 1)]
        for level in range(levels):
            below = kappa[level - 1] if level > 0 else 0.0
            above = kappa[level] if level < levels - 1 else 0.0
            pivot = 1.0 + below + above
            if level > 0:
                pivot = pivot + below * upper[-1]
            inverse.append(1.0 / pivot)
            upper.append(-above * inverse[-1])
        for kind in range(kinds):
            forward = []
            for level in range(levels):
                tile = tiles_ref[(kind * levels + level) * plan.blocks + block]
                right = sea * tile
                if level > 0:
                    right = right + kappa[level - 1] * forward[-1]
                forward.append(right * inverse[level])
            value = forward[-1]
            store(kind, levels - 1, lanes, value)
            for level in range(levels - 2, -1, -1):
                value = forward[level] - upper[level] * value
                store(kind, level, lanes, value)


def vertical(plan, me, returned, kappa, sea_mask, levels):
    def kernel(me_ref, kappa_ref, sea_ref, *refs):
        in_refs, (out_ref, tiles_ref) = refs[: plan.parts], refs[plan.parts :]

        def store(kind, level, lanes, value):
            out_ref[kind * levels + level, :, lanes] = value

        solve_columns(plan, me_ref, in_refs, tiles_ref, kappa_ref, sea_ref, levels, store)

    return call(
        kernel,
        jax.ShapeDtypeStruct((plan.fields, plan.rows, plan.cols), jnp.float32),
        [me, kappa, sea_mask] + returned,
        scalars=(0,),
        scratch=[plan.tiles],
    )


def finish(plan, me, returned, temper_field, kappa, sea_mask, sigma, beta, ssh_coef, obs, devices):
    levels = sigma.shape[1]
    rows, cols = plan.rows, plan.cols
    records = 2 * levels + 1
    owner_row, tile_index, obs_frac, obs_count, owner_col = obs
    slots = owner_row.shape[1]
    extra = [] if temper_field is None else [temper_field]

    def kernel(me_ref, ssh_ref, count_ref, kappa_ref, sea_ref, sigma_ref, beta_ref,
               owner_ref, tile_ref, frac_ref, column_ref, *refs):
        inc_ref, height_ref, send_ref, profile_ref, tiles_ref = refs[-5:]

        def store(kind, level, lanes, value):
            profile_ref[(kind + len(extra)) * levels + level, :, lanes] = value

        solve_columns(
            plan, me_ref, refs[len(extra) :], tiles_ref, kappa_ref, sea_ref, levels, store
        )
        for block in range(plan.blocks):
            lanes = slice(block * LANES, (block + 1) * LANES)
            height = None
            for level in range(levels):
                source = refs[0] if extra else profile_ref
                temper = sigma_ref[0, level, :, lanes] * source[level, :, lanes]
                saline = (
                    sigma_ref[1, level, :, lanes] * profile_ref[levels + level, :, lanes]
                    + beta_ref[level, :, lanes] * temper
                )
                term = ssh_ref[0, level] * temper + ssh_ref[1, level] * saline
                height = term if height is None else height + term
                profile_ref[level, :, lanes] = temper
                profile_ref[levels + level, :, lanes] = saline
                inc_ref[0, level, :, lanes] = temper
                inc_ref[1, level, :, lanes] = saline
            profile_ref[2 * levels, :, lanes] = height
            height_ref[:, lanes] = height

        cell = tile_ref[...]
        row, col = cell // cols, cell % cols
        frac_x, frac_y = frac_ref[0:1, :], frac_ref[1:2, :]
        along = lax.broadcasted_iota(jnp.int32, (cols, slots), 0)
        weight_x = jnp.where(along == col, 1.0 - frac_x, jnp.where(along == col + 1, frac_x, 0.0))
        across = lax.broadcasted_iota(jnp.int32, (rows, slots), 0)
        weight_y = jnp.where(across == row, 1.0 - frac_y, jnp.where(across == row + 1, frac_y, 0.0))
        partial = dot_split(
            split(profile_ref[...].reshape(records * rows, cols)), split(weight_x)
        ).reshape(records, rows, slots)
        interp = jnp.sum(partial * weight_y[None], axis=1)
        slot = lax.broadcasted_iota(jnp.int32, (1, slots), 1)
        interp = interp * (slot < count_ref[0]).astype(jnp.float32)
        earlier = lax.broadcasted_iota(jnp.int32, (slots, slots), 0) < lax.broadcasted_iota(
            jnp.int32, (slots, slots), 1
        )
        owner = owner_ref[...]
        same = jnp.where((column_ref[...] == owner) & earlier, 1.0, 0.0)
        rank = jnp.sum(same, axis=0, keepdims=True).astype(jnp.int32)
        padded = jnp.concatenate(
            [interp, jnp.zeros((RANK_ROWS - records, slots), jnp.float32)], axis=0
        )
        ranked = jnp.concatenate(
            [jnp.where(rank == r, padded, 0.0) for r in range(CAP)], axis=0
        )
        ranked = jnp.concatenate(
            [ranked, jnp.zeros((LANES - CAP * RANK_ROWS, slots), jnp.float32)], axis=0
        )
        to_owner = (owner == lax.broadcasted_iota(jnp.int32, (devices, slots), 0)).astype(
            jnp.float32
        )
        send_ref[...] = lax.dot_general(
            to_owner, ranked, NT, precision=lax.Precision.HIGHEST, preferred_element_type=jnp.float32
        )

    operands = [me, ssh_coef, obs_count, kappa, sea_mask, sigma, beta,
                owner_row, tile_index, obs_frac, owner_col] + extra + returned
    outs = [
        jax.ShapeDtypeStruct((2, levels, rows, cols), jnp.float32),
        jax.ShapeDtypeStruct((rows, cols), jnp.float32),
        jax.ShapeDtypeStruct((devices, LANES), jnp.float32),
    ]
    moved = sum(a.size * a.dtype.itemsize for a in operands + outs)
    return pl.pallas_call(
        kernel,
        out_shape=outs,
        in_specs=[pl.BlockSpec(memory_space=pltpu.SMEM)] * 3
        + [pl.BlockSpec(memory_space=pltpu.VMEM)] * (len(operands) - 3),
        out_specs=[pl.BlockSpec(memory_space=pltpu.VMEM)] * 3,
        scratch_shapes=[pltpu.VMEM((records, rows, cols), jnp.float32), plan.tiles],
        compiler_params=pltpu.CompilerParams(vmem_limit_bytes=32 * 2**20),
        cost_estimate=pl.CostEstimate(flops=1, bytes_accessed=1, transcendentals=0),
    )(*operands)


def receive(arrived, records):
    devices = arrived.shape[0]

    def kernel(in_ref, out_ref):
        turned = jnp.transpose(in_ref[...])
        for r in range(CAP):
            out_ref[:, r, :] = turned[r * RANK_ROWS : r * RANK_ROWS + records, :]

    out = call(kernel, jax.ShapeDtypeStruct((records, CAP, devices), jnp.float32), [arrived])
    return jnp.swapaxes(out, 0, 1)


def body(gx_count, gy_count, control, sigma, kappa, beta, sea_mask, x_inverse, y_inverse, ssh_coef,
         obs_owner, tile_index, obs_frac, obs_count):
    _, kinds, levels, rows, cols = control.shape
    devices = gx_count * gy_count
    plan = Plan(levels, rows, cols, gy_count // 2)
    chunks = kinds
    if not plan.fits:
        plan, chunks = Plan(kinds * levels, rows, cols, gy_count // 2), 1
    me = jnp.stack([lax.axis_index("gx"), lax.axis_index("gy")]).astype(jnp.int32)
    x_parts = prepare_x(x_inverse)
    fields = [control[0, 0] if chunks > 1 else control.reshape(plan.fields, rows, cols)]
    if chunks > 1:
        control = after(control, fields[0])
        fields += [control[0, kind] for kind in range(1, kinds)]
    y_columns = y_inverse.reshape(y_inverse.shape[0], gy_count // 2, 2, rows)
    y_columns = jnp.where(me[1] % 2 == 0, y_columns[:, :, 0], y_columns[:, :, 1])
    y_columns = y_columns.reshape(y_inverse.shape[0], -1)
    y_far = gather_far(y_columns, "gx", gx_count)
    y_held = gather_near(y_columns, "gx", gx_count) + y_far
    y_parts = prepare_y([m for m, _ in y_held], [p for _, p in y_held], me, rows)
    side_pairs = [(i, i ^ 1) for i in range(gy_count)]
    result = None
    for step in range(STEPS):
        own, other, sent = [], [], []
        for chunk in range(chunks):
            near = gather_near(fields[chunk], "gx", gx_count)
            total = zonal_start(plan, near, me, *x_parts)
            if sent:
                hold = [total, y_parts[0]] + lines
            elif step == 0:
                hold = [total, y_far[0][1]] + fields[1:]
            else:
                hold = [total] + returned[::-1]
            far = gather_far(fields[chunk], "gx", gx_count, hold)
            if own:
                total = after(total, own[-1])
            packed = zonal_end(plan, total, far, me, *x_parts, sea_mask)
            sent.append(exchange(packed, "gy", gy_count))
            if other:
                sums = add_sides(plan, me, own[-1], other[-1])
            ready = sums[0] if other else y_parts[0]
            lines = [after(line, ready) for line in sent[chunk]]
            for_own, for_other = meridional(plan, me, lines, *y_parts)
            own.append(for_own)
            other.append(lax.ppermute(for_other, "gy", side_pairs))
        for chunk in range(chunks):
            if chunk == 0 and chunks > 1:
                blocks = [after(block, own[-1]) for block in sums]
            else:
                if chunk > 0 and step < STEPS - 1:
                    own[chunk] = after(own[chunk], fields[chunk - 1])
                blocks = add_sides(plan, me, own[chunk], other[chunk])
            returned = exchange(blocks, "gy", gy_count)
            if chunk < chunks - 1:
                returned = [after(block, other[-1]) for block in returned]
            if step < STEPS - 1 or chunk < chunks - 1:
                fields[chunk] = vertical(plan, me, returned, kappa, sea_mask, levels)
            else:
                returned = [after(block, *fields[:chunk]) for block in returned]
                obs = (
                    obs_owner.reshape(1, -1),
                    tile_index.reshape(1, -1),
                    obs_frac,
                    obs_count,
                    obs_owner,
                )
                result = finish(
                    plan, me, returned, fields[0] if chunks > 1 else None, kappa, sea_mask, sigma,
                    beta, ssh_coef, obs, devices,
                )
    increments, height, outgoing = result
    arrived = lax.all_to_all(outgoing, ("gx", "gy"), split_axis=0, concat_axis=0, tiled=True)
    return increments[None], height[None], receive(arrived, kinds * levels + 1)


def solution(mesh):
    return jax.shard_map(
        functools.partial(body, mesh.shape["gx"], mesh.shape["gy"]),
        mesh=mesh,
        in_specs=(
            P(None, None, None, "gy", "gx"),
            P(None, None, "gy", "gx"),
            P(None, "gy", "gx"),
            P(None, "gy", "gx"),
            P("gy", "gx"),
            P("gx", None),
            P("gx", None),
            P(),
            P(("gx", "gy"), None),
            P(("gx", "gy")),
            P(None, ("gx", "gy")),
            P(("gx", "gy")),
        ),
        out_specs=(
            P(None, None, None, "gy", "gx"),
            P(None, "gy", "gx"),
            P(None, None, ("gx", "gy")),
        ),
        check_vma=False,
    )
```
